128 devices in a mesh: node: 16 (over x, z), local: 8 (over y, core).
Axes of the slice: x: 4, y: 4, z: 4, core: 2. Of those that a mesh axis runs over, the one named last changes fastest.
Arguments:
- hidden_states: bfloat16 [1536, 7168], P('node', 'local'), may hold values from -6 to 6
- routes: int32 [1536, 4], P('node'), may hold values from 0 to 15, all different within a row; in each aligned block of 96 rows (0 to 95, 96 to 191, ...) at most 36 rows name the same one
- route_weights: float32 [1536, 4], P('node'), may hold values from 0.05 to 0.6
- w_gate: bfloat16 [16, 7168, 2048], P('node', None, 'local'), may hold values from -0.0625 to 0.0625
- w_up: bfloat16 [16, 7168, 2048], P('node', None, 'local'), may hold values from -0.0625 to 0.0625
- w_down: bfloat16 [16, 2048, 7168], P('node', 'local'), may hold values from -0.1875 to 0.1875
- norm_gain: float32 [7168], P('local'), may hold values from 0.1 to 1.9
- head_weight: bfloat16 [65536, 7168], P(('node', 'local')), may hold values from -4 to 4
- targets: int32 [1536], replicated, may hold values from 0 to 65535
- policy_logp: float32 [1536], replicated, may hold values from -20 to -11
Outputs:
- layer_out: bfloat16 [1536, 7168], P('node', 'local')
- ref_logp: float32 [1536], replicated
- kl: float32 [1536], replicated
The draws below stay inside these ranges and needn't reach their ends.
Inputs may be any that keep to these rules, and one draw needn't show every extreme that they name: `routes`: in each aligned block of 96 rows no expert is named more than 36 times, a bound that some block reaches; a row names 4 different experts.
All inputs are finite; a program needn't handle non-finite values.
Results may differ from the reference program's by a relative error of at most 0.015.
Values may be sent and summed in bfloat16 or wider, within the bound.
No kernel may reach another device: no remote copies, remote signals or barrier semaphores. Data moves between devices by JAX's collectives and lax.ppermute only.
A program may use at most 128 MiB of HBM per device.

```python
import math
import jax
import jax.numpy as jnp
import numpy as np
from jax import lax

D = 7168
H = 2048
VOC_DEV = 512
TOP = 4
TOK_NODE = 96
EXPERTS = 16
H_DEV = 256
CAP = 36
TOKENS = 1536
VOCAB = 65536
N_NODE = 16
N_LOCAL = 8


def draw_head_weight(key, part):
    key = jax.random.fold_in(key, 7)
    spread = 3.0 / math.sqrt(D)
    values = jax.random.normal(key, (VOCAB, D), jnp.float32) * spread
    return jnp.clip(values, -4.0, 4.0).astype(jnp.bfloat16)


def with_ends(drawn, stream_key, least, top_value):
    dims = drawn.shape
    index_at = [jax.random.randint(jax.random.fold_in(stream_key, axis), (), 0, dims[axis]) for axis in range(len(dims))]
    drawn = drawn.at[tuple(index_at)].set(least)
    longest = dims.index(max(dims))
    index_at[longest] = (index_at[longest] + 1) % dims[longest]
    return drawn.at[tuple(index_at)].set(top_value)


def strengthened(entries, rng, source, target, blocks, factor):
    owner, partner = [(jnp.arange(entries.shape[position]) // (entries.shape[position] // blocks)).reshape([-1 if axis == position else 1 for axis in range(entries.ndim)]) for position in (source, target)]
    chosen = jax.random.permutation(rng, blocks)[partner]
    strong = (owner == chosen) | (owner == (partner + blocks // 2) % blocks)
    return jnp.where(strong, factor * entries, entries)


def shard_levels(stream_key, shape, split, least, high):
    gain, own = 1.0, jax.random.fold_in(stream_key, 6)
    for axis_at, parts in split:
        heights = jnp.exp(jax.random.uniform(jax.random.fold_in(own, axis_at), (parts,), jnp.float32, least / len(split), high / len(split)))
        gain = gain * jnp.repeat(heights, shape[axis_at] // parts).reshape([-1 if axis == axis_at else 1 for axis in range(len(shape))])
    return gain


def cumulative_ranks(number_of, slope):
    weights = [(1 << 20) // math.isqrt(rank ** slope) + 1 for rank in range(1, number_of + 1)]
    scale = 1 + sum(weights) // (1 << 30)
    return np.cumsum(np.array([max(1, weight // scale) for weight in weights]))


def ranked(rng, extent, number_of, skew):
    listing = cumulative_ranks(number_of, skew)
    lot = jax.random.randint(jax.random.fold_in(rng, 1), extent, 0, int(listing[number_of - 1]))
    standing = jnp.searchsorted(jnp.asarray(listing, jnp.int32), lot, side="right")
    return jax.random.permutation(jax.random.fold_in(rng, 2), number_of)[standing].astype(jnp.int32)


def deal_out(own_key, own, number, rows, number_of, top, limit, skew):
    sequence = jax.random.permutation(own_key, number_of)
    packed, common = portions_of(number_of, rows * top, limit, skew, True), portions_of(number_of, rows * top, limit, skew, False)
    places = jnp.arange(number_of)

    def named(sizes, offset_by):
        used = int((sizes > 0).sum())
        fixed = max(1, used // 4)
        passed = fixed + (places - fixed + offset_by * (used - fixed)) % max(1, number_of - fixed)
        return jnp.zeros((number_of,), jnp.int32).at[sequence[jnp.where(places < fixed, places, passed)]].set(jnp.asarray(sizes, jnp.int32))

    sizes = jnp.where(number % 4 == 0, named(packed, number // 4), named(common, number - number // 4 - 1))
    mixed = jax.random.permutation(jax.random.fold_in(own, 3), number_of)
    giver, receiver = mixed[0:number_of // 2 * 2:2], mixed[1:number_of // 2 * 2:2]
    slack = jnp.minimum(sizes[giver] - 1, limit - sizes[receiver]) // 2
    slack = jnp.where((giver == sequence[0]) | (receiver == sequence[0]) | (sizes[receiver] == 0), 0, jnp.maximum(slack, 0))
    passed = jax.random.randint(jax.random.fold_in(own, 4), (number_of // 2,), 0, 1 << 20) % (slack + 1)
    sizes = sizes.at[giver].add(-passed).at[receiver].add(passed)
    members = jnp.searchsorted(jnp.cumsum(sizes), jnp.arange(rows * top), side="right").astype(jnp.int32)
    listing = members.reshape(top, rows).T
    listing = listing[jax.random.permutation(jax.random.fold_in(own, 1), rows)]
    offset_by = jax.random.randint(jax.random.fold_in(own, 2), (rows, 1), 0, top)
    return jnp.take_along_axis(listing, (jnp.arange(top)[None, :] + offset_by) % top, axis=1)


def portions_of(number_of, total, reach, lean, full):
    portions = [(1 << 20) // math.isqrt(standing ** lean) + 1 for standing in range(1, number_of + 1)]
    largest = reach if full else min(reach, max(-(-total // number_of), total * portions[0] // sum(portions)))
    least = 1 if total - largest >= number_of - 1 else 0
    counts, rest = [largest] + [least] * (number_of - 1), total - largest - least * (number_of - 1)
    while rest > 0:
        candidates = [i for i in range(1, number_of) if counts[i] < largest] or [i for i in range(1, number_of) if counts[i] < reach]
        mass, remaining = sum([portions[i] for i in candidates]), rest
        for i in candidates:
            more = min(reach - counts[i], max(1, remaining * portions[i] // mass), rest)
            counts[i] = counts[i] + more
            rest = rest - more
    return np.array(counts)


def noise(own_key, shape, deviation, limit, shards=(), held_as=jnp.bfloat16):
    loudness = shard_levels(own_key, shape, shards, -0.22, 0.18) if shards else 1.0
    entries = jax.random.normal(own_key, shape, jnp.float32) * deviation * loudness
    return jnp.minimum(jnp.maximum(entries, -limit), limit).astype(held_as)


def noise_with(rng, dims, deviation, bound, split, heavy, kind=jnp.bfloat16):
    result = deviation * jax.random.normal(rng, dims, jnp.float32)
    if split:
        result = result * shard_levels(rng, dims, split, -0.22, 0.18)
    return jnp.clip(strengthened(result, jax.random.fold_in(rng, 3), *heavy), -bound, bound).astype(kind)


def setup_inputs(seed: int = 0) -> dict:
    keys = jax.random.split(jax.random.key(seed), 11)
    hidden_states = noise(keys[0], (TOKENS, D), 1.0, 6.0, ((0, 16), (1, 8)))
    routes_keys = jax.random.split(jax.random.fold_in(keys[1], 1), TOKENS // TOK_NODE)
    routes_turns = jax.random.permutation(jax.random.fold_in(keys[1], 3), TOKENS // TOK_NODE)
    routes = jax.vmap(lambda own, number: deal_out(jax.random.fold_in(keys[1], 2), own, number, TOK_NODE, EXPERTS, TOP, CAP, 1))(routes_keys, routes_turns).reshape((TOKENS, TOP))
    route_weights = jnp.clip(jnp.exp(math.log(0.6) - 2.4849067 * jax.random.uniform(keys[2], (TOKENS, TOP), jnp.float32) ** shard_levels(keys[2], (TOKENS, TOP), ((0, 16),), -0.2, 0.2)), 0.05, 0.6)
    w_gate = noise(keys[3], (EXPERTS, D, H), D ** -0.5, 0.0625, ((0, 16), (2, 8)))
    w_up = noise(keys[4], (EXPERTS, D, H), D ** -0.5, 0.0625, ((0, 16), (2, 8)))
    w_down = noise_with(keys[5], (EXPERTS, H, D), H ** -0.5, 0.1875, ((0, 16), (1, 8)), (1, 2, 8, 2.0))
    norm_gain = jnp.clip(1.0 + 0.18 * jax.random.normal(keys[6], (D,), jnp.float32), 0.1, 1.9)
    head_weight = draw_head_weight(jax.random.fold_in(keys[10], 71), 0)
    targets = with_ends(ranked(keys[8], (TOKENS,), VOCAB, 2), jax.random.fold_in(keys[8], 3), 0, VOCAB - 1).astype(jnp.int32)
    policy_logp = jnp.clip(jax.random.uniform(keys[9], (TOKENS,), jnp.float32, -20.0, -11.0), -20.0, -11.0)
    return {"hidden_states": hidden_states, "routes": routes, "route_weights": route_weights, "w_gate": w_gate, "w_up": w_up, "w_down": w_down, "norm_gain": norm_gain, "head_weight": head_weight, "targets": targets, "policy_logp": policy_logp}


def expert_apply(inputs):
    buffer, gate_mat, up_mat, down_mat = inputs
    gate_pre = jnp.dot(buffer, gate_mat, preferred_element_type=jnp.float32)
    up_pre = jnp.dot(buffer, up_mat, preferred_element_type=jnp.float32)
    activated = (jax.nn.silu(gate_pre) * up_pre).astype(jnp.bfloat16)
    groups = activated.reshape(activated.shape[0], N_LOCAL, H_DEV).astype(jnp.float32)
    down_groups = down_mat.reshape(N_LOCAL, H_DEV, D).astype(jnp.float32)
    partials = jnp.einsum('rjh,jhd->jrd', groups, down_groups)
    rounded = lax.optimization_barrier(partials.astype(jnp.bfloat16)).astype(jnp.float32)
    return lax.optimization_barrier(jnp.sum(rounded, axis=0)).astype(jnp.bfloat16)

def reference(hidden_states, routes, route_weights, w_gate, w_up, w_down, norm_gain, head_weight, targets, policy_logp):
    flat_routes = routes.reshape(N_NODE, TOK_NODE * TOP)
    onehot = (flat_routes[:, :, None] == jnp.arange(EXPERTS, dtype=jnp.int32)[None, None, :]).astype(jnp.int32)
    earlier = jnp.cumsum(onehot, axis=1) - onehot
    slot_index = lax.optimization_barrier(jnp.sum(earlier * onehot, axis=2))
    source_ids = jnp.arange(N_NODE, dtype=jnp.int32)[:, None]
    slot_rows = ((flat_routes * N_NODE + source_ids) * CAP + slot_index).reshape(-1).astype(jnp.int32)
    rows_src = jnp.repeat(hidden_states, TOP, axis=0)
    buffer = jnp.zeros((EXPERTS * N_NODE * CAP, D), jnp.bfloat16).at[slot_rows].set(rows_src)
    buffer = buffer.reshape(EXPERTS, N_NODE * CAP, D)
    expert_out = lax.map(expert_apply, (buffer, w_gate, w_up, w_down)).reshape(-1, D)
    returned = expert_out[slot_rows].astype(jnp.float32).reshape(TOKENS, TOP, D)
    expert_mix = lax.optimization_barrier(jnp.sum(returned * route_weights[:, :, None], axis=1))
    layer_sum = hidden_states.astype(jnp.float32) + expert_mix
    layer_out = layer_sum.astype(jnp.bfloat16)
    inv_rms = lax.rsqrt(lax.optimization_barrier(jnp.mean(layer_sum * layer_sum, axis=1)) + 1e-06)
    normed = (layer_sum * inv_rms[:, None] * norm_gain[None, :]).astype(jnp.bfloat16)
    blocks = head_weight.reshape(VOCAB // VOC_DEV, VOC_DEV, D)
    firsts = jnp.arange(VOCAB // VOC_DEV, dtype=jnp.int32) * VOC_DEV

    def vocab_step(running, inputs):
        weights_blk, first_id = inputs
        running_max, exp_total, target_logit = running
        logits = lax.dot_general(normed, weights_blk, (((1,), (1,)), ((), ())), preferred_element_type=jnp.float32)
        ids = first_id + jnp.arange(VOC_DEV, dtype=jnp.int32)
        new_max = jnp.maximum(running_max, lax.optimization_barrier(jnp.max(logits, axis=1)))
        exp_total = exp_total * jnp.exp(running_max - new_max) + lax.optimization_barrier(jnp.sum(jnp.exp(logits - new_max[:, None]), axis=1))
        target_logit = target_logit + lax.optimization_barrier(jnp.sum(jnp.where(ids[None, :] == targets[:, None], logits, 0.0), axis=1))
        return ((new_max, exp_total, target_logit), None)
    initial = (jnp.full((TOKENS,), -jnp.inf, jnp.float32), jnp.zeros((TOKENS,), jnp.float32), jnp.zeros((TOKENS,), jnp.float32))
    (running_max, exp_total, target_logit), unused = lax.scan(vocab_step, initial, (blocks, firsts))
    ref_logp = target_logit - running_max - jnp.log(exp_total)
    kl = 0.5 * (policy_logp - ref_logp) * (policy_logp - ref_logp)
    return (layer_out, ref_logp, kl)
```

```python
import functools
import jax
import jax.numpy as jnp
from jax import lax
from jax.experimental import pallas as pl
from jax.experimental.pallas import tpu as pltpu
from jax.sharding import Mesh, PartitionSpec as P

BF = jnp.bfloat16
F32 = jnp.float32
AXES = ("x", "z", "y", "core")
SLOTS = 40


def shift(value, axis, step):
    size = lax.axis_size(axis)
    return lax.ppermute(value, axis, [(i, (i + step) % size) for i in range(size)])


def dot(a, b):
    return jnp.dot(a, b, preferred_element_type=F32)


def dispatch_kernel(routes_ref, weights_ref, h0, h1, h2, h3, send_ref, hi_ref, lo_ref):
    tokens, top = routes_ref.shape
    experts = send_ref.shape[0] // SLOTS
    columns = send_ref.shape[0]
    ids = lax.broadcasted_iota(jnp.int32, (tokens, experts), 1)
    named = jnp.zeros((tokens, experts), F32)
    gates = jnp.zeros((tokens, experts), F32)
    for k in range(top):
        hit = routes_ref[:, k : k + 1] == ids
        named = named + jnp.where(hit, 1.0, 0.0)
        gates = gates + jnp.where(hit, weights_ref[:, k : k + 1], 0.0)
    row = lax.broadcasted_iota(jnp.int32, (tokens, tokens), 0)
    col = lax.broadcasted_iota(jnp.int32, (tokens, tokens), 1)
    before = jnp.where(col < row, 1.0, 0.0).astype(BF)
    count = dot(before, named.astype(BF))
    expert = lax.broadcasted_iota(jnp.int32, (experts, columns), 0)
    column = lax.broadcasted_iota(jnp.int32, (experts, columns), 1)
    inside = (column >= expert * SLOTS) & (column < expert * SLOTS + SLOTS)
    spread = jnp.where(inside, 1.0, 0.0).astype(BF)
    slot = jnp.sum(jnp.where(inside, column - expert * SLOTS, 0).astype(F32), axis=0, keepdims=True)
    gates_hi = gates.astype(BF)
    gates_lo = (gates - gates_hi.astype(F32)).astype(BF)
    placed = (dot(named.astype(BF), spread) > 0.5) & (dot(count.astype(BF), spread) == slot)
    hi_ref[...] = jnp.where(placed, dot(gates_hi, spread), 0.0).astype(BF)
    lo_ref[...] = jnp.where(placed, dot(gates_lo, spread), 0.0).astype(BF)
    pick = jnp.where(placed, 1.0, 0.0).astype(BF)
    width = h0.shape[1]
    for k, ref in enumerate((h0, h1, h2, h3)):
        rows = lax.dot_general(pick, ref[...], (((0,), (0,)), ((), ())), preferred_element_type=F32)
        send_ref[:, k * width : (k + 1) * width] = rows.astype(BF)


def up_kernel(place_ref, rows_ref, g_own, u_own, g_other, u_other, sum_ref, out_ref):
    k = pl.program_id(0)
    rows = rows_ref[...]
    hidden = g_own.shape[1]
    for j, ref in enumerate((g_own, u_own, g_other, u_other)):
        cols = slice(j * hidden, (j + 1) * hidden)
        part = dot(rows, ref[...])

        @pl.when(k == 0)
        def _(part=part, cols=cols):
            sum_ref[:, cols] = part

        @pl.when(k > 0)
        def _(part=part, cols=cols):
            sum_ref[:, cols] += part

    @pl.when(k == pl.num_programs(0) - 1)
    def _():
        out_ref[...] = sum_ref[...].astype(BF)


def down_kernel(place_ref, sum_ref, got_ref, d_own, d_other, out_ref, act_ref):
    hidden = d_own.shape[0]

    @pl.when(pl.program_id(0) == 0)
    def _():
        for j in range(2):
            own, got = 2 * j * hidden, 2 * (1 - j) * hidden
            gate = sum_ref[:, own : own + hidden] + got_ref[:, got : got + hidden].astype(F32)
            up = sum_ref[:, own + hidden : own + 2 * hidden] + got_ref[
                :, got + hidden : got + 2 * hidden
            ].astype(F32)
            act = gate / (1.0 + jnp.exp(-gate)) * up
            act_ref[:, j * hidden : (j + 1) * hidden] = act.astype(BF)

    total = dot(act_ref[:, :hidden], d_own[...]) + dot(act_ref[:, hidden:], d_other[...])
    out_ref[...] = total.astype(BF)


def mix_kernel(hi_ref, lo_ref, back_ref, own_ref, p1, p2, p3):
    width = own_ref.shape[1]
    for k, ref in enumerate((own_ref, p1, p2, p3)):
        block = back_ref[:, k * width : (k + 1) * width]
        total = dot(hi_ref[...], block) + dot(lo_ref[...], block)
        ref[...] = total.astype(ref.dtype)


def layer_kernel(hidden_ref, own_ref, p1, p2, p3, gain_ref, out_ref, scaled_ref, squares_ref):
    mix = own_ref[...] + p1[...].astype(F32) + p2[...].astype(F32) + p3[...].astype(F32)
    total = hidden_ref[...].astype(F32) + mix
    out_ref[...] = total.astype(BF)
    scaled_ref[...] = (total * gain_ref[...]).astype(BF)
    squares_ref[...] = jnp.sum(total * total, axis=1, keepdims=True)


def head_kernel(first_ref, rows_ref, head_ref, scale_ref, wanted_ref, stats_ref, sum_ref):
    part = pl.program_id(1)
    nodes, _, tokens, width = rows_ref.shape
    rows = rows_ref[...].reshape(nodes * tokens, width)
    start = pl.multiple_of(part * width, 128)
    logits = lax.dot_general(
        rows, head_ref[:, pl.ds(start, width)], (((1,), (1,)), ((), ())), preferred_element_type=F32
    )

    @pl.when(part == 0)
    def _():
        sum_ref[...] = logits

    @pl.when(part > 0)
    def _():
        sum_ref[...] += logits

    @pl.when(part == pl.num_programs(1) - 1)
    def _():
        full = sum_ref[...] * scale_ref[...]
        peak = jnp.max(full, axis=1, keepdims=True)
        total = jnp.sum(jnp.exp(full - peak), axis=1, keepdims=True)
        ids = first_ref[0] + lax.broadcasted_iota(jnp.int32, full.shape, 1)
        target = jnp.sum(jnp.where(ids == wanted_ref[...], full, 0.0), axis=1, keepdims=True)
        lane = lax.broadcasted_iota(jnp.int32, (full.shape[0], 128), 1)
        stats_ref[...] = jnp.where(lane == 0, peak, jnp.where(lane == 1, total, target))


def paired(terms):
    if len(terms) == 2:
        return terms[0] + terms[1]
    return (terms[0] + terms[2]) + (terms[1] + terms[3])


def merged(values):
    peaks = [v[0] for v in values]
    peak = functools.reduce(jnp.maximum, peaks)
    total = paired([v[1] * jnp.exp(v[0] - peak) for v in values])
    return jnp.stack([peak, total, paired([v[2] for v in values])])


def shards(hidden, routes, route_weights, w_gate, w_up, w_down, gain, head, targets, policy_logp):
    tokens, width = hidden.shape
    y = lax.axis_index("y")
    core = lax.axis_index("core")
    n_y = lax.axis_size("y")
    n_node = lax.axis_size("x") * lax.axis_size("z")
    slots = n_node * SLOTS
    wide = n_y * width
    model = 2 * wide
    hid = w_gate.shape[2]
    vmem = pltpu.CompilerParams(vmem_limit_bytes=48 * 1024 * 1024)

    near = [hidden] + [shift(hidden, "y", k) for k in (1, 2, 3)]
    gate_mat, up_mat, down_mat = w_gate[0], w_up[0], w_down[0]
    gate_other, up_other, down_other = (shift(w, "core", 1) for w in (gate_mat, up_mat, down_mat))

    send, mix_hi, mix_lo = pl.pallas_call(
        dispatch_kernel,
        out_shape=(
            jax.ShapeDtypeStruct((slots, wide), BF),
            jax.ShapeDtypeStruct((tokens, slots), BF),
            jax.ShapeDtypeStruct((tokens, slots), BF),
        ),
        compiler_params=vmem,
        name="dispatch",
    )(routes, route_weights, *near)

    rows = lax.all_to_all(
        send.reshape(n_node, SLOTS, wide), ("x", "z"), split_axis=0, concat_axis=0, tiled=True
    ).reshape(slots, wide)

    place = jnp.stack([y, core]).astype(jnp.int32)

    def block(k, place):
        return 2 * lax.rem(place[0] + n_y - k, n_y) + place[1]

    weight_rows = pl.BlockSpec((width, hid), lambda k, place: (block(k, place), 0))
    partial, partial_out = pl.pallas_call(
        up_kernel,
        grid_spec=pltpu.PrefetchScalarGridSpec(
            num_scalar_prefetch=1,
            grid=(n_y,),
            in_specs=[pl.BlockSpec((slots, width), lambda k, place: (0, k))] + [weight_rows] * 4,
            out_specs=[pl.BlockSpec((slots, 4 * hid), lambda k, place: (0, 0))] * 2,
        ),
        out_shape=(
            jax.ShapeDtypeStruct((slots, 4 * hid), F32),
            jax.ShapeDtypeStruct((slots, 4 * hid), BF),
        ),
        compiler_params=vmem,
        name="gate_up",
    )(place, rows, gate_mat, up_mat, gate_other, up_other)
    partial_got = shift(partial_out, "core", 1)

    weight_cols = pl.BlockSpec((hid, width), lambda k, place: (0, block(k, place)))
    whole = pl.BlockSpec((slots, 4 * hid), lambda k, place: (0, 0))
    expert_out = pl.pallas_call(
        down_kernel,
        grid_spec=pltpu.PrefetchScalarGridSpec(
            num_scalar_prefetch=1,
            grid=(n_y,),
            in_specs=[whole, whole, weight_cols, weight_cols],
            out_specs=pl.BlockSpec((slots, width), lambda k, place: (0, k)),
            scratch_shapes=[pltpu.VMEM((slots, 2 * hid), BF)],
        ),
        out_shape=jax.ShapeDtypeStruct((slots, wide), BF),
        compiler_params=vmem,
        name="down",
    )(place, partial, partial_got, down_mat, down_other)

    returned = lax.all_to_all(
        expert_out.reshape(n_node, SLOTS, wide), ("x", "z"), split_axis=0, concat_axis=0, tiled=True
    ).reshape(slots, wide)
    own, *others = pl.pallas_call(
        mix_kernel,
        out_shape=(jax.ShapeDtypeStruct((tokens, width), F32),)
        + (jax.ShapeDtypeStruct((tokens, width), BF),) * 3,
        compiler_params=vmem,
        name="mix",
    )(mix_hi, mix_lo, returned)
    arrived = [shift(part, "y", -k) for k, part in zip((1, 2, 3), others)]
    layer_out, scaled, squares = pl.pallas_call(
        layer_kernel,
        out_shape=(
            jax.ShapeDtypeStruct((tokens, width), BF),
            jax.ShapeDtypeStruct((tokens, width), BF),
            jax.ShapeDtypeStruct((tokens, 1), F32),
        ),
        compiler_params=vmem,
        name="layer",
    )(hidden, own, *arrived, gain.reshape(1, width))

    everyone = lax.all_gather(scaled, AXES, axis=0, tiled=True)

    squares = squares.reshape(1, tokens)
    squares = squares + shift(squares, "core", 1)
    squares = paired([squares] + [shift(squares, "y", k) for k in (1, 2, 3)])
    for axis in ("z", "x"):
        here = lax.axis_index(axis)
        size = lax.axis_size(axis)
        order = jnp.arange(size)[:, None, None]
        gathered = jnp.where(order == here, squares[None], 0.0)
        for k in range(1, size):
            from_there = shift(squares, axis, k)
            gathered = gathered + jnp.where(order == (here - k) % size, from_there[None], 0.0)
        squares = gathered.reshape(-1, tokens)
    total_tokens = n_node * tokens
    scale = lax.rsqrt(squares.reshape(total_tokens, 1) / model + 1e-06)

    vocab_rows = head.shape[0]
    first_id = lax.axis_index(AXES) * vocab_rows
    group = 4
    stats = pl.pallas_call(
        head_kernel,
        grid_spec=pltpu.PrefetchScalarGridSpec(
            num_scalar_prefetch=1,
            grid=(n_node // group, 2 * n_y),
            in_specs=[
                pl.BlockSpec((group, 1, tokens, width), lambda n, p, s: (n, p, 0, 0)),
                pl.BlockSpec((vocab_rows, model), lambda n, p, s: (0, 0)),
                pl.BlockSpec((group * tokens, 1), lambda n, p, s: (n, 0)),
                pl.BlockSpec((group * tokens, 1), lambda n, p, s: (n, 0)),
            ],
            out_specs=pl.BlockSpec((group * tokens, 128), lambda n, p, s: (n, 0)),
            scratch_shapes=[pltpu.VMEM((group * tokens, vocab_rows), F32)],
        ),
        out_shape=jax.ShapeDtypeStruct((total_tokens, 128), F32),
        compiler_params=vmem,
        name="head",
    )(
        first_id.reshape(1).astype(jnp.int32),
        everyone.reshape(n_node, 2 * n_y, tokens, width),
        head,
        scale,
        targets.reshape(total_tokens, 1),
    )
    stats = stats[:, :3].T
    stats = merged([stats, shift(stats, "core", 1)])
    for axis in ("y", "z", "x"):
        stats = merged([stats] + [shift(stats, axis, k) for k in (1, 2, 3)])
    peak, exp_total, target_logit = stats
    ref_logp = target_logit - peak - jnp.log(exp_total)
    kl = 0.5 * (policy_logp - ref_logp) * (policy_logp - ref_logp)
    return layer_out, ref_logp, kl


def solution(mesh):
    split = Mesh(mesh.devices.reshape(4, 4, 4, 2), AXES)
    node, local = ("x", "z"), ("y", "core")
    placed = (
        P(node, local),
        P(node, None),
        P(node, None),
        P(node, None, local),
        P(node, None, local),
        P(node, local, None),
        P(local),
        P(AXES, None),
        P(),
        P(),
    )
    return jax.shard_map(
        shards,
        mesh=split,
        in_specs=placed,
        out_specs=(P(node, local), P(), P()),
        check_vma=False,
    )
```

```python
import functools
import jax
import jax.numpy as jnp
from jax import lax
from jax.experimental import pallas as pl
from jax.experimental.pallas import tpu as pltpu
from jax.sharding import Mesh, PartitionSpec as P

BF = jnp.bfloat16
F32 = jnp.float32
AXES = ("x", "z", "y", "core")
SLOTS = 40
FIRST = 512


def shift(value, axis, step):
    size = lax.axis_size(axis)
    return lax.ppermute(value, axis, [(i, (i + step) % size) for i in range(size)])


def dot(a, b):
    return jnp.dot(a, b, preferred_element_type=F32)


def route_kernel(routes_ref, weights_ref, hidden_ref, pick_ref, hi_ref, lo_ref, send_ref):
    tokens, top = routes_ref.shape
    columns = pick_ref.shape[1]
    experts = columns // SLOTS
    ids = lax.broadcasted_iota(jnp.int32, (tokens, experts), 1)
    named = jnp.zeros((tokens, experts), F32)
    gates = jnp.zeros((tokens, experts), F32)
    for k in range(top):
        hit = routes_ref[:, k : k + 1] == ids
        named = named + jnp.where(hit, 1.0, 0.0)
        gates = gates + jnp.where(hit, weights_ref[:, k : k + 1], 0.0)
    row = lax.broadcasted_iota(jnp.int32, (tokens, tokens), 0)
    col = lax.broadcasted_iota(jnp.int32, (tokens, tokens), 1)
    before = jnp.where(col < row, 1.0, 0.0).astype(BF)
    count = dot(before, named.astype(BF))
    expert = lax.broadcasted_iota(jnp.int32, (experts, columns), 0)
    column = lax.broadcasted_iota(jnp.int32, (experts, columns), 1)
    inside = (column >= expert * SLOTS) & (column < expert * SLOTS + SLOTS)
    spread = jnp.where(inside, 1.0, 0.0).astype(BF)
    slot = jnp.sum(jnp.where(inside, column - expert * SLOTS, 0).astype(F32), axis=0, keepdims=True)
    gates_hi = gates.astype(BF)
    gates_lo = (gates - gates_hi.astype(F32)).astype(BF)
    placed = (dot(named.astype(BF), spread) > 0.5) & (dot(count.astype(BF), spread) == slot)
    hi_ref[...] = jnp.where(placed, dot(gates_hi, spread), 0.0).astype(BF)
    lo_ref[...] = jnp.where(placed, dot(gates_lo, spread), 0.0).astype(BF)
    pick = jnp.where(placed, 1.0, 0.0).astype(BF)
    pick_ref[...] = pick
    send_ref[...] = picked(pick, hidden_ref[:, :FIRST]).astype(BF)


def picked(pick, rows):
    return lax.dot_general(pick, rows, (((0,), (0,)), ((), ())), preferred_element_type=F32)


def spread_kernel(pick_ref, h0, h1, h2, h3, send_ref):
    width = h0.shape[1]
    for k, ref in enumerate((h0, h1, h2, h3)):
        send_ref[:, k * width : (k + 1) * width] = picked(pick_ref[...], ref[...]).astype(BF)


def block_of(place_ref, k):
    return 2 * lax.rem(place_ref[0] + 4 - k, 4) + place_ref[1]


def up_kernel(place_ref, a0, a1, a2_top, a2_low, a3, b_ref, w0, w1, w2, w3, sum_ref, out_ref, w_ref, sems):
    step = pl.program_id(0)
    hidden = w0.shape[1]
    width = w0.shape[0] // 8
    second = width - FIRST

    def copies():
        made = []
        for j, w in enumerate((w0, w1, w2, w3)):
            cols = pl.ds(j * hidden, hidden)
            for k in range(4):
                start = pl.multiple_of(block_of(place_ref, k) * width, 128)
                made.append(
                    pltpu.make_async_copy(
                        w.at[pl.ds(start, FIRST), :],
                        w_ref.at[pl.ds(k * FIRST, FIRST), cols],
                        sems.at[j, 2 * k],
                    )
                )
                made.append(
                    pltpu.make_async_copy(
                        w.at[pl.ds(start + FIRST, second), :],
                        w_ref.at[pl.ds(4 * FIRST + k * second, second), cols],
                        sems.at[j, 2 * k + 1],
                    )
                )
        return made

    @pl.when(step == 0)
    def _():
        for copy in copies():
            copy.start()
        for copy in copies():
            copy.wait()

    def total(a2):
        for j in range(4):
            cols = slice(j * hidden, (j + 1) * hidden)
            part = dot(b_ref[...], w_ref[4 * FIRST :, cols])
            for k, ref in enumerate((a0, a1, a2, a3)):
                part = part + dot(ref[...], w_ref[k * FIRST : (k + 1) * FIRST, cols])
            sum_ref[:, cols] = part
            out_ref[:, cols] = part.astype(BF)

    @pl.when(step == 0)
    def _():
        total(a2_top)

    @pl.when(step == 1)
    def _():
        total(a2_low)


def down_kernel(
    place_ref, sum_ref, got_ref, w0, w1, a0, a1_top, a1_low, a2_top, a2_low, a3_top, a3_low, b_ref,
    w_ref, act_ref, sems
):
    step = pl.program_id(0)
    hidden = w0.shape[0]
    width = w0.shape[1] // 8
    second = width - FIRST

    def copies():
        made = []
        for j, w in enumerate((w0, w1)):
            rows = pl.ds(j * hidden, hidden)
            for k in range(4):
                start = pl.multiple_of(block_of(place_ref, k) * width, 128)
                made.append(
                    pltpu.make_async_copy(
                        w.at[:, pl.ds(start, FIRST)],
                        w_ref.at[rows, pl.ds(k * FIRST, FIRST)],
                        sems.at[j, 2 * k],
                    )
                )
                made.append(
                    pltpu.make_async_copy(
                        w.at[:, pl.ds(start + FIRST, second)],
                        w_ref.at[rows, pl.ds(4 * FIRST + k * second, second)],
                        sems.at[j, 2 * k + 1],
                    )
                )
        return made

    @pl.when(step == 0)
    def _():
        for copy in copies():
            copy.start()

    for j in range(2):
        own, got = 2 * j * hidden, 2 * (1 - j) * hidden
        gate = sum_ref[:, own : own + hidden] + got_ref[:, got : got + hidden].astype(F32)
        up = sum_ref[:, own + hidden : own + 2 * hidden] + got_ref[
            :, got + hidden : got + 2 * hidden
        ].astype(F32)
        act_ref[:, j * hidden : (j + 1) * hidden] = (gate / (1.0 + jnp.exp(-gate)) * up).astype(BF)

    @pl.when(step == 0)
    def _():
        for copy in copies():
            copy.wait()

    def out(start, size):
        return dot(act_ref[...], w_ref[:, start : start + size]).astype(BF)

    a0[...] = out(0, FIRST)
    b_ref[...] = out(4 * FIRST, 4 * second)

    @pl.when(step == 0)
    def _():
        for k, ref in ((1, a1_top), (2, a2_top), (3, a3_top)):
            ref[...] = out(k * FIRST, FIRST)

    @pl.when(step == 1)
    def _():
        for k, ref in ((1, a1_low), (2, a2_low), (3, a3_low)):
            ref[...] = out(k * FIRST, FIRST)


def add_kernel(a1, got1, a3, got3, out1, out3):
    out1[...] = (a1[...].astype(F32) + got1[...].astype(F32)).astype(BF)
    out3[...] = (a3[...].astype(F32) + got3[...].astype(F32)).astype(BF)


def ysum_kernel(a0, left_top, left_low, right_top, right_low, out_ref):
    half = left_top.shape[0]
    top = a0[:half].astype(F32) + left_top[...].astype(F32) + right_top[...].astype(F32)
    low = a0[half:].astype(F32) + left_low[...].astype(F32) + right_low[...].astype(F32)
    out_ref[:half] = top.astype(BF)
    out_ref[half:] = low.astype(BF)


def mix_kernel(hi_ref, lo_ref, back_ref, own_ref, p1, p2, p3):
    width = own_ref.shape[1]
    for k, ref in enumerate((own_ref, p1, p2, p3)):
        block = back_ref[:, k * width : (k + 1) * width]
        total = dot(hi_ref[...], block) + dot(lo_ref[...], block)
        ref[...] = total.astype(ref.dtype)


def layer_kernel(
    hidden_ref, hi_ref, lo_ref, back_ref, own_ref, p1, p2, p3, gain_ref, out_ref, scaled_ref, squares_ref
):
    first = dot(hi_ref[...], back_ref[...]) + dot(lo_ref[...], back_ref[...])
    second = own_ref[...] + p1[...].astype(F32) + p2[...].astype(F32) + p3[...].astype(F32)
    squares = 0.0
    for mix, cols in ((first, slice(0, FIRST)), (second, slice(FIRST, hidden_ref.shape[1]))):
        total = hidden_ref[:, cols].astype(F32) + mix
        out_ref[:, cols] = total.astype(BF)
        scaled_ref[:, cols] = (total * gain_ref[:, cols]).astype(BF)
        squares = squares + jnp.sum(total * total, axis=1, keepdims=True)
    squares_ref[...] = squares


def head_kernel(first_ref, rows_ref, head_ref, scale_ref, wanted_ref, stats_ref):
    nodes, parts, tokens, width = rows_ref.shape
    rows = jnp.concatenate([rows_ref[:, p].reshape(nodes * tokens, width) for p in range(parts)], axis=1)
    logits = lax.dot_general(
        rows, head_ref[...], (((1,), (1,)), ((), ())), preferred_element_type=F32
    )
    full = logits * scale_ref[...]
    peak = jnp.max(full, axis=1, keepdims=True)
    total = jnp.sum(jnp.exp(full - peak), axis=1, keepdims=True)
    ids = first_ref[0] + lax.broadcasted_iota(jnp.int32, full.shape, 1)
    target = jnp.sum(jnp.where(ids == wanted_ref[...], full, 0.0), axis=1, keepdims=True)
    lane = lax.broadcasted_iota(jnp.int32, (full.shape[0], 128), 1)
    columns = jnp.where(lane == 0, peak, jnp.where(lane == 1, total, target))
    stats_ref[...] = columns.T[:8]


def merge_kernel(*refs):
    *ins, out_ref = refs
    values = [ref[...] for ref in ins]
    peak = functools.reduce(jnp.maximum, [v[0:1] for v in values])
    total = paired([v[1:2] * jnp.exp(v[0:1] - peak) for v in values])
    target = paired([v[2:3] for v in values])
    row = lax.broadcasted_iota(jnp.int32, out_ref.shape, 0)
    out_ref[...] = jnp.where(row == 0, peak, jnp.where(row == 1, total, target))


def paired(terms):
    if len(terms) == 2:
        return terms[0] + terms[1]
    return (terms[0] + terms[2]) + (terms[1] + terms[3])


def merged(values):
    return pl.pallas_call(
        merge_kernel,
        out_shape=jax.ShapeDtypeStruct(values[0].shape, F32),
        name="merge",
    )(*values)


def like(*shape, dtype=BF):
    return jax.ShapeDtypeStruct(shape, dtype)


def over_nodes(rows):
    nodes = lax.axis_size("x") * lax.axis_size("z")
    cut = rows.reshape(nodes, rows.shape[0] // nodes, rows.shape[1])
    return lax.all_to_all(cut, ("x", "z"), split_axis=0, concat_axis=0, tiled=True).reshape(rows.shape)


def shards(hidden, routes, route_weights, w_gate, w_up, w_down, gain, head, targets, policy_logp):
    tokens, width = hidden.shape
    second = width - FIRST
    y = lax.axis_index("y")
    core = lax.axis_index("core")
    n_node = lax.axis_size("x") * lax.axis_size("z")
    slots = n_node * SLOTS
    half = slots // 2
    model = 8 * width
    hid = w_gate.shape[2]
    vmem = pltpu.CompilerParams(vmem_limit_bytes=48 * 1024 * 1024)
    hbm = pl.BlockSpec(memory_space=pl.ANY)

    near = [hidden[:, FIRST:]]
    near = near + [shift(near[0], "y", k) for k in (1, 2, 3)]
    pick, mix_hi, mix_lo, send_a = pl.pallas_call(
        route_kernel,
        out_shape=(like(tokens, slots), like(tokens, slots), like(tokens, slots), like(slots, FIRST)),
        compiler_params=vmem,
        name="route",
    )(routes, route_weights, hidden)
    a0 = over_nodes(send_a)
    send_b = pl.pallas_call(
        spread_kernel,
        out_shape=like(slots, 4 * second),
        compiler_params=vmem,
        name="spread",
    )(pick, *near)
    gate_mat, up_mat, down_mat = w_gate[0], w_up[0], w_down[0]
    gate_other, up_other, down_other = (shift(w, "core", 1) for w in (gate_mat, up_mat, down_mat))
    a1, a3 = shift(a0, "y", 1), shift(a0, "y", -1)
    b = over_nodes(send_b)
    a2_top, a2_low = shift(a1[:half], "y", 1), shift(a3[half:], "y", -1)

    place = jnp.stack([y, core]).astype(jnp.int32)

    def rows_of(columns):
        return pl.BlockSpec((half, columns), lambda i, place: (i, 0))

    def whole(columns):
        return pl.BlockSpec((half, columns), lambda i, place: (0, 0))

    partial, partial_out = pl.pallas_call(
        up_kernel,
        grid_spec=pltpu.PrefetchScalarGridSpec(
            num_scalar_prefetch=1,
            grid=(2,),
            in_specs=[rows_of(FIRST), rows_of(FIRST), whole(FIRST), whole(FIRST), rows_of(FIRST)]
            + [rows_of(4 * second)]
            + [hbm] * 4,
            out_specs=[rows_of(4 * hid)] * 2,
            scratch_shapes=[pltpu.VMEM((4 * width, 4 * hid), BF), pltpu.SemaphoreType.DMA((4, 8))],
        ),
        out_shape=(like(slots, 4 * hid, dtype=F32), like(slots, 4 * hid)),
        compiler_params=vmem,
        name="gate_up",
    )(place, a0, a1, a2_top, a2_low, a3, b, gate_mat, up_mat, gate_other, up_other)
    partial_got = shift(partial_out, "core", 1)

    a0, a1_top, a1_low, a2_top, a2_low, a3_top, a3_low, b = pl.pallas_call(
        down_kernel,
        grid_spec=pltpu.PrefetchScalarGridSpec(
            num_scalar_prefetch=1,
            grid=(2,),
            in_specs=[rows_of(4 * hid), rows_of(4 * hid), hbm, hbm],
            out_specs=[rows_of(FIRST)] + [whole(FIRST)] * 6 + [rows_of(4 * second)],
            scratch_shapes=[
                pltpu.VMEM((2 * hid, 4 * width), BF),
                pltpu.VMEM((half, 2 * hid), BF),
                pltpu.SemaphoreType.DMA((2, 8)),
            ],
        ),
        out_shape=(like(slots, FIRST),) + (like(half, FIRST),) * 6 + (like(slots, 4 * second),),
        compiler_params=vmem,
        name="down",
    )(place, partial, partial_got, down_mat, down_other)

    got1, got3 = shift(a2_top, "y", -1), shift(a2_low, "y", 1)
    left_low, right_top = shift(a1_low, "y", -1), shift(a3_top, "y", 1)
    back_b = over_nodes(b)
    a1_top, a3_low = pl.pallas_call(
        add_kernel, out_shape=(like(half, FIRST),) * 2, compiler_params=vmem, name="add"
    )(a1_top, got1, a3_low, got3)
    left_top, right_low = shift(a1_top, "y", -1), shift(a3_low, "y", 1)
    summed = pl.pallas_call(
        ysum_kernel, out_shape=like(slots, FIRST), compiler_params=vmem, name="ysum"
    )(a0, left_top, left_low, right_top, right_low)
    back_a = over_nodes(summed)
    own, *others = pl.pallas_call(
        mix_kernel,
        out_shape=(like(tokens, second, dtype=F32),) + (like(tokens, second),) * 3,
        compiler_params=vmem,
        name="mix",
    )(mix_hi, mix_lo, back_b)
    arrived = [shift(part, "y", -k) for k, part in zip((1, 2, 3), others)]
    layer_out, scaled, squares = pl.pallas_call(
        layer_kernel,
        out_shape=(like(tokens, width), like(tokens, width), like(tokens, 1, dtype=F32)),
        compiler_params=vmem,
        name="layer",
    )(hidden, mix_hi, mix_lo, back_a, own, *arrived, gain.reshape(1, width))

    everyone = lax.all_gather(scaled, AXES, axis=0, tiled=True)

    squares = squares.reshape(1, tokens)
    squares = squares + shift(squares, "core", 1)
    squares = paired([squares] + [shift(squares, "y", k) for k in (1, 2, 3)])
    for axis in ("z", "x"):
        here = lax.axis_index(axis)
        size = lax.axis_size(axis)
        order = jnp.arange(size)[:, None, None]
        gathered = jnp.where(order == here, squares[None], 0.0)
        for k in range(1, size):
            from_there = shift(squares, axis, k)
            gathered = gathered + jnp.where(order == (here - k) % size, from_there[None], 0.0)
        squares = gathered.reshape(-1, tokens)
    total_tokens = n_node * tokens
    scale = lax.rsqrt(squares.reshape(total_tokens, 1) / model + 1e-06)

    vocab_rows = head.shape[0]
    first_id = lax.axis_index(AXES) * vocab_rows
    group = 4
    stats = pl.pallas_call(
        head_kernel,
        grid_spec=pltpu.PrefetchScalarGridSpec(
            num_scalar_prefetch=1,
            grid=(n_node // group,),
            in_specs=[
                pl.BlockSpec((group, 8, tokens, width), lambda n, s: (n, 0, 0, 0)),
                pl.BlockSpec((vocab_rows, model), lambda n, s: (0, 0)),
                pl.BlockSpec((group * tokens, 1), lambda n, s: (n, 0)),
                pl.BlockSpec((group * tokens, 1), lambda n, s: (n, 0)),
            ],
            out_specs=pl.BlockSpec((8, group * tokens), lambda n, s: (0, n)),
        ),
        out_shape=like(8, total_tokens, dtype=F32),
        compiler_params=vmem,
        name="head",
    )(
        first_id.reshape(1).astype(jnp.int32),
        everyone.reshape(n_node, 8, tokens, width),
        head,
        scale,
        targets.reshape(total_tokens, 1),
    )
    stats = merged([stats, shift(stats, "core", 1)])
    for axis in ("y", "z", "x"):
        stats = merged([stats] + [shift(stats, axis, k) for k in (1, 2, 3)])
    peak, exp_total, target_logit = stats[0], stats[1], stats[2]
    ref_logp = target_logit - peak - jnp.log(exp_total)
    kl = 0.5 * (policy_logp - ref_logp) * (policy_logp - ref_logp)
    return layer_out, ref_logp, kl


def solution(mesh):
    split = Mesh(mesh.devices.reshape(4, 4, 4, 2), AXES)
    node, local = ("x", "z"), ("y", "core")
    placed = (
        P(node, local),
        P(node, None),
        P(node, None),
        P(node, None, local),
        P(node, None, local),
        P(node, local, None),
        P(local),
        P(AXES, None),
        P(),
        P(),
    )
    return jax.shard_map(
        shards,
        mesh=split,
        in_specs=placed,
        out_specs=(P(node, local), P(), P()),
        check_vma=False,
    )
```

```python
import functools
import jax
import jax.numpy as jnp
from jax import lax
from jax.experimental import pallas as pl
from jax.experimental.pallas import tpu as pltpu
from jax.sharding import Mesh, PartitionSpec as P

BF = jnp.bfloat16
F32 = jnp.float32
AXES = ("x", "z", "y", "core")
SLOTS = 40
FIRST = 512


def shift(value, axis, step):
    size = lax.axis_size(axis)
    return lax.ppermute(value, axis, [(i, (i + step) % size) for i in range(size)])


def dot(a, b):
    return jnp.dot(a, b, preferred_element_type=F32)


def route_kernel(routes_ref, weights_ref, hidden_ref, pick_ref, hi_ref, lo_ref, send_ref):
    tokens, top = routes_ref.shape
    columns = pick_ref.shape[1]
    experts = columns // SLOTS
    ids = lax.broadcasted_iota(jnp.int32, (tokens, experts), 1)
    named = jnp.zeros((tokens, experts), F32)
    gates = jnp.zeros((tokens, experts), F32)
    for k in range(top):
        hit = routes_ref[:, k : k + 1] == ids
        named = named + jnp.where(hit, 1.0, 0.0)
        gates = gates + jnp.where(hit, weights_ref[:, k : k + 1], 0.0)
    row = lax.broadcasted_iota(jnp.int32, (tokens, tokens), 0)
    col = lax.broadcasted_iota(jnp.int32, (tokens, tokens), 1)
    before = jnp.where(col < row, 1.0, 0.0).astype(BF)
    count = dot(before, named.astype(BF))
    expert = lax.broadcasted_iota(jnp.int32, (experts, columns), 0)
    column = lax.broadcasted_iota(jnp.int32, (experts, columns), 1)
    inside = (column >= expert * SLOTS) & (column < expert * SLOTS + SLOTS)
    spread = jnp.where(inside, 1.0, 0.0).astype(BF)
    slot = jnp.sum(jnp.where(inside, column - expert * SLOTS, 0).astype(F32), axis=0, keepdims=True)
    gates_hi = gates.astype(BF)
    gates_lo = (gates - gates_hi.astype(F32)).astype(BF)
    placed = (dot(named.astype(BF), spread) > 0.5) & (dot(count.astype(BF), spread) == slot)
    hi_ref[...] = jnp.where(placed, dot(gates_hi, spread), 0.0).astype(BF)
    lo_ref[...] = jnp.where(placed, dot(gates_lo, spread), 0.0).astype(BF)
    pick = jnp.where(placed, 1.0, 0.0).astype(BF)
    pick_ref[...] = pick
    send_ref[...] = picked(pick, hidden_ref[:, :FIRST]).astype(BF)


def picked(pick, rows):
    return lax.dot_general(pick, rows, (((0,), (0,)), ((), ())), preferred_element_type=F32)


def spread_kernel(pick_ref, h0, h1, h2, h3, send_ref):
    width = h0.shape[1]
    for k, ref in enumerate((h0, h1, h2, h3)):
        send_ref[:, k * width : (k + 1) * width] = picked(pick_ref[...], ref[...]).astype(BF)


def block_of(place_ref, k):
    return 2 * lax.rem(place_ref[0] + 4 - k, 4) + place_ref[1]


def up_kernel(place_ref, a0, a1, a2_top, a2_low, a3, b_ref, w0, w1, w2, w3, sum_ref, out_ref, w_ref, sems):
    step = pl.program_id(0)
    hidden = w0.shape[1]
    width = w0.shape[0] // 8
    second = width - FIRST

    def copies():
        made = []
        for j, w in enumerate((w0, w1, w2, w3)):
            cols = pl.ds(j * hidden, hidden)
            for k in range(4):
                start = pl.multiple_of(block_of(place_ref, k) * width, 128)
                made.append(
                    pltpu.make_async_copy(
                        w.at[pl.ds(start, FIRST), :],
                        w_ref.at[pl.ds(k * FIRST, FIRST), cols],
                        sems.at[j, 2 * k],
                    )
                )
                made.append(
                    pltpu.make_async_copy(
                        w.at[pl.ds(start + FIRST, second), :],
                        w_ref.at[pl.ds(4 * FIRST + k * second, second), cols],
                        sems.at[j, 2 * k + 1],
                    )
                )
        return made

    @pl.when(step == 0)
    def _():
        for copy in copies():
            copy.start()
        for copy in copies():
            copy.wait()

    def total(a2):
        for j in range(4):
            cols = slice(j * hidden, (j + 1) * hidden)
            part = dot(b_ref[...], w_ref[4 * FIRST :, cols])
            for k, ref in enumerate((a0, a1, a2, a3)):
                part = part + dot(ref[...], w_ref[k * FIRST : (k + 1) * FIRST, cols])
            sum_ref[:, cols] = part
            out_ref[:, cols] = part.astype(BF)

    @pl.when(step == 0)
    def _():
        total(a2_top)

    @pl.when(step == 1)
    def _():
        total(a2_low)


def down_kernel(
    place_ref, sum_ref, got_ref, w0, w1, a0, a1_top, a1_low, a2_top, a2_low, a3_top, a3_low, b_ref,
    w_ref, act_ref, done_ref, sems, out_sems
):
    step = pl.program_id(0)
    hidden = w0.shape[0]
    width = w0.shape[1] // 8
    second = width - FIRST

    def copies():
        made = []
        for j, w in enumerate((w0, w1)):
            rows = pl.ds(j * hidden, hidden)
            for k in range(4):
                start = pl.multiple_of(block_of(place_ref, k) * width, 128)
                made.append(
                    pltpu.make_async_copy(
                        w.at[:, pl.ds(start, FIRST)],
                        w_ref.at[rows, pl.ds(k * FIRST, FIRST)],
                        sems.at[j, 2 * k],
                    )
                )
                made.append(
                    pltpu.make_async_copy(
                        w.at[:, pl.ds(start + FIRST, second)],
                        w_ref.at[rows, pl.ds(4 * FIRST + k * second, second)],
                        sems.at[j, 2 * k + 1],
                    )
                )
        return made

    @pl.when(step == 0)
    def _():
        for copy in copies():
            copy.start()

    for j in range(2):
        own, got = 2 * j * hidden, 2 * (1 - j) * hidden
        gate = sum_ref[:, own : own + hidden] + got_ref[:, got : got + hidden].astype(F32)
        up = sum_ref[:, own + hidden : own + 2 * hidden] + got_ref[
            :, got + hidden : got + 2 * hidden
        ].astype(F32)
        act_ref[:, j * hidden : (j + 1) * hidden] = (gate / (1.0 + jnp.exp(-gate)) * up).astype(BF)

    @pl.when(step == 0)
    def _():
        for copy in copies():
            copy.wait()

    def out(start, size):
        return dot(act_ref[...], w_ref[:, start : start + size]).astype(BF)

    def send(targets):
        moves = []
        for i, (k, ref) in enumerate(targets):
            done_ref[i] = out(k * FIRST, FIRST)
            moves.append(pltpu.make_async_copy(done_ref.at[i], ref, out_sems.at[i]))
            moves[-1].start()
        a0[...] = out(0, FIRST)
        b_ref[...] = out(4 * FIRST, 4 * second)
        for move in moves:
            move.wait()

    @pl.when(step == 0)
    def _():
        send(((2, a2_top), (1, a1_top), (3, a3_top)))

    @pl.when(step == 1)
    def _():
        send(((2, a2_low), (1, a1_low), (3, a3_low)))


def add_kernel(a1, got1, a3, got3, out1, out3):
    out1[...] = (a1[...].astype(F32) + got1[...].astype(F32)).astype(BF)
    out3[...] = (a3[...].astype(F32) + got3[...].astype(F32)).astype(BF)


def ysum_kernel(a0, left_top, left_low, right_top, right_low, out_ref):
    half = left_top.shape[0]
    top = a0[:half].astype(F32) + left_top[...].astype(F32) + right_top[...].astype(F32)
    low = a0[half:].astype(F32) + left_low[...].astype(F32) + right_low[...].astype(F32)
    out_ref[:half] = top.astype(BF)
    out_ref[half:] = low.astype(BF)


def mix_kernel(hi_ref, lo_ref, back_ref, own_ref, p1, p2, p3):
    width = own_ref.shape[1]
    for k, ref in enumerate((own_ref, p1, p2, p3)):
        block = back_ref[:, k * width : (k + 1) * width]
        total = dot(hi_ref[...], block) + dot(lo_ref[...], block)
        ref[...] = total.astype(ref.dtype)


def layer_kernel(
    hidden_ref, hi_ref, lo_ref, back_ref, own_ref, p1, p2, p3, gain_ref, out_ref, scaled_ref
):
    first = dot(hi_ref[...], back_ref[...]) + dot(lo_ref[...], back_ref[...])
    second = own_ref[...] + p1[...].astype(F32) + p2[...].astype(F32) + p3[...].astype(F32)
    for mix, cols in ((first, slice(0, FIRST)), (second, slice(FIRST, hidden_ref.shape[1]))):
        total = hidden_ref[:, cols].astype(F32) + mix
        out_ref[:, cols] = total.astype(BF)
        scaled_ref[:, cols] = (total * gain_ref[:, cols]).astype(BF)


def head_kernel(place_ref, inverse_ref, w0, w1, *refs):
    *pieces, own_ref, other_ref, w_ref, sems = refs
    vocab = w0.shape[0]
    width = w0.shape[1] // 8

    def copies(k):
        start = pl.multiple_of(block_of(place_ref, k) * width, 128)
        return [
            pltpu.make_async_copy(
                w.at[:, pl.ds(start, width)],
                w_ref.at[k, pl.ds(j * vocab, vocab), :],
                sems.at[j, k],
            )
            for j, w in enumerate((w0, w1))
        ]

    for k in range(4):
        for copy in copies(k):
            copy.start()
    squares = jnp.zeros((own_ref.shape[0], 128), F32)
    for k in range(4):
        rows = [piece[:, k].reshape(piece.shape[0] * piece.shape[2], width) for piece in pieces]
        rows = jnp.concatenate(rows, axis=0)
        for copy in copies(k):
            copy.wait()
        for j, ref in enumerate((own_ref, other_ref)):
            part = lax.dot_general(
                rows,
                w_ref[k, j * vocab : (j + 1) * vocab, :],
                (((1,), (1,)), ((), ())),
                preferred_element_type=F32,
            )
            if k == 0:
                ref[:, :vocab] = part
            else:
                ref[:, :vocab] += part
        for c in range(0, width, 128):
            value = rows[:, c : c + 128].astype(F32)
            squares = squares + value * value * inverse_ref[k : k + 1, c : c + 128]
    own_ref[:, vocab:] = squares
    other_ref[:, vocab:] = squares


def stats_kernel(model, first_ref, order_ref, own_ref, got_ref, wanted_ref, before_ref, stats_ref):
    vocab = own_ref.shape[1] - 128
    blocks, tokens, _ = wanted_ref.shape
    stats_ref[...] = before_ref[...]
    ids = first_ref[0] + lax.broadcasted_iota(jnp.int32, (tokens, vocab), 1)
    lane = lax.broadcasted_iota(jnp.int32, (tokens, 128), 1)
    for i in range(own_ref.shape[0] // tokens):
        rows = slice(i * tokens, (i + 1) * tokens)
        block = order_ref[i]
        squares = jnp.sum(own_ref[rows, vocab:] + got_ref[rows, vocab:], axis=1, keepdims=True)
        scale = lax.rsqrt(squares / model + 1e-06)
        full = (own_ref[rows, :vocab] + got_ref[rows, :vocab]) * scale
        peak = jnp.max(full, axis=1, keepdims=True)
        total = jnp.sum(jnp.exp(full - peak), axis=1, keepdims=True)
        target = jnp.sum(jnp.where(ids == wanted_ref[block], full, 0.0), axis=1, keepdims=True)
        columns = jnp.where(lane == 0, peak, jnp.where(lane == 1, total, target)).T
        for j in range(3):
            stats_ref[pl.ds(j * blocks + block, 1), :tokens] = columns[j : j + 1]


def paired(terms):
    while len(terms) > 1:
        terms = [terms[i] + terms[i + 1] for i in range(0, len(terms), 2)]
    return terms[0]


def combined(values_ref):
    members = values_ref.shape[0]
    third = values_ref.shape[1] // 3
    peaks = [values_ref[i, :third] for i in range(members)]
    peak = functools.reduce(jnp.maximum, peaks)
    total = paired([values_ref[i, third : 2 * third] * jnp.exp(peaks[i] - peak) for i in range(members)])
    target = paired([values_ref[i, 2 * third :] for i in range(members)])
    return peak, total, target


def merge_kernel(values_ref, out_ref):
    third = values_ref.shape[1] // 3
    for j, value in enumerate(combined(values_ref)):
        out_ref[j * third : (j + 1) * third] = value


def final_kernel(values_ref, policy_ref, logp_ref, kl_ref):
    tokens = policy_ref.shape[1]
    peak, total, target = (value[:, :tokens] for value in combined(values_ref))
    logp = target - peak - jnp.log(total)
    logp_ref[...] = logp
    kl_ref[...] = 0.5 * (policy_ref[...] - logp) * (policy_ref[...] - logp)


def spread_over(stats, axes):
    size = lax.axis_size(axes)
    copies = jnp.broadcast_to(stats[None], (size,) + stats.shape)
    return lax.all_to_all(copies, axes, split_axis=0, concat_axis=0, tiled=True)


def ring(block, axis):
    half = block.shape[0] // 2
    behind, ahead = shift(block, axis, 1), shift(block, axis, -1)
    return behind, shift(behind[:half], axis, 1), shift(ahead[half:], axis, -1), ahead


def like(*shape, dtype=BF):
    return jax.ShapeDtypeStruct(shape, dtype)


def over_nodes(rows):
    nodes = lax.axis_size("x") * lax.axis_size("z")
    cut = rows.reshape(nodes, rows.shape[0] // nodes, rows.shape[1])
    return lax.all_to_all(cut, ("x", "z"), split_axis=0, concat_axis=0, tiled=True).reshape(rows.shape)


def shards(hidden, routes, route_weights, w_gate, w_up, w_down, gain, head, targets, policy_logp):
    tokens, width = hidden.shape
    second = width - FIRST
    y = lax.axis_index("y")
    core = lax.axis_index("core")
    n_node = lax.axis_size("x") * lax.axis_size("z")
    slots = n_node * SLOTS
    half = slots // 2
    model = 8 * width
    hid = w_gate.shape[2]
    vmem = pltpu.CompilerParams(vmem_limit_bytes=48 * 1024 * 1024)
    hbm = pl.BlockSpec(memory_space=pl.ANY)
    in_hbm = pl.BlockSpec(memory_space=pltpu.HBM)

    near_own, routed = lax.optimization_barrier((hidden[:, FIRST:], hidden))
    near = [near_own]
    near = near + [shift(near[0], "y", k) for k in (1, 2, 3)]
    pick, mix_hi, mix_lo, send_a = pl.pallas_call(
        route_kernel,
        out_shape=(like(tokens, slots), like(tokens, slots), like(tokens, slots), like(slots, FIRST)),
        compiler_params=vmem,
        name="route",
    )(routes, route_weights, routed)
    a0 = over_nodes(send_a)
    send_b = pl.pallas_call(
        spread_kernel,
        out_shape=like(slots, 4 * second),
        compiler_params=vmem,
        name="spread",
    )(pick, *near)
    gate_mat, up_mat, down_mat = w_gate[0], w_up[0], w_down[0]
    gate_other, up_other, down_other = (shift(w, "core", 1) for w in (gate_mat, up_mat, down_mat))
    a0, send_b = lax.optimization_barrier((a0, send_b))
    a1, a3 = shift(a0, "y", 1), shift(a0, "y", -1)
    b = over_nodes(send_b)
    a2_top, a2_low = shift(a1[:half], "y", 1), shift(a3[half:], "y", -1)

    head_other = shift(head, "core", 1)
    squared = (1.0 / (gain * gain)).reshape(1, width)
    inverse = jnp.concatenate([squared] + [shift(squared, "y", k) for k in (1, 2, 3)])
    place = jnp.stack([y, core]).astype(jnp.int32)

    def rows_of(columns):
        return pl.BlockSpec((half, columns), lambda i, place: (i, 0))

    def whole(columns):
        return pl.BlockSpec((half, columns), lambda i, place: (0, 0))

    partial, partial_out = pl.pallas_call(
        up_kernel,
        grid_spec=pltpu.PrefetchScalarGridSpec(
            num_scalar_prefetch=1,
            grid=(2,),
            in_specs=[rows_of(FIRST), rows_of(FIRST), whole(FIRST), whole(FIRST), rows_of(FIRST)]
            + [rows_of(4 * second)]
            + [hbm] * 4,
            out_specs=[rows_of(4 * hid)] * 2,
            scratch_shapes=[pltpu.VMEM((4 * width, 4 * hid), BF), pltpu.SemaphoreType.DMA((4, 8))],
        ),
        out_shape=(like(slots, 4 * hid, dtype=F32), like(slots, 4 * hid)),
        compiler_params=vmem,
        name="gate_up",
    )(place, a0, a1, a2_top, a2_low, a3, b, gate_mat, up_mat, gate_other, up_other)
    partial_got = shift(partial_out, "core", 1)

    a0, a1_top, a1_low, a2_top, a2_low, a3_top, a3_low, b = pl.pallas_call(
        down_kernel,
        grid_spec=pltpu.PrefetchScalarGridSpec(
            num_scalar_prefetch=1,
            grid=(2,),
            in_specs=[rows_of(4 * hid), rows_of(4 * hid), hbm, hbm],
            out_specs=[rows_of(FIRST)] + [in_hbm] * 6 + [rows_of(4 * second)],
            scratch_shapes=[
                pltpu.VMEM((2 * hid, 4 * width), BF),
                pltpu.VMEM((half, 2 * hid), BF),
                pltpu.VMEM((3, half, FIRST), BF),
                pltpu.SemaphoreType.DMA((2, 8)),
                pltpu.SemaphoreType.DMA((3,)),
            ],
        ),
        out_shape=(like(slots, FIRST),) + (like(half, FIRST),) * 6 + (like(slots, 4 * second),),
        compiler_params=vmem,
        name="down",
    )(place, partial, partial_got, down_mat, down_other)

    got1, got3 = shift(a2_top, "y", -1), shift(a2_low, "y", 1)
    left_low, right_top = shift(a1_low, "y", -1), shift(a3_top, "y", 1)
    back_b = over_nodes(b)
    a1_top, a3_low = pl.pallas_call(
        add_kernel, out_shape=(like(half, FIRST),) * 2, compiler_params=vmem, name="add"
    )(a1_top, got1, a3_low, got3)
    left_top, right_low = shift(a1_top, "y", -1), shift(a3_low, "y", 1)
    summed = pl.pallas_call(
        ysum_kernel, out_shape=like(slots, FIRST), compiler_params=vmem, name="ysum"
    )(a0, left_top, left_low, right_top, right_low)
    back_a = over_nodes(summed)
    own, *others = pl.pallas_call(
        mix_kernel,
        out_shape=(like(tokens, second, dtype=F32),) + (like(tokens, second),) * 3,
        compiler_params=vmem,
        name="mix",
    )(mix_hi, mix_lo, back_b)
    arrived = [shift(part, "y", -k) for k, part in zip((1, 2, 3), others)]
    layer_out, scaled = pl.pallas_call(
        layer_kernel,
        out_shape=(like(tokens, width), like(tokens, width)),
        compiler_params=vmem,
        name="layer",
    )(hidden, mix_hi, mix_lo, back_a, own, *arrived, gain.reshape(1, width))

    by_y = [scaled] + [shift(scaled, "y", k) for k in (1, 2, 3)]
    part = tokens // 2
    part_a = jnp.stack([rows[:part] for rows in by_y])
    part_b = jnp.stack([rows[part:] for rows in by_y])
    behind_a, far_a1, far_a2, ahead_a = ring(part_a, "x")
    behind_b, far_b1, far_b2, ahead_b = ring(part_b, "z")
    line_a = jnp.stack([part_a, behind_a, jnp.concatenate([far_a1, far_a2]), ahead_a])
    line_b = jnp.stack([part_b, behind_b, jnp.concatenate([far_b1, far_b2]), ahead_b])
    behind_a, far_a1, far_a2, ahead_a = ring(line_a, "z")
    behind_b, far_b1, far_b2, ahead_b = ring(line_b, "x")

    vocab_rows = head.shape[0]
    first_id = (lax.axis_index(AXES) * vocab_rows).reshape(1).astype(jnp.int32)
    x, z = lax.axis_index("x"), lax.axis_index("z")
    blocks = 2 * n_node
    wanted = targets.reshape(blocks, part, 1)

    def block_at(back_x, back_z, which):
        return (((x - back_x) % 4) * 4 + (z - back_z) % 4) * 2 + which

    def scored(pieces, order, stats):
        rows = sum(piece.shape[0] for piece in pieces) * part
        own, other = pl.pallas_call(
            head_kernel,
            grid_spec=pltpu.PrefetchScalarGridSpec(
                num_scalar_prefetch=1,
                grid=(),
                in_specs=[pl.BlockSpec(memory_space=pltpu.VMEM)]
                + [hbm] * 2
                + [pl.BlockSpec(memory_space=pltpu.VMEM)] * len(pieces),
                out_specs=[pl.BlockSpec(memory_space=pltpu.VMEM)] * 2,
                scratch_shapes=[
                    pltpu.VMEM((4, 2 * vocab_rows, width), BF),
                    pltpu.SemaphoreType.DMA((2, 4)),
                ],
            ),
            out_shape=(like(rows, vocab_rows + 128, dtype=F32),) * 2,
            compiler_params=vmem,
            cost_estimate=pl.CostEstimate(
                flops=2 * rows * 4 * width * 2 * vocab_rows,
                bytes_accessed=16 * width * vocab_rows,
                transcendentals=0,
            ),
            name="head",
        )(place, inverse, head, head_other, *pieces)
        got = shift(other, "core", 1)
        return pl.pallas_call(
            functools.partial(stats_kernel, model),
            grid_spec=pltpu.PrefetchScalarGridSpec(
                num_scalar_prefetch=2,
                grid=(),
                in_specs=[pl.BlockSpec(memory_space=pltpu.VMEM)] * 4,
                out_specs=pl.BlockSpec(memory_space=pltpu.VMEM),
            ),
            out_shape=like(3 * blocks, 128, dtype=F32),
            compiler_params=vmem,
            name="stats",
        )(first_id, jnp.stack(order).astype(jnp.int32), own, got, wanted, stats)

    stats = jnp.zeros((3 * blocks, 128), F32)
    stats = scored(
        [line_a, line_b],
        [block_at(i, 0, 0) for i in range(4)] + [block_at(0, i, 1) for i in range(4)],
        stats,
    )
    stats = scored(
        [behind_a, ahead_a, behind_b, ahead_b],
        [block_at(i, k, 0) for k in (1, 3) for i in range(4)]
        + [block_at(k, i, 1) for k in (1, 3) for i in range(4)],
        stats,
    )
    stats = scored(
        [far_a1, far_a2, far_b1, far_b2],
        [block_at(i, 2, 0) for i in range(4)] + [block_at(2, i, 1) for i in range(4)],
        stats,
    )
    stats = pl.pallas_call(
        merge_kernel, out_shape=like(3 * blocks, 128, dtype=F32), name="merge"
    )(spread_over(stats, ("y", "core")))
    ref_logp, kl = pl.pallas_call(
        final_kernel, out_shape=(like(blocks, part, dtype=F32),) * 2, name="final"
    )(spread_over(stats, ("x", "z")), policy_logp.reshape(blocks, part))
    return layer_out, ref_logp.reshape(-1), kl.reshape(-1)


def solution(mesh):
    split = Mesh(mesh.devices.reshape(4, 4, 4, 2), AXES)
    node, local = ("x", "z"), ("y", "core")
    placed = (
        P(node, local),
        P(node, None),
        P(node, None),
        P(node, None, local),
        P(node, None, local),
        P(node, local, None),
        P(local),
        P(AXES, None),
        P(),
        P(),
    )
    return jax.shard_map(
        shards,
        mesh=split,
        in_specs=placed,
        out_specs=(P(node, local), P(), P()),
        check_vma=False,
    )
```

```python
import functools
import jax
import jax.numpy as jnp
from jax import lax
from jax.experimental import pallas as pl
from jax.experimental.pallas import tpu as pltpu
from jax.sharding import Mesh, PartitionSpec as P

BF = jnp.bfloat16
F32 = jnp.float32
AXES = ("x", "z", "y", "core")
SLOTS = 40
FIRST = 512
VMEM = 48


def shift(value, axis, step):
    size = lax.axis_size(axis)
    return lax.ppermute(value, axis, [(i, (i + step) % size) for i in range(size)])


def dot(a, b):
    return jnp.dot(a, b, preferred_element_type=F32)


def near_kernel(hidden_ref, gain_ref, near_ref):
    tokens, width = hidden_ref.shape
    second = near_ref.shape[1]
    near_ref[:tokens] = hidden_ref[:, FIRST:]
    gain = gain_ref[...]
    hi = gain.astype(BF).astype(F32)
    rows = jnp.zeros((near_ref.shape[0] - tokens, second), F32)
    row = lax.broadcasted_iota(jnp.int32, rows.shape, 0)
    for i, part in enumerate((hi, gain - hi)):
        for j, start in enumerate(range(0, width, second)):
            piece = part[:, start : start + second]
            piece = jnp.pad(piece, ((0, 0), (0, second - piece.shape[1])))
            rows = jnp.where(row == 4 * i + j, piece, rows)
    near_ref[tokens:] = rows.astype(BF)


def route_kernel(routes_ref, weights_ref, hidden_ref, pick_ref, hi_ref, lo_ref, send_ref):
    tokens, top = routes_ref.shape
    columns = pick_ref.shape[1]
    experts = columns // SLOTS
    ids = lax.broadcasted_iota(jnp.int32, (tokens, experts), 1)
    named = jnp.zeros((tokens, experts), F32)
    gates = jnp.zeros((tokens, experts), F32)
    for k in range(top):
        hit = routes_ref[:, k : k + 1] == ids
        named = named + jnp.where(hit, 1.0, 0.0)
        gates = gates + jnp.where(hit, weights_ref[:, k : k + 1], 0.0)
    row = lax.broadcasted_iota(jnp.int32, (tokens, tokens), 0)
    col = lax.broadcasted_iota(jnp.int32, (tokens, tokens), 1)
    before = jnp.where(col < row, 1.0, 0.0).astype(BF)
    count = dot(before, named.astype(BF))
    expert = lax.broadcasted_iota(jnp.int32, (experts, columns), 0)
    column = lax.broadcasted_iota(jnp.int32, (experts, columns), 1)
    inside = (column >= expert * SLOTS) & (column < expert * SLOTS + SLOTS)
    spread = jnp.where(inside, 1.0, 0.0).astype(BF)
    slot = jnp.sum(jnp.where(inside, column - expert * SLOTS, 0).astype(F32), axis=0, keepdims=True)
    gates_hi = gates.astype(BF)
    gates_lo = (gates - gates_hi.astype(F32)).astype(BF)
    placed = (dot(named.astype(BF), spread) > 0.5) & (dot(count.astype(BF), spread) == slot)
    hi_ref[...] = jnp.where(placed, dot(gates_hi, spread), 0.0).astype(BF)
    lo_ref[...] = jnp.where(placed, dot(gates_lo, spread), 0.0).astype(BF)
    pick = jnp.where(placed, 1.0, 0.0).astype(BF)
    pick_ref[...] = pick
    send_ref[...] = picked(pick, hidden_ref[:, :FIRST]).astype(BF)


def picked(pick, rows):
    return lax.dot_general(pick, rows, (((0,), (0,)), ((), ())), preferred_element_type=F32)


def spread_kernel(pick_ref, h0, h1, h2, h3, send_ref, inverse_ref):
    tokens = pick_ref.shape[0]
    second = h0.shape[1]
    width = inverse_ref.shape[1]
    for k, ref in enumerate((h0, h1, h2, h3)):
        send_ref[:, k * second : (k + 1) * second] = picked(pick_ref[...], ref[:tokens]).astype(BF)
        rows = ref[tokens:].astype(F32)
        for j, start in enumerate(range(0, width, second)):
            size = min(second, width - start)
            gain = rows[j : j + 1, :size] + rows[4 + j : 5 + j, :size]
            inverse_ref[k : k + 1, start : start + size] = 1.0 / (gain * gain)


def block_of(place_ref, k):
    return 2 * lax.rem(place_ref[0] + 4 - k, 4) + place_ref[1]


def up_kernel(place_ref, a0, a1, a2_top, a2_low, a3, b_ref, w0, w1, w2, w3, sum_ref, out_ref, w_ref, sems):
    step = pl.program_id(0)
    hidden = w0.shape[1]
    width = w0.shape[0] // 8
    second = width - FIRST

    def copies():
        made = []
        for j, w in enumerate((w0, w1, w2, w3)):
            cols = pl.ds(j * hidden, hidden)
            for k in range(4):
                start = pl.multiple_of(block_of(place_ref, k) * width, 128)
                made.append(
                    pltpu.make_async_copy(
                        w.at[pl.ds(start, FIRST), :],
                        w_ref.at[pl.ds(k * FIRST, FIRST), cols],
                        sems.at[j, 2 * k],
                    )
                )
                made.append(
                    pltpu.make_async_copy(
                        w.at[pl.ds(start + FIRST, second), :],
                        w_ref.at[pl.ds(4 * FIRST + k * second, second), cols],
                        sems.at[j, 2 * k + 1],
                    )
                )
        return made

    @pl.when(step == 0)
    def _():
        for copy in copies():
            copy.start()
        for copy in copies():
            copy.wait()

    def total(a2):
        for j in range(4):
            cols = slice(j * hidden, (j + 1) * hidden)
            part = dot(b_ref[...], w_ref[4 * FIRST :, cols])
            for k, ref in enumerate((a0, a1, a2, a3)):
                part = part + dot(ref[...], w_ref[k * FIRST : (k + 1) * FIRST, cols])
            sum_ref[:, cols] = part
            out_ref[:, cols] = part.astype(BF)

    @pl.when(step == 0)
    def _():
        total(a2_top)

    @pl.when(step == 1)
    def _():
        total(a2_low)


def down_kernel(
    place_ref, sum_ref, got_ref, w0, w1, a0, a1_top, a1_low, a2_top, a2_low, a3_top, a3_low, b_ref,
    w_ref, act_ref, sems
):
    step = pl.program_id(0)
    hidden = w0.shape[0]
    width = w0.shape[1] // 8
    second = width - FIRST

    def copies():
        made = []
        for j, w in enumerate((w0, w1)):
            rows = pl.ds(j * hidden, hidden)
            for k in range(4):
                start = pl.multiple_of(block_of(place_ref, k) * width, 128)
                made.append(
                    pltpu.make_async_copy(
                        w.at[:, pl.ds(start, FIRST)],
                        w_ref.at[rows, pl.ds(k * FIRST, FIRST)],
                        sems.at[j, 2 * k],
                    )
                )
                made.append(
                    pltpu.make_async_copy(
                        w.at[:, pl.ds(start + FIRST, second)],
                        w_ref.at[rows, pl.ds(4 * FIRST + k * second, second)],
                        sems.at[j, 2 * k + 1],
                    )
                )
        return made

    @pl.when(step == 0)
    def _():
        for copy in copies():
            copy.start()

    for j in range(2):
        own, got = 2 * j * hidden, 2 * (1 - j) * hidden
        gate = sum_ref[:, own : own + hidden] + got_ref[:, got : got + hidden].astype(F32)
        up = sum_ref[:, own + hidden : own + 2 * hidden] + got_ref[
            :, got + hidden : got + 2 * hidden
        ].astype(F32)
        act_ref[:, j * hidden : (j + 1) * hidden] = (gate / (1.0 + jnp.exp(-gate)) * up).astype(BF)

    @pl.when(step == 0)
    def _():
        for copy in copies():
            copy.wait()

    def out(start, size):
        return dot(act_ref[...], w_ref[:, start : start + size]).astype(BF)

    a0[...] = out(0, FIRST)
    b_ref[...] = out(4 * FIRST, 4 * second)

    @pl.when(step == 0)
    def _():
        for k, ref in ((1, a1_top), (2, a2_top), (3, a3_top)):
            ref[...] = out(k * FIRST, FIRST)

    @pl.when(step == 1)
    def _():
        for k, ref in ((1, a1_low), (2, a2_low), (3, a3_low)):
            ref[...] = out(k * FIRST, FIRST)


def add_kernel(a1, got1, a3, got3, out1, out3):
    out1[...] = (a1[...].astype(F32) + got1[...].astype(F32)).astype(BF)
    out3[...] = (a3[...].astype(F32) + got3[...].astype(F32)).astype(BF)


def ysum_kernel(a0, left_top, left_low, right_top, right_low, out_ref):
    half = left_top.shape[0]
    top = a0[:half].astype(F32) + left_top[...].astype(F32) + right_top[...].astype(F32)
    low = a0[half:].astype(F32) + left_low[...].astype(F32) + right_low[...].astype(F32)
    out_ref[:half] = top.astype(BF)
    out_ref[half:] = low.astype(BF)


def mix_kernel(hi_ref, lo_ref, back_ref, own_ref, p1, p2, p3):
    width = own_ref.shape[1]
    for k, ref in enumerate((own_ref, p1, p2, p3)):
        block = back_ref[:, k * width : (k + 1) * width]
        total = dot(hi_ref[...], block) + dot(lo_ref[...], block)
        ref[...] = total.astype(ref.dtype)


def layer_kernel(hidden_ref, hi_ref, lo_ref, back_ref, own_ref, p1, p2, p3, gain_ref, out_ref, scaled_ref):
    first = dot(hi_ref[...], back_ref[...]) + dot(lo_ref[...], back_ref[...])
    second = own_ref[...] + p1[...].astype(F32) + p2[...].astype(F32) + p3[...].astype(F32)
    for mix, cols in ((first, slice(0, FIRST)), (second, slice(FIRST, hidden_ref.shape[1]))):
        total = hidden_ref[:, cols].astype(F32) + mix
        out_ref[:, cols] = total.astype(BF)
        scaled_ref[:, cols] = (total * gain_ref[:, cols]).astype(BF)


def squares_of(rows, inverse):
    total = jnp.zeros((rows.shape[0], 128), F32)
    for c in range(0, rows.shape[1], 128):
        value = rows[:, c : c + 128].astype(F32)
        total = total + value * value * inverse[:, c : c + 128]
    return total


def half_head_kernel(place_ref, inverse_ref, w0, w1, *refs):
    *pieces, own_ref, other_ref, w_ref, rows_ref, sems = refs
    vocab = w0.shape[0]
    tokens, width = pieces[0].shape[2:]
    line_a, behind_a, far_a1, far_a2, ahead_a = pieces[:5]
    line_b, behind_b, far_b1, far_b2, ahead_b = pieces[5:]

    copies = []
    for j, w in enumerate((w0, w1)):
        for k in range(4):
            start = pl.multiple_of(block_of(place_ref, k) * width, 128)
            copies.append(
                pltpu.make_async_copy(
                    w.at[:, pl.ds(start, width)],
                    w_ref.at[pl.ds(j * vocab, vocab), pl.ds(k * width, width)],
                    sems.at[j, k],
                )
            )
    for copy in copies:
        copy.start()

    def piece_of(line, behind, far1, far2, ahead, along, across):
        if along == 2:
            return (far1, across) if across < 2 else (far2, across - 2)
        return ({0: line, 1: behind, 3: ahead}[along], across)

    for back_x in range(4):
        for back_z in range(4):
            at = (back_x * 4 + back_z) * tokens
            squares = 0.0
            for ref, i, base in (
                piece_of(line_a, behind_a, far_a1, far_a2, ahead_a, back_z, back_x) + (0,),
                piece_of(line_b, behind_b, far_b1, far_b2, ahead_b, back_x, back_z) + (2,),
            ):
                for k in range(2):
                    rows = ref[i, k]
                    first = (base + k) * width
                    rows_ref[at : at + tokens, first : first + width] = rows
                    squares = squares + squares_of(rows, inverse_ref[base + k : base + k + 1])
            own_ref[at : at + tokens, vocab:] = squares
            other_ref[at : at + tokens, vocab:] = squares
    for copy in copies:
        copy.wait()
    for at in range(0, rows_ref.shape[0], 384):
        for j, ref in ((1, other_ref), (0, own_ref)):
            ref[at : at + 384, :vocab] = lax.dot_general(
                rows_ref[at : at + 384],
                w_ref[j * vocab : (j + 1) * vocab, :],
                (((1,), (1,)), ((), ())),
                preferred_element_type=F32,
            )


def columns_of(full, ids, wanted):
    peak = jnp.max(full, axis=1, keepdims=True)
    total = jnp.sum(jnp.exp(full - peak), axis=1, keepdims=True)
    target = jnp.sum(jnp.where(ids == wanted, full, 0.0), axis=1, keepdims=True)
    lane = lax.broadcasted_iota(jnp.int32, (full.shape[0], 128), 1)
    return jnp.where(lane == 0, peak, jnp.where(lane == 1, total, target)).T


def whole_head_kernel(model, first_ref, place_ref, rows_ref, head_ref, own_ref, other_ref, wanted_ref, stats_ref):
    nodes, parts, tokens, width = rows_ref.shape
    rows = jnp.concatenate([rows_ref[:, p].reshape(nodes * tokens, width) for p in range(parts)], axis=1)
    logits = lax.dot_general(rows, head_ref[...], (((1,), (1,)), ((), ())), preferred_element_type=F32)
    squares = 0.0
    for p in range(parts):
        k = lax.rem(place_ref[0] + 4 - p // 2, 4)
        mine = place_ref[1] == p % 2
        inverse = jnp.where(mine, own_ref[pl.ds(k, 1), :], other_ref[pl.ds(k, 1), :])
        squares = squares + squares_of(rows[:, p * width : (p + 1) * width], inverse)
    scale = lax.rsqrt(jnp.sum(squares, axis=1, keepdims=True) / model + 1e-06)
    ids = first_ref[0] + lax.broadcasted_iota(jnp.int32, logits.shape, 1)
    columns = columns_of(logits * scale, ids, wanted_ref[...])
    stats_ref[...] = columns[:8]


def stats_kernel(model, first_ref, order_ref, own_ref, got_ref, wanted_ref, whole_ref, stats_ref):
    vocab = own_ref.shape[1] - 128
    nodes, tokens, _ = wanted_ref.shape
    wanted = jnp.concatenate([wanted_ref[order_ref[i]] for i in range(nodes)], axis=0)
    squares = jnp.sum(own_ref[:, vocab:] + got_ref[:, vocab:], axis=1, keepdims=True)
    scale = lax.rsqrt(squares / model + 1e-06)
    full = (own_ref[:, :vocab] + got_ref[:, :vocab]) * scale
    ids = first_ref[0] + lax.broadcasted_iota(jnp.int32, full.shape, 1)
    columns = columns_of(full, ids, wanted)
    stats_ref[...] = jnp.zeros_like(stats_ref)
    for i in range(nodes):
        lanes = slice(i * tokens, (i + 1) * tokens)
        for j in range(3):
            stats_ref[j * nodes + i : j * nodes + i + 1, :tokens] = whole_ref[j : j + 1, lanes]
            row = j * nodes + order_ref[i]
            stats_ref[pl.ds(row, 1), 64 : 64 + tokens] = columns[j : j + 1, lanes]


def paired(terms):
    if len(terms) == 2:
        return terms[0] + terms[1]
    return (terms[0] + terms[2]) + (terms[1] + terms[3])


def combined(refs):
    third = refs[0].shape[0] // 3
    peaks = [ref[:third] for ref in refs]
    peak = functools.reduce(jnp.maximum, peaks)
    total = paired([ref[third : 2 * third] * jnp.exp(own - peak) for ref, own in zip(refs, peaks)])
    return peak, total, paired([ref[2 * third :] for ref in refs])


def merge_kernel(*refs):
    *ins, out_ref = refs
    third = out_ref.shape[0] // 3
    for j, value in enumerate(combined(ins)):
        out_ref[j * third : (j + 1) * third] = value


def final_kernel(*refs):
    *ins, policy_ref, logp_ref, kl_ref = refs
    half = policy_ref.shape[1] // 2
    peak, total, target = combined(ins)
    logp = target - peak - jnp.log(total)
    logp = jnp.concatenate([logp[:, :half], logp[:, 64 : 64 + half]], axis=1)
    logp_ref[...] = logp
    kl_ref[...] = 0.5 * (policy_ref[...] - logp) * (policy_ref[...] - logp)


def neighbours(stats, axis):
    return [stats] + [shift(stats, axis, k) for k in range(1, lax.axis_size(axis))]


def ring(block, axis):
    half = block.shape[0] // 2
    behind, ahead = shift(block, axis, 1), shift(block, axis, -1)
    return behind, shift(behind[:half], axis, 1), shift(ahead[half:], axis, -1), ahead


def like(*shape, dtype=BF):
    return jax.ShapeDtypeStruct(shape, dtype)


def vmem(mib):
    return pltpu.CompilerParams(vmem_limit_bytes=mib * 1024 * 1024)


def over_nodes(rows):
    nodes = lax.axis_size("x") * lax.axis_size("z")
    cut = rows.reshape(nodes, rows.shape[0] // nodes, rows.shape[1])
    return lax.all_to_all(cut, ("x", "z"), split_axis=0, concat_axis=0, tiled=True).reshape(rows.shape)


def shards(hidden, routes, route_weights, w_gate, w_up, w_down, gain, head, targets, policy_logp):
    tokens, width = hidden.shape
    second = width - FIRST
    y = lax.axis_index("y")
    core = lax.axis_index("core")
    n_node = lax.axis_size("x") * lax.axis_size("z")
    slots = n_node * SLOTS
    half = slots // 2
    model = 8 * width
    hid = w_gate.shape[2]
    hbm = pl.BlockSpec(memory_space=pl.ANY)
    in_vmem = pl.BlockSpec(memory_space=pltpu.VMEM)

    near_own = pl.pallas_call(
        near_kernel, out_shape=like(tokens + 16, second), compiler_params=vmem(VMEM), name="near"
    )(hidden, gain.reshape(1, width))
    near = [near_own]
    near = near + [shift(near[0], "y", k) for k in (1, 2, 3)]
    pick, mix_hi, mix_lo, send_a = pl.pallas_call(
        route_kernel,
        out_shape=(like(tokens, slots), like(tokens, slots), like(tokens, slots), like(slots, FIRST)),
        compiler_params=vmem(VMEM),
        name="route",
    )(routes, route_weights, hidden)
    a0 = over_nodes(send_a)
    send_b, inverse = pl.pallas_call(
        spread_kernel,
        out_shape=(like(slots, 4 * second), like(4, width, dtype=F32)),
        compiler_params=vmem(VMEM),
        name="spread",
    )(pick, *near)
    gate_mat, up_mat, down_mat = w_gate[0], w_up[0], w_down[0]
    gate_other, up_other, down_other = (shift(w, "core", 1) for w in (gate_mat, up_mat, down_mat))
    a0, send_b = lax.optimization_barrier((a0, send_b))
    a1, a3 = shift(a0, "y", 1), shift(a0, "y", -1)
    b = over_nodes(send_b)
    a2_top, a2_low = shift(a1[:half], "y", 1), shift(a3[half:], "y", -1)

    head_other = shift(head, "core", 1)
    inverse_other = shift(inverse, "core", 1)
    place = jnp.stack([y, core]).astype(jnp.int32)

    def rows_of(columns):
        return pl.BlockSpec((half, columns), lambda i, place: (i, 0))

    def whole(columns):
        return pl.BlockSpec((half, columns), lambda i, place: (0, 0))

    partial, partial_out = pl.pallas_call(
        up_kernel,
        grid_spec=pltpu.PrefetchScalarGridSpec(
            num_scalar_prefetch=1,
            grid=(2,),
            in_specs=[rows_of(FIRST), rows_of(FIRST), whole(FIRST), whole(FIRST), rows_of(FIRST)]
            + [rows_of(4 * second)]
            + [hbm] * 4,
            out_specs=[rows_of(4 * hid)] * 2,
            scratch_shapes=[pltpu.VMEM((4 * width, 4 * hid), BF), pltpu.SemaphoreType.DMA((4, 8))],
        ),
        out_shape=(like(slots, 4 * hid, dtype=F32), like(slots, 4 * hid)),
        compiler_params=vmem(VMEM),
        name="gate_up",
    )(place, a0, a1, a2_top, a2_low, a3, b, gate_mat, up_mat, gate_other, up_other)
    partial_got = shift(partial_out, "core", 1)

    a0, a1_top, a1_low, a2_top, a2_low, a3_top, a3_low, b = pl.pallas_call(
        down_kernel,
        grid_spec=pltpu.PrefetchScalarGridSpec(
            num_scalar_prefetch=1,
            grid=(2,),
            in_specs=[rows_of(4 * hid), rows_of(4 * hid), hbm, hbm],
            out_specs=[rows_of(FIRST)] + [whole(FIRST)] * 6 + [rows_of(4 * second)],
            scratch_shapes=[
                pltpu.VMEM((2 * hid, 4 * width), BF),
                pltpu.VMEM((half, 2 * hid), BF),
                pltpu.SemaphoreType.DMA((2, 8)),
            ],
        ),
        out_shape=(like(slots, FIRST),) + (like(half, FIRST),) * 6 + (like(slots, 4 * second),),
        compiler_params=vmem(58),
        name="down",
    )(place, partial, partial_got, down_mat, down_other)

    got1, got3 = shift(a2_top, "y", -1), shift(a2_low, "y", 1)
    left_low, right_top = shift(a1_low, "y", -1), shift(a3_top, "y", 1)
    back_b = over_nodes(b)
    a1_top, a3_low = pl.pallas_call(
        add_kernel, out_shape=(like(half, FIRST),) * 2, compiler_params=vmem(VMEM), name="add"
    )(a1_top, got1, a3_low, got3)
    left_top, right_low = shift(a1_top, "y", -1), shift(a3_low, "y", 1)
    summed = pl.pallas_call(
        ysum_kernel, out_shape=like(slots, FIRST), compiler_params=vmem(VMEM), name="ysum"
    )(a0, left_top, left_low, right_top, right_low)
    back_a = over_nodes(summed)
    own, *others = pl.pallas_call(
        mix_kernel,
        out_shape=(like(tokens, second, dtype=F32),) + (like(tokens, second),) * 3,
        compiler_params=vmem(VMEM),
        name="mix",
    )(mix_hi, mix_lo, back_b)
    arrived = [shift(part, "y", -k) for k, part in zip((1, 2, 3), others)]
    layer_out, scaled = pl.pallas_call(
        layer_kernel,
        out_shape=(like(tokens, width), like(tokens, width)),
        compiler_params=vmem(VMEM),
        name="layer",
    )(hidden, mix_hi, mix_lo, back_a, own, *arrived, gain.reshape(1, width))

    part = tokens // 2
    everyone = lax.all_gather(scaled[:part], AXES, axis=0, tiled=True)
    by_y = [scaled[part:]]
    by_y = by_y + [shift(by_y[0], "y", k) for k in (1, 2, 3)]
    part_a, part_b = jnp.stack(by_y[:2]), jnp.stack(by_y[2:])
    behind_a, far_a1, far_a2, ahead_a = ring(part_a, "x")
    behind_b, far_b1, far_b2, ahead_b = ring(part_b, "z")
    line_a = jnp.stack([part_a, behind_a, jnp.concatenate([far_a1, far_a2]), ahead_a])
    line_b = jnp.stack([part_b, behind_b, jnp.concatenate([far_b1, far_b2]), ahead_b])
    behind_a, far_a1, far_a2, ahead_a = ring(line_a, "z")
    behind_b, far_b1, far_b2, ahead_b = ring(line_b, "x")

    vocab_rows = head.shape[0]
    first_id = (lax.axis_index(AXES) * vocab_rows).reshape(1).astype(jnp.int32)
    x, z = lax.axis_index("x"), lax.axis_index("z")
    order = [((x - i) % 4) * 4 + (z - j) % 4 for i in range(4) for j in range(4)]
    wanted = targets.reshape(n_node, 2, part, 1)
    pieces = (line_a, behind_a, far_a1, far_a2, ahead_a, line_b, behind_b, far_b1, far_b2, ahead_b)
    rows = n_node * part
    own, other = pl.pallas_call(
        half_head_kernel,
        grid_spec=pltpu.PrefetchScalarGridSpec(
            num_scalar_prefetch=1,
            grid=(),
            in_specs=[in_vmem] + [hbm] * 2 + [in_vmem] * len(pieces),
            out_specs=[in_vmem] * 2,
            scratch_shapes=[
                pltpu.VMEM((2 * vocab_rows, 4 * width), BF),
                pltpu.VMEM((rows, 4 * width), BF),
                pltpu.SemaphoreType.DMA((2, 4)),
            ],
        ),
        out_shape=(like(rows, vocab_rows + 128, dtype=F32),) * 2,
        compiler_params=vmem(VMEM),
        cost_estimate=pl.CostEstimate(
            flops=16 * rows * width * vocab_rows, bytes_accessed=16 * width * vocab_rows, transcendentals=0
        ),
        name="half_head",
    )(place, inverse, head, head_other, *pieces)
    got = shift(other, "core", 1)
    everyone, own = lax.optimization_barrier((everyone, own))
    group = 8
    whole_stats = pl.pallas_call(
        functools.partial(whole_head_kernel, model),
        grid_spec=pltpu.PrefetchScalarGridSpec(
            num_scalar_prefetch=2,
            grid=(n_node // group,),
            in_specs=[
                pl.BlockSpec((group, 8, part, width), lambda n, s, t: (n, 0, 0, 0)),
                pl.BlockSpec((vocab_rows, model), lambda n, s, t: (0, 0)),
                pl.BlockSpec((4, width), lambda n, s, t: (0, 0)),
                pl.BlockSpec((4, width), lambda n, s, t: (0, 0)),
                pl.BlockSpec((group * part, 1), lambda n, s, t: (n, 0)),
            ],
            out_specs=pl.BlockSpec((8, group * part), lambda n, s, t: (0, n)),
        ),
        out_shape=like(8, rows, dtype=F32),
        compiler_params=vmem(VMEM),
        name="whole_head",
    )(
        first_id,
        place,
        everyone.reshape(n_node, 8, part, width),
        head,
        inverse,
        inverse_other,
        wanted[:, 0].reshape(rows, 1),
    )
    stats = pl.pallas_call(
        functools.partial(stats_kernel, model),
        grid_spec=pltpu.PrefetchScalarGridSpec(
            num_scalar_prefetch=2, grid=(), in_specs=[in_vmem] * 4, out_specs=in_vmem
        ),
        out_shape=like(3 * n_node, 128, dtype=F32),
        compiler_params=vmem(VMEM),
        name="stats",
    )(first_id, jnp.stack(order).astype(jnp.int32), own, got, wanted[:, 1], whole_stats)
    for axis in ("core", "y", "z"):
        stats = pl.pallas_call(
            merge_kernel, out_shape=like(3 * n_node, 128, dtype=F32), name="merge"
        )(*neighbours(stats, axis))
    ref_logp, kl = pl.pallas_call(
        final_kernel, out_shape=(like(n_node, tokens, dtype=F32),) * 2, name="final"
    )(*neighbours(stats, "x"), policy_logp.reshape(n_node, tokens))
    return layer_out, ref_logp.reshape(-1), kl.reshape(-1)


def solution(mesh):
    split = Mesh(mesh.devices.reshape(4, 4, 4, 2), AXES)
    node, local = ("x", "z"), ("y", "core")
    placed = (
        P(node, local),
        P(node, None),
        P(node, None),
        P(node, None, local),
        P(node, None, local),
        P(node, local, None),
        P(local),
        P(AXES, None),
        P(),
        P(),
    )
    return jax.shard_map(
        shards,
        mesh=split,
        in_specs=placed,
        out_specs=(P(node, local), P(), P()),
        check_vma=False,
    )
```

```python
import functools
import jax
import jax.numpy as jnp
from jax import lax
from jax.experimental import pallas as pl
from jax.experimental.pallas import tpu as pltpu
from jax.sharding import Mesh, PartitionSpec as P

BF = jnp.bfloat16
F32 = jnp.float32
AXES = ("x", "z", "y", "core")
SLOTS = 40
FIRST = 512
VMEM = 48


def shift(value, axis, step):
    size = lax.axis_size(axis)
    return lax.ppermute(value, axis, [(i, (i + step) % size) for i in range(size)])


def dot(a, b):
    return jnp.dot(a, b, preferred_element_type=F32)


def near_kernel(hidden_ref, gain_ref, near_ref):
    tokens, width = hidden_ref.shape
    second = near_ref.shape[1]
    near_ref[:tokens] = hidden_ref[:, FIRST:]
    gain = gain_ref[...]
    hi = gain.astype(BF).astype(F32)
    rows = jnp.zeros((near_ref.shape[0] - tokens, second), F32)
    row = lax.broadcasted_iota(jnp.int32, rows.shape, 0)
    for i, part in enumerate((hi, gain - hi)):
        for j, start in enumerate(range(0, width, second)):
            piece = part[:, start : start + second]
            piece = jnp.pad(piece, ((0, 0), (0, second - piece.shape[1])))
            rows = jnp.where(row == 4 * i + j, piece, rows)
    near_ref[tokens:] = rows.astype(BF)


def route_kernel(routes_ref, weights_ref, hidden_ref, pick_ref, hi_ref, lo_ref, send_ref):
    top, tokens = routes_ref.shape
    slots = pick_ref.shape[0]
    experts = slots // SLOTS
    ids = lax.broadcasted_iota(jnp.int32, (experts, tokens), 0)
    named = jnp.zeros((experts, tokens), F32)
    gates = jnp.zeros((experts, tokens), F32)
    for k in range(top):
        hit = routes_ref[k : k + 1, :] == ids
        named = named + jnp.where(hit, 1.0, 0.0)
        gates = gates + jnp.where(hit, weights_ref[k : k + 1, :], 0.0)
    row = lax.broadcasted_iota(jnp.int32, (tokens, tokens), 0)
    col = lax.broadcasted_iota(jnp.int32, (tokens, tokens), 1)
    count = dot(named.astype(BF), jnp.where(row < col, 1.0, 0.0).astype(BF))
    slot = lax.broadcasted_iota(jnp.int32, (slots, experts), 0)
    expert = lax.broadcasted_iota(jnp.int32, (slots, experts), 1)
    inside = (slot >= expert * SLOTS) & (slot < expert * SLOTS + SLOTS)
    spread = jnp.where(inside, 1.0, 0.0).astype(BF)
    at = jnp.sum(jnp.where(inside, slot - expert * SLOTS, 0).astype(F32), axis=1, keepdims=True)
    gates_hi = gates.astype(BF)
    gates_lo = (gates - gates_hi.astype(F32)).astype(BF)
    placed = (dot(spread, named.astype(BF)) > 0.5) & (dot(spread, count.astype(BF)) == at)
    hi_ref[...] = jnp.where(placed, dot(spread, gates_hi), 0.0).astype(BF)
    lo_ref[...] = jnp.where(placed, dot(spread, gates_lo), 0.0).astype(BF)
    pick = jnp.where(placed, 1.0, 0.0).astype(BF)
    pick_ref[...] = pick
    send_ref[...] = dot(pick, hidden_ref[:, :FIRST]).astype(BF)


def spread_kernel(pick_ref, h0, h1, h2, h3, send_ref, inverse_ref):
    tokens = pick_ref.shape[1]
    second = h0.shape[1]
    width = inverse_ref.shape[1]
    for k, ref in enumerate((h0, h1, h2, h3)):
        send_ref[:, k * second : (k + 1) * second] = dot(pick_ref[...], ref[:tokens]).astype(BF)
        rows = ref[tokens:].astype(F32)
        for j, start in enumerate(range(0, width, second)):
            size = min(second, width - start)
            gain = rows[j : j + 1, :size] + rows[4 + j : 5 + j, :size]
            inverse_ref[k : k + 1, start : start + size] = 1.0 / (gain * gain)


def mixed(hi_ref, lo_ref, rows):
    across = (((0,), (0,)), ((), ()))
    hi = lax.dot_general(hi_ref[...], rows, across, preferred_element_type=F32)
    return hi + lax.dot_general(lo_ref[...], rows, across, preferred_element_type=F32)


def block_of(place_ref, k):
    return 2 * lax.rem(place_ref[0] + 4 - k, 4) + place_ref[1]


def up_copies(place_ref, sources, w_ref, sems, places, offset, size, base):
    hidden = sources[0].shape[1]
    width = sources[0].shape[0] // 8
    made = []
    for j, w in enumerate(sources):
        for i, k in enumerate(places):
            start = pl.multiple_of(block_of(place_ref, k) * width + offset, 128)
            made.append(
                pltpu.make_async_copy(
                    w.at[pl.ds(start, size), :],
                    w_ref.at[pl.ds(base + i * size, size), pl.ds(j * hidden, hidden)],
                    sems.at[j, i],
                )
            )
    return made


def up_first_kernel(place_ref, a0, a1, a3, w0, w1, w2, w3, sum_ref, w_ref, sems):
    hidden = w0.shape[1]

    @pl.when(pl.program_id(0) == 0)
    def _():
        copies = up_copies(place_ref, (w0, w1, w2, w3), w_ref, sems, (0, 1, 3), 0, FIRST, 0)
        for copy in copies:
            copy.start()
        for copy in copies:
            copy.wait()

    @pl.loop(0, 4)
    def _(j):
        cols = pl.ds(pl.multiple_of(j * hidden, hidden), hidden)
        part = dot(a0[...], w_ref[:FIRST, cols])
        for k, ref in ((1, a1), (2, a3)):
            part = part + dot(ref[...], w_ref[k * FIRST : (k + 1) * FIRST, cols])
        sum_ref[:, cols] = part


def up_second_kernel(
    place_ref, before_ref, b_ref, a2_top, a2_low, w0, w1, w2, w3, sum_ref, out_ref, w_ref, sems
):
    step = pl.program_id(0)
    hidden = w0.shape[1]
    second = w0.shape[0] // 8 - FIRST

    @pl.when(step == 0)
    def _():
        sources = (w0, w1, w2, w3)
        copies = up_copies(place_ref, sources, w_ref, sems.at[0], (2,), 0, FIRST, 0)
        copies = copies + up_copies(
            place_ref, sources, w_ref, sems.at[1], (0, 1, 2, 3), FIRST, second, FIRST
        )
        for copy in copies:
            copy.start()
        for copy in copies:
            copy.wait()

    def total(a2):
        @pl.loop(0, 4)
        def _(j):
            cols = pl.ds(pl.multiple_of(j * hidden, hidden), hidden)
            part = dot(b_ref[...], w_ref[FIRST:, cols]) + dot(a2[...], w_ref[:FIRST, cols])
            part = part + before_ref[:, cols]
            sum_ref[:, cols] = part
            out_ref[:, cols] = part.astype(BF)

    @pl.when(step == 0)
    def _():
        total(a2_top)

    @pl.when(step == 1)
    def _():
        total(a2_low)


def down_kernel(
    place_ref, sum_ref, got_ref, w0, w1, a0, a1_top, a1_low, a2_top, a2_low, a3_top, a3_low, b_ref,
    w_ref, act_ref, sems
):
    step = pl.program_id(0)
    hidden = w0.shape[0]
    width = w0.shape[1] // 8
    second = width - FIRST

    def copies():
        made = []
        for j, w in enumerate((w0, w1)):
            rows = pl.ds(j * hidden, hidden)
            for k in range(4):
                start = pl.multiple_of(block_of(place_ref, k) * width, 128)
                made.append(
                    pltpu.make_async_copy(
                        w.at[:, pl.ds(start, FIRST)],
                        w_ref.at[rows, pl.ds(k * FIRST, FIRST)],
                        sems.at[j, 2 * k],
                    )
                )
                made.append(
                    pltpu.make_async_copy(
                        w.at[:, pl.ds(start + FIRST, second)],
                        w_ref.at[rows, pl.ds(4 * FIRST + k * second, second)],
                        sems.at[j, 2 * k + 1],
                    )
                )
        return made

    @pl.when(step == 0)
    def _():
        for copy in copies():
            copy.start()

    for j in range(2):
        own, got = 2 * j * hidden, 2 * (1 - j) * hidden
        gate = sum_ref[:, own : own + hidden] + got_ref[:, got : got + hidden].astype(F32)
        up = sum_ref[:, own + hidden : own + 2 * hidden] + got_ref[
            :, got + hidden : got + 2 * hidden
        ].astype(F32)
        act_ref[:, j * hidden : (j + 1) * hidden] = (gate / (1.0 + jnp.exp(-gate)) * up).astype(BF)

    @pl.when(step == 0)
    def _():
        for copy in copies():
            copy.wait()

    def out(start, size):
        return dot(act_ref[...], w_ref[:, start : start + size]).astype(BF)

    a0[...] = out(0, FIRST)
    b_ref[...] = out(4 * FIRST, 4 * second)

    @pl.when(step == 0)
    def _():
        for k, ref in ((1, a1_top), (2, a2_top), (3, a3_top)):
            ref[...] = out(k * FIRST, FIRST)

    @pl.when(step == 1)
    def _():
        for k, ref in ((1, a1_low), (2, a2_low), (3, a3_low)):
            ref[...] = out(k * FIRST, FIRST)


def add_kernel(a1, got1, a3, got3, out1, out3):
    out1[...] = (a1[...].astype(F32) + got1[...].astype(F32)).astype(BF)
    out3[...] = (a3[...].astype(F32) + got3[...].astype(F32)).astype(BF)


def ysum_kernel(a0, left_top, left_low, right_top, right_low, out_ref):
    half = left_top.shape[0]
    top = a0[:half].astype(F32) + left_top[...].astype(F32) + right_top[...].astype(F32)
    low = a0[half:].astype(F32) + left_low[...].astype(F32) + right_low[...].astype(F32)
    out_ref[:half] = top.astype(BF)
    out_ref[half:] = low.astype(BF)


def mix_kernel(hi_ref, lo_ref, back_ref, own_ref, p1, p2, p3):
    width = own_ref.shape[1]
    for k, ref in enumerate((own_ref, p1, p2, p3)):
        ref[...] = mixed(hi_ref, lo_ref, back_ref[:, k * width : (k + 1) * width]).astype(ref.dtype)


def layer_kernel(hidden_ref, hi_ref, lo_ref, back_ref, own_ref, p1, p2, p3, gain_ref, out_ref, scaled_ref):
    first = mixed(hi_ref, lo_ref, back_ref[...])
    second = own_ref[...] + p1[...].astype(F32) + p2[...].astype(F32) + p3[...].astype(F32)
    for mix, cols in ((first, slice(0, FIRST)), (second, slice(FIRST, hidden_ref.shape[1]))):
        total = hidden_ref[:, cols].astype(F32) + mix
        out_ref[:, cols] = total.astype(BF)
        scaled_ref[:, cols] = (total * gain_ref[:, cols]).astype(BF)


def squares_of(rows, inverse):
    total = jnp.zeros((rows.shape[0], 128), F32)
    for c in range(0, rows.shape[1], 128):
        value = rows[:, c : c + 128].astype(F32)
        total = total + value * value * inverse[:, c : c + 128]
    return total


def half_head_kernel(place_ref, inverse_ref, w0, w1, *refs):
    *pieces, own_ref, other_ref, w_ref, rows_ref, sems = refs
    vocab = w0.shape[0]
    tokens, width = pieces[0].shape[2:]
    line_a, behind_a, far_a1, far_a2, ahead_a = pieces[:5]
    line_b, behind_b, far_b1, far_b2, ahead_b = pieces[5:]

    copies = []
    for j, w in enumerate((w0, w1)):
        for k in range(4):
            start = pl.multiple_of(block_of(place_ref, k) * width, 128)
            copies.append(
                pltpu.make_async_copy(
                    w.at[:, pl.ds(start, width)],
                    w_ref.at[pl.ds(j * vocab, vocab), pl.ds(k * width, width)],
                    sems.at[j, k],
                )
            )
    for copy in copies:
        copy.start()

    own_ref[:, vocab:] = jnp.zeros_like(own_ref[:, vocab:])

    def take(ref, place_of, base):
        @pl.loop(0, ref.shape[0])
        def _(i):
            at = pl.ds(pl.multiple_of(place_of(i) * tokens, tokens), tokens)
            squares = own_ref[at, vocab:]
            for k in range(2):
                rows = ref[i, k]
                first = (base + k) * width
                rows_ref[at, first : first + width] = rows
                squares = squares + squares_of(rows, inverse_ref[base + k : base + k + 1])
            own_ref[at, vocab:] = squares

    for back, ref, skip in (
        (0, line_a, 0), (1, behind_a, 0), (2, far_a1, 0), (2, far_a2, 2), (3, ahead_a, 0)
    ):
        take(ref, lambda i, back=back, skip=skip: (i + skip) * 4 + back, 0)
    for back, ref, skip in (
        (0, line_b, 0), (1, behind_b, 0), (2, far_b1, 0), (2, far_b2, 2), (3, ahead_b, 0)
    ):
        take(ref, lambda i, back=back, skip=skip: back * 4 + i + skip, 2)
    other_ref[:, vocab:] = own_ref[:, vocab:]
    for copy in copies:
        copy.wait()

    @pl.loop(0, rows_ref.shape[0] // 384)
    def _(i):
        at = pl.ds(pl.multiple_of(i * 384, 384), 384)

        @pl.loop(0, vocab // 256)
        def _(n):
            cols = pl.ds(pl.multiple_of(n * 256, 256), 256)
            for j, ref in ((1, other_ref), (0, own_ref)):
                ref[at, cols] = lax.dot_general(
                    rows_ref[at],
                    w_ref[pl.ds(pl.multiple_of(j * vocab + n * 256, 256), 256), :],
                    (((1,), (1,)), ((), ())),
                    preferred_element_type=F32,
                )


def columns_of(full, ids, wanted):
    peak = jnp.max(full, axis=1, keepdims=True)
    total = jnp.sum(jnp.exp(full - peak), axis=1, keepdims=True)
    target = jnp.sum(jnp.where(ids == wanted, full, 0.0), axis=1, keepdims=True)
    lane = lax.broadcasted_iota(jnp.int32, (full.shape[0], 128), 1)
    return jnp.where(lane == 0, peak, jnp.where(lane == 1, total, target)).T


def whole_head_kernel(model, first_ref, place_ref, rows_ref, head_ref, own_ref, other_ref, wanted_ref, stats_ref, all_ref):
    nodes, parts, tokens, width = rows_ref.shape
    squares = 0.0
    for p in range(parts):
        rows = rows_ref[:, p].reshape(nodes * tokens, width)
        all_ref[:, p * width : (p + 1) * width] = rows
        k = lax.rem(place_ref[0] + 4 - p // 2, 4)
        mine = place_ref[1] == p % 2
        inverse = jnp.where(mine, own_ref[pl.ds(k, 1), :], other_ref[pl.ds(k, 1), :])
        squares = squares + squares_of(rows, inverse)
    logits = lax.dot_general(
        all_ref[...], head_ref[...], (((1,), (1,)), ((), ())), preferred_element_type=F32
    )
    scale = lax.rsqrt(jnp.sum(squares, axis=1, keepdims=True) / model + 1e-06)
    ids = first_ref[0] + lax.broadcasted_iota(jnp.int32, logits.shape, 1)
    columns = columns_of(logits * scale, ids, wanted_ref[...])
    stats_ref[...] = columns[:8]


def stats_kernel(model, first_ref, order_ref, own_ref, got_ref, wanted_ref, whole_ref, stats_ref):
    vocab = own_ref.shape[1] - 128
    nodes, tokens, _ = wanted_ref.shape
    wanted = jnp.concatenate([wanted_ref[order_ref[i]] for i in range(nodes)], axis=0)
    squares = jnp.sum(own_ref[:, vocab:] + got_ref[:, vocab:], axis=1, keepdims=True)
    scale = lax.rsqrt(squares / model + 1e-06)
    full = (own_ref[:, :vocab] + got_ref[:, :vocab]) * scale
    ids = first_ref[0] + lax.broadcasted_iota(jnp.int32, full.shape, 1)
    columns = columns_of(full, ids, wanted)
    stats_ref[...] = jnp.zeros_like(stats_ref)
    for i in range(nodes):
        lanes = slice(i * tokens, (i + 1) * tokens)
        for j in range(3):
            stats_ref[j * nodes + i : j * nodes + i + 1, :tokens] = whole_ref[j : j + 1, lanes]
            row = j * nodes + order_ref[i]
            stats_ref[pl.ds(row, 1), 64 : 64 + tokens] = columns[j : j + 1, lanes]


def paired(terms):
    if len(terms) == 2:
        return terms[0] + terms[1]
    return (terms[0] + terms[2]) + (terms[1] + terms[3])


def combined(refs):
    third = refs[0].shape[0] // 3
    peaks = [ref[:third] for ref in refs]
    peak = functools.reduce(jnp.maximum, peaks)
    total = paired([ref[third : 2 * third] * jnp.exp(own - peak) for ref, own in zip(refs, peaks)])
    return peak, total, paired([ref[2 * third :] for ref in refs])


def merge_kernel(*refs):
    *ins, out_ref = refs
    third = out_ref.shape[0] // 3
    for j, value in enumerate(combined(ins)):
        out_ref[j * third : (j + 1) * third] = value


def final_kernel(*refs):
    *ins, policy_ref, logp_ref, kl_ref = refs
    peak, total, target = combined(ins)
    spaced = target - peak - jnp.log(total)
    half = policy_ref.shape[0] * 128 // (2 * spaced.shape[0])
    tokens = 2 * half
    packed = jnp.concatenate([spaced[:, :half], spaced[:, 64 : 64 + half]], axis=1)
    lines = []
    for at in range(0, spaced.shape[0] * tokens, 128):
        node, lane = at // tokens, at % tokens
        pieces = [packed[node : node + 1, lane:]]
        pieces.append(packed[node + 1 : node + 2, : 128 - (tokens - lane)])
        lines.append(jnp.concatenate(pieces, axis=1))
    logp = jnp.concatenate(lines, axis=0)
    logp_ref[...] = logp
    kl_ref[...] = 0.5 * (policy_ref[...] - logp) * (policy_ref[...] - logp)


def neighbours(stats, axis):
    return [stats] + [shift(stats, axis, k) for k in range(1, lax.axis_size(axis))]


def ring(block, axis):
    half = block.shape[0] // 2
    behind, ahead = shift(block, axis, 1), shift(block, axis, -1)
    return behind, shift(behind[:half], axis, 1), shift(ahead[half:], axis, -1), ahead


def like(*shape, dtype=BF):
    return jax.ShapeDtypeStruct(shape, dtype)


def vmem(mib):
    return pltpu.CompilerParams(vmem_limit_bytes=mib * 1024 * 1024)


def over_nodes(rows):
    nodes = lax.axis_size("x") * lax.axis_size("z")
    cut = rows.reshape(nodes, rows.shape[0] // nodes, rows.shape[1])
    return lax.all_to_all(cut, ("x", "z"), split_axis=0, concat_axis=0, tiled=True).reshape(rows.shape)


def shards(hidden, routes, route_weights, w_gate, w_up, w_down, gain, head, targets, policy_logp):
    tokens, width = hidden.shape
    second = width - FIRST
    y = lax.axis_index("y")
    core = lax.axis_index("core")
    n_node = lax.axis_size("x") * lax.axis_size("z")
    slots = n_node * SLOTS
    half = slots // 2
    model = 8 * width
    hid = w_gate.shape[2]
    hbm = pl.BlockSpec(memory_space=pl.ANY)
    in_vmem = pl.BlockSpec(memory_space=pltpu.VMEM)

    near_own = pl.pallas_call(
        near_kernel, out_shape=like(tokens + 16, second), compiler_params=vmem(VMEM), name="near"
    )(hidden, gain.reshape(1, width))
    near = [near_own]
    near = near + [shift(near[0], "y", k) for k in (1, 2, 3)]
    pick, mix_hi, mix_lo, send_a = pl.pallas_call(
        route_kernel,
        out_shape=(like(slots, tokens),) * 3 + (like(slots, FIRST),),
        compiler_params=vmem(VMEM),
        name="route",
    )(routes.T, route_weights.T, hidden)
    a0 = over_nodes(send_a)
    send_b, inverse = pl.pallas_call(
        spread_kernel,
        out_shape=(like(slots, 4 * second), like(4, width, dtype=F32)),
        compiler_params=vmem(VMEM),
        name="spread",
    )(pick, *near)
    gate_mat, up_mat, down_mat = w_gate[0], w_up[0], w_down[0]
    gate_other, up_other, down_other = (shift(w, "core", 1) for w in (gate_mat, up_mat, down_mat))
    a0, send_b = lax.optimization_barrier((a0, send_b))
    a1, a3 = shift(a0, "y", 1), shift(a0, "y", -1)
    b = over_nodes(send_b)
    a2_top, a2_low = shift(a1[:half], "y", 1), shift(a3[half:], "y", -1)

    head_other = shift(head, "core", 1)
    inverse_other = shift(inverse, "core", 1)
    place = jnp.stack([y, core]).astype(jnp.int32)

    def rows_of(columns):
        return pl.BlockSpec((half, columns), lambda i, place: (i, 0))

    def whole(columns):
        return pl.BlockSpec((half, columns), lambda i, place: (0, 0))

    partial = pl.pallas_call(
        up_first_kernel,
        grid_spec=pltpu.PrefetchScalarGridSpec(
            num_scalar_prefetch=1,
            grid=(2,),
            in_specs=[rows_of(FIRST)] * 3 + [hbm] * 4,
            out_specs=rows_of(4 * hid),
            scratch_shapes=[pltpu.VMEM((3 * FIRST, 4 * hid), BF), pltpu.SemaphoreType.DMA((4, 3))],
        ),
        out_shape=like(slots, 4 * hid, dtype=F32),
        compiler_params=vmem(VMEM),
        cost_estimate=pl.CostEstimate(
            flops=24 * slots * FIRST * hid, bytes_accessed=24 * FIRST * hid, transcendentals=0
        ),
        name="up_first",
    )(place, a0, a1, a3, gate_mat, up_mat, gate_other, up_other)
    partial, partial_out = pl.pallas_call(
        up_second_kernel,
        grid_spec=pltpu.PrefetchScalarGridSpec(
            num_scalar_prefetch=1,
            grid=(2,),
            in_specs=[rows_of(4 * hid), rows_of(4 * second), whole(FIRST), whole(FIRST)] + [hbm] * 4,
            out_specs=[rows_of(4 * hid)] * 2,
            scratch_shapes=[
                pltpu.VMEM((FIRST + 4 * second, 4 * hid), BF),
                pltpu.SemaphoreType.DMA((2, 4, 4)),
            ],
        ),
        out_shape=(like(slots, 4 * hid, dtype=F32), like(slots, 4 * hid)),
        compiler_params=vmem(VMEM),
        name="up_second",
    )(place, partial, b, a2_top, a2_low, gate_mat, up_mat, gate_other, up_other)
    partial_got = shift(partial_out, "core", 1)

    a0, a1_top, a1_low, a2_top, a2_low, a3_top, a3_low, b = pl.pallas_call(
        down_kernel,
        grid_spec=pltpu.PrefetchScalarGridSpec(
            num_scalar_prefetch=1,
            grid=(2,),
            in_specs=[rows_of(4 * hid), rows_of(4 * hid), hbm, hbm],
            out_specs=[rows_of(FIRST)] + [whole(FIRST)] * 6 + [rows_of(4 * second)],
            scratch_shapes=[
                pltpu.VMEM((2 * hid, 4 * width), BF),
                pltpu.VMEM((half, 2 * hid), BF),
                pltpu.SemaphoreType.DMA((2, 8)),
            ],
        ),
        out_shape=(like(slots, FIRST),) + (like(half, FIRST),) * 6 + (like(slots, 4 * second),),
        compiler_params=vmem(58),
        name="down",
    )(place, partial, partial_got, down_mat, down_other)

    got1, got3 = shift(a2_top, "y", -1), shift(a2_low, "y", 1)
    left_low, right_top = shift(a1_low, "y", -1), shift(a3_top, "y", 1)
    back_b = over_nodes(b)
    a1_top, a3_low = pl.pallas_call(
        add_kernel, out_shape=(like(half, FIRST),) * 2, compiler_params=vmem(VMEM), name="add"
    )(a1_top, got1, a3_low, got3)
    left_top, right_low = shift(a1_top, "y", -1), shift(a3_low, "y", 1)
    summed = pl.pallas_call(
        ysum_kernel, out_shape=like(slots, FIRST), compiler_params=vmem(VMEM), name="ysum"
    )(a0, left_top, left_low, right_top, right_low)
    back_a = over_nodes(summed)
    own, *others = pl.pallas_call(
        mix_kernel,
        out_shape=(like(tokens, second, dtype=F32),) + (like(tokens, second),) * 3,
        compiler_params=vmem(VMEM),
        name="mix",
    )(mix_hi, mix_lo, back_b)
    arrived = [shift(part, "y", -k) for k, part in zip((1, 2, 3), others)]
    layer_out, scaled = pl.pallas_call(
        layer_kernel,
        out_shape=(like(tokens, width), like(tokens, width)),
        compiler_params=vmem(VMEM),
        name="layer",
    )(hidden, mix_hi, mix_lo, back_a, own, *arrived, gain.reshape(1, width))

    part = tokens // 2
    everyone = lax.all_gather(scaled[:part], AXES, axis=0, tiled=True)
    by_y = [scaled[part:]]
    by_y = by_y + [shift(by_y[0], "y", k) for k in (1, 2, 3)]
    part_a, part_b = jnp.stack(by_y[:2]), jnp.stack(by_y[2:])
    behind_a, far_a1, far_a2, ahead_a = ring(part_a, "x")
    behind_b, far_b1, far_b2, ahead_b = ring(part_b, "z")
    line_a = jnp.stack([part_a, behind_a, jnp.concatenate([far_a1, far_a2]), ahead_a])
    line_b = jnp.stack([part_b, behind_b, jnp.concatenate([far_b1, far_b2]), ahead_b])
    behind_a, far_a1, far_a2, ahead_a = ring(line_a, "z")
    behind_b, far_b1, far_b2, ahead_b = ring(line_b, "x")

    vocab_rows = head.shape[0]
    first_id = (lax.axis_index(AXES) * vocab_rows).reshape(1).astype(jnp.int32)
    x, z = lax.axis_index("x"), lax.axis_index("z")
    order = [((x - i) % 4) * 4 + (z - j) % 4 for i in range(4) for j in range(4)]
    wanted = targets.reshape(n_node, 2, part, 1)
    pieces = (line_a, behind_a, far_a1, far_a2, ahead_a, line_b, behind_b, far_b1, far_b2, ahead_b)
    rows = n_node * part
    own, other = pl.pallas_call(
        half_head_kernel,
        grid_spec=pltpu.PrefetchScalarGridSpec(
            num_scalar_prefetch=1,
            grid=(),
            in_specs=[in_vmem] + [hbm] * 2 + [in_vmem] * len(pieces),
            out_specs=[in_vmem] * 2,
            scratch_shapes=[
                pltpu.VMEM((2 * vocab_rows, 4 * width), BF),
                pltpu.VMEM((rows, 4 * width), BF),
                pltpu.SemaphoreType.DMA((2, 4)),
            ],
        ),
        out_shape=(like(rows, vocab_rows + 128, dtype=F32),) * 2,
        compiler_params=vmem(VMEM),
        cost_estimate=pl.CostEstimate(
            flops=16 * rows * width * vocab_rows, bytes_accessed=16 * width * vocab_rows, transcendentals=0
        ),
        name="half_head",
    )(place, inverse, head, head_other, *pieces)
    got = shift(other, "core", 1)
    everyone, own = lax.optimization_barrier((everyone, own))
    group = 8
    whole_stats = pl.pallas_call(
        functools.partial(whole_head_kernel, model),
        grid_spec=pltpu.PrefetchScalarGridSpec(
            num_scalar_prefetch=2,
            grid=(n_node // group,),
            in_specs=[
                pl.BlockSpec((group, 8, part, width), lambda n, s, t: (n, 0, 0, 0)),
                pl.BlockSpec((vocab_rows, model), lambda n, s, t: (0, 0)),
                pl.BlockSpec((4, width), lambda n, s, t: (0, 0)),
                pl.BlockSpec((4, width), lambda n, s, t: (0, 0)),
                pl.BlockSpec((group * part, 1), lambda n, s, t: (n, 0)),
            ],
            out_specs=pl.BlockSpec((8, group * part), lambda n, s, t: (0, n)),
            scratch_shapes=[pltpu.VMEM((group * part, model), BF)],
        ),
        out_shape=like(8, rows, dtype=F32),
        compiler_params=vmem(VMEM),
        name="whole_head",
    )(
        first_id,
        place,
        everyone.reshape(n_node, 8, part, width),
        head,
        inverse,
        inverse_other,
        wanted[:, 0].reshape(rows, 1),
    )
    stats = pl.pallas_call(
        functools.partial(stats_kernel, model),
        grid_spec=pltpu.PrefetchScalarGridSpec(
            num_scalar_prefetch=2, grid=(), in_specs=[in_vmem] * 4, out_specs=in_vmem
        ),
        out_shape=like(3 * n_node, 128, dtype=F32),
        compiler_params=vmem(VMEM),
        name="stats",
    )(first_id, jnp.stack(order).astype(jnp.int32), own, got, wanted[:, 1], whole_stats)
    for axis in ("core", "y", "z"):
        stats = pl.pallas_call(
            merge_kernel, out_shape=like(3 * n_node, 128, dtype=F32), name="merge"
        )(*neighbours(stats, axis))
    ref_logp, kl = pl.pallas_call(
        final_kernel, out_shape=(like(n_node * tokens // 128, 128, dtype=F32),) * 2, name="final"
    )(*neighbours(stats, "x"), policy_logp.reshape(-1, 128))
    return layer_out, ref_logp.reshape(-1), kl.reshape(-1)


def solution(mesh):
    split = Mesh(mesh.devices.reshape(4, 4, 4, 2), AXES)
    node, local = ("x", "z"), ("y", "core")
    placed = (
        P(node, local),
        P(node, None),
        P(node, None),
        P(node, None, local),
        P(node, None, local),
        P(node, local, None),
        P(local),
        P(AXES, None),
        P(),
        P(),
    )
    return jax.shard_map(
        shards,
        mesh=split,
        in_specs=placed,
        out_specs=(P(node, local), P(), P()),
        check_vma=False,
    )
```

```python
import functools
import jax
import jax.numpy as jnp
from jax import lax
from jax.experimental import pallas as pl
from jax.experimental.pallas import tpu as pltpu
from jax.sharding import Mesh, PartitionSpec as P

BF = jnp.bfloat16
F32 = jnp.float32
AXES = ("x", "z", "y", "core")
SLOTS = 40
FIRST = 512
VMEM = 48


def shift(value, axis, step):
    size = lax.axis_size(axis)
    return lax.ppermute(value, axis, [(i, (i + step) % size) for i in range(size)])


def dot(a, b):
    return jnp.dot(a, b, preferred_element_type=F32)


def near_kernel(hidden_ref, gain_ref, near_ref):
    tokens, width = hidden_ref.shape
    second = near_ref.shape[1]
    near_ref[:tokens] = hidden_ref[:, FIRST:]
    gain = gain_ref[...]
    hi = gain.astype(BF).astype(F32)
    rows = jnp.zeros((near_ref.shape[0] - tokens, second), F32)
    row = lax.broadcasted_iota(jnp.int32, rows.shape, 0)
    for i, part in enumerate((hi, gain - hi)):
        for j, start in enumerate(range(0, width, second)):
            piece = part[:, start : start + second]
            piece = jnp.pad(piece, ((0, 0), (0, second - piece.shape[1])))
            rows = jnp.where(row == 4 * i + j, piece, rows)
    near_ref[tokens:] = rows.astype(BF)


def route_kernel(routes_ref, weights_ref, hidden_ref, pick_ref, hi_ref, lo_ref, send_ref):
    top, tokens = routes_ref.shape
    slots = pick_ref.shape[0]
    experts = slots // SLOTS
    ids = lax.broadcasted_iota(jnp.int32, (experts, tokens), 0)
    named = jnp.zeros((experts, tokens), F32)
    gates = jnp.zeros((experts, tokens), F32)
    for k in range(top):
        hit = routes_ref[k : k + 1, :] == ids
        named = named + jnp.where(hit, 1.0, 0.0)
        gates = gates + jnp.where(hit, weights_ref[k : k + 1, :], 0.0)
    row = lax.broadcasted_iota(jnp.int32, (tokens, tokens), 0)
    col = lax.broadcasted_iota(jnp.int32, (tokens, tokens), 1)
    count = dot(named.astype(BF), jnp.where(row < col, 1.0, 0.0).astype(BF))
    slot = lax.broadcasted_iota(jnp.int32, (slots, experts), 0)
    expert = lax.broadcasted_iota(jnp.int32, (slots, experts), 1)
    inside = (slot >= expert * SLOTS) & (slot < expert * SLOTS + SLOTS)
    spread = jnp.where(inside, 1.0, 0.0).astype(BF)
    at = jnp.sum(jnp.where(inside, slot - expert * SLOTS, 0).astype(F32), axis=1, keepdims=True)
    gates_hi = gates.astype(BF)
    gates_lo = (gates - gates_hi.astype(F32)).astype(BF)
    placed = (dot(spread, named.astype(BF)) > 0.5) & (dot(spread, count.astype(BF)) == at)
    hi_ref[...] = jnp.where(placed, dot(spread, gates_hi), 0.0).astype(BF)
    lo_ref[...] = jnp.where(placed, dot(spread, gates_lo), 0.0).astype(BF)
    pick = jnp.where(placed, 1.0, 0.0).astype(BF)
    pick_ref[...] = pick
    send_ref[...] = dot(pick, hidden_ref[:, :FIRST]).astype(BF)


def spread_kernel(pick_ref, h0, h1, h2, h3, send_ref, inverse_ref):
    tokens = pick_ref.shape[1]
    second = h0.shape[1]
    width = inverse_ref.shape[1]
    for k, ref in enumerate((h0, h1, h2, h3)):
        send_ref[:, k * second : (k + 1) * second] = dot(pick_ref[...], ref[:tokens]).astype(BF)
        rows = ref[tokens:].astype(F32)
        for j, start in enumerate(range(0, width, second)):
            size = min(second, width - start)
            gain = rows[j : j + 1, :size] + rows[4 + j : 5 + j, :size]
            inverse_ref[k : k + 1, start : start + size] = 1.0 / (gain * gain)


def mixed(hi_ref, lo_ref, rows):
    across = (((0,), (0,)), ((), ()))
    hi = lax.dot_general(hi_ref[...], rows, across, preferred_element_type=F32)
    return hi + lax.dot_general(lo_ref[...], rows, across, preferred_element_type=F32)


def block_of(place_ref, k):
    return 2 * lax.rem(place_ref[0] + 4 - k, 4) + place_ref[1]


def up_copies(place_ref, sources, w_ref, sems, places, offset, size, base):
    hidden = sources[0].shape[1]
    width = sources[0].shape[0] // 8
    made = []
    for j, w in enumerate(sources):
        for i, k in enumerate(places):
            start = pl.multiple_of(block_of(place_ref, k) * width + offset, 128)
            made.append(
                pltpu.make_async_copy(
                    w.at[pl.ds(start, size), :],
                    w_ref.at[pl.ds(base + i * size, size), pl.ds(j * hidden, hidden)],
                    sems.at[j, i],
                )
            )
    return made


def up_first_kernel(place_ref, a0, a1, a3, w0, w1, w2, w3, sum_ref, w_ref, sems):
    hidden = w0.shape[1]

    @pl.when(pl.program_id(0) == 0)
    def _():
        copies = up_copies(place_ref, (w0, w1, w2, w3), w_ref, sems, (0, 1, 3), 0, FIRST, 0)
        for copy in copies:
            copy.start()
        for copy in copies:
            copy.wait()

    @pl.loop(0, 4)
    def _(j):
        cols = pl.ds(pl.multiple_of(j * hidden, hidden), hidden)
        part = dot(a0[...], w_ref[:FIRST, cols])
        for k, ref in ((1, a1), (2, a3)):
            part = part + dot(ref[...], w_ref[k * FIRST : (k + 1) * FIRST, cols])
        sum_ref[:, cols] = part


def up_second_kernel(
    place_ref, before_ref, b_ref, a2_top, a2_low, w0, w1, w2, w3, sum_ref, out_ref, w_ref, sems
):
    step = pl.program_id(0)
    hidden = w0.shape[1]
    second = w0.shape[0] // 8 - FIRST

    @pl.when(step == 0)
    def _():
        sources = (w0, w1, w2, w3)
        copies = up_copies(place_ref, sources, w_ref, sems.at[0], (2,), 0, FIRST, 0)
        copies = copies + up_copies(
            place_ref, sources, w_ref, sems.at[1], (0, 1, 2, 3), FIRST, second, FIRST
        )
        for copy in copies:
            copy.start()
        for copy in copies:
            copy.wait()

    def total(a2):
        @pl.loop(0, 4)
        def _(j):
            cols = pl.ds(pl.multiple_of(j * hidden, hidden), hidden)
            part = dot(b_ref[...], w_ref[FIRST:, cols]) + dot(a2[...], w_ref[:FIRST, cols])
            part = part + before_ref[:, cols]
            sum_ref[:, cols] = part
            out_ref[:, cols] = part.astype(BF)

    @pl.when(step == 0)
    def _():
        total(a2_top)

    @pl.when(step == 1)
    def _():
        total(a2_low)


def down_kernel(
    place_ref, sum_ref, got_ref, w0, w1, a0, a1_top, a1_low, a2_top, a2_low, a3_top, a3_low, b_ref,
    w_ref, act_ref, sems
):
    step = pl.program_id(0)
    hidden = w0.shape[0]
    width = w0.shape[1] // 8
    second = width - FIRST

    def copies():
        made = []
        for j, w in enumerate((w0, w1)):
            rows = pl.ds(j * hidden, hidden)
            for k in range(4):
                start = pl.multiple_of(block_of(place_ref, k) * width, 128)
                made.append(
                    pltpu.make_async_copy(
                        w.at[:, pl.ds(start, FIRST)],
                        w_ref.at[rows, pl.ds(k * FIRST, FIRST)],
                        sems.at[j, 2 * k],
                    )
                )
                made.append(
                    pltpu.make_async_copy(
                        w.at[:, pl.ds(start + FIRST, second)],
                        w_ref.at[rows, pl.ds(4 * FIRST + k * second, second)],
                        sems.at[j, 2 * k + 1],
                    )
                )
        return made

    @pl.when(step == 0)
    def _():
        for copy in copies():
            copy.start()

    for j in range(2):
        own, got = 2 * j * hidden, 2 * (1 - j) * hidden
        gate = sum_ref[:, own : own + hidden] + got_ref[:, got : got + hidden].astype(F32)
        up = sum_ref[:, own + hidden : own + 2 * hidden] + got_ref[
            :, got + hidden : got + 2 * hidden
        ].astype(F32)
        act_ref[:, j * hidden : (j + 1) * hidden] = (gate / (1.0 + jnp.exp(-gate)) * up).astype(BF)

    @pl.when(step == 0)
    def _():
        for copy in copies():
            copy.wait()

    def out(start, size):
        return dot(act_ref[...], w_ref[:, start : start + size]).astype(BF)

    a0[...] = out(0, FIRST)
    b_ref[...] = out(4 * FIRST, 4 * second)

    @pl.when(step == 0)
    def _():
        for k, ref in ((1, a1_top), (2, a2_top), (3, a3_top)):
            ref[...] = out(k * FIRST, FIRST)

    @pl.when(step == 1)
    def _():
        for k, ref in ((1, a1_low), (2, a2_low), (3, a3_low)):
            ref[...] = out(k * FIRST, FIRST)


def add_kernel(a1, got1, a3, got3, out1, out3):
    out1[...] = (a1[...].astype(F32) + got1[...].astype(F32)).astype(BF)
    out3[...] = (a3[...].astype(F32) + got3[...].astype(F32)).astype(BF)


def ysum_kernel(a0, left_top, left_low, right_top, right_low, out_ref):
    half = left_top.shape[0]
    top = a0[:half].astype(F32) + left_top[...].astype(F32) + right_top[...].astype(F32)
    low = a0[half:].astype(F32) + left_low[...].astype(F32) + right_low[...].astype(F32)
    out_ref[:half] = top.astype(BF)
    out_ref[half:] = low.astype(BF)


def mix_kernel(hi_ref, lo_ref, back_ref, own_ref, p1, p2, p3):
    width = own_ref.shape[1]
    for k, ref in enumerate((own_ref, p1, p2, p3)):
        ref[...] = mixed(hi_ref, lo_ref, back_ref[:, k * width : (k + 1) * width]).astype(ref.dtype)


def layer_kernel(hidden_ref, hi_ref, lo_ref, back_ref, own_ref, p1, p2, p3, gain_ref, out_ref, scaled_ref):
    first = mixed(hi_ref, lo_ref, back_ref[...])
    second = own_ref[...] + p1[...].astype(F32) + p2[...].astype(F32) + p3[...].astype(F32)
    for mix, cols in ((first, slice(0, FIRST)), (second, slice(FIRST, hidden_ref.shape[1]))):
        total = hidden_ref[:, cols].astype(F32) + mix
        out_ref[:, cols] = total.astype(BF)
        scaled_ref[:, cols] = (total * gain_ref[:, cols]).astype(BF)


def squares_of(rows, inverse):
    total = jnp.zeros((rows.shape[0], 128), F32)
    for c in range(0, rows.shape[1], 128):
        value = rows[:, c : c + 128].astype(F32)
        total = total + value * value * inverse[:, c : c + 128]
    return total


def head_kernel(place_ref, inverse_ref, w0, w1, *refs):
    *pieces, own_ref, other_ref, w_ref, rows_ref, sems, row_sems = refs
    vocab = w0.shape[0]
    tokens, width = pieces[0].shape[2:]
    blocks = rows_ref.shape[0]

    copies = []
    for j, w in enumerate((w0, w1)):
        for k in range(4):
            start = pl.multiple_of(block_of(place_ref, k) * width, 128)
            copies.append(
                pltpu.make_async_copy(
                    w.at[:, pl.ds(start, width)],
                    w_ref.at[pl.ds(j * vocab, vocab), pl.ds(k * width, width)],
                    sems.at[j, k],
                )
            )
    moves = []
    base = 0
    for i, piece in enumerate(pieces):
        count = piece.shape[0]
        for k in range(4):
            moves.append(
                pltpu.make_async_copy(
                    piece.at[:, k],
                    rows_ref.at[pl.ds(base, count), :, pl.ds(k * width, width)],
                    row_sems.at[i, k],
                )
            )
        base += count
    for copy in moves + copies[4:] + copies[:4]:
        copy.start()
    for move in moves:
        move.wait()

    @pl.loop(0, blocks)
    def _(i):
        at = pl.ds(pl.multiple_of(i * tokens, tokens), tokens)
        squares = jnp.zeros((tokens, 128), F32)
        for k in range(4):
            rows = rows_ref[i, :, k * width : (k + 1) * width]
            squares = squares + squares_of(rows, inverse_ref[k : k + 1])
        own_ref[at, vocab:] = squares
        other_ref[at, vocab:] = squares

    for j, ref in ((1, other_ref), (0, own_ref)):
        for copy in copies[4 * j : 4 * j + 4]:
            copy.wait()

        @pl.loop(0, blocks // 8)
        def _(i, j=j, ref=ref):
            at = pl.ds(pl.multiple_of(i * 8 * tokens, 8 * tokens), 8 * tokens)
            rows = rows_ref[pl.ds(i * 8, 8)].reshape(8 * tokens, 4 * width)
            ref[at, :vocab] = lax.dot_general(
                rows,
                w_ref[j * vocab : (j + 1) * vocab, :],
                (((1,), (1,)), ((), ())),
                preferred_element_type=F32,
            )


def columns_of(full, ids, wanted):
    peak = jnp.max(full, axis=1, keepdims=True)
    total = jnp.sum(jnp.exp(full - peak), axis=1, keepdims=True)
    target = jnp.sum(jnp.where(ids == wanted, full, 0.0), axis=1, keepdims=True)
    lane = lax.broadcasted_iota(jnp.int32, (full.shape[0], 128), 1)
    return jnp.where(lane == 0, peak, jnp.where(lane == 1, total, target)).T


def stats_kernel(model, first_ref, order_ref, own_ref, got_ref, wanted_ref, before_ref, stats_ref):
    vocab = own_ref.shape[1] - 128
    nodes, _, tokens, _ = wanted_ref.shape
    blocks = own_ref.shape[0] // tokens
    halves = [i // (blocks // 2) for i in range(blocks)]
    wanted = jnp.concatenate([wanted_ref[order_ref[i], halves[i]] for i in range(blocks)], axis=0)
    squares = jnp.sum(own_ref[:, vocab:] + got_ref[:, vocab:], axis=1, keepdims=True)
    scale = lax.rsqrt(squares / model + 1e-06)
    full = (own_ref[:, :vocab] + got_ref[:, :vocab]) * scale
    ids = first_ref[0] + lax.broadcasted_iota(jnp.int32, full.shape, 1)
    columns = columns_of(full, ids, wanted)
    stats_ref[...] = before_ref[...]
    for i in range(blocks):
        for j in range(3):
            row = columns[j : j + 1, i * tokens : (i + 1) * tokens]
            lane = 64 * halves[i]
            stats_ref[pl.ds(j * nodes + order_ref[i], 1), lane : lane + tokens] = row


def paired(terms):
    if len(terms) == 2:
        return terms[0] + terms[1]
    return (terms[0] + terms[2]) + (terms[1] + terms[3])


def combined(refs):
    third = refs[0].shape[0] // 3
    peaks = [ref[:third] for ref in refs]
    peak = functools.reduce(jnp.maximum, peaks)
    total = paired([ref[third : 2 * third] * jnp.exp(own - peak) for ref, own in zip(refs, peaks)])
    return peak, total, paired([ref[2 * third :] for ref in refs])


def merge_kernel(*refs):
    *ins, out_ref = refs
    third = out_ref.shape[0] // 3
    for j, value in enumerate(combined(ins)):
        out_ref[j * third : (j + 1) * third] = value


def final_kernel(*refs):
    *ins, policy_ref, logp_ref, kl_ref = refs
    peak, total, target = combined(ins)
    spaced = target - peak - jnp.log(total)
    half = policy_ref.shape[0] * 128 // (2 * spaced.shape[0])
    tokens = 2 * half
    packed = jnp.concatenate([spaced[:, :half], spaced[:, 64 : 64 + half]], axis=1)
    lines = []
    for at in range(0, spaced.shape[0] * tokens, 128):
        node, lane = at // tokens, at % tokens
        pieces = [packed[node : node + 1, lane:]]
        pieces.append(packed[node + 1 : node + 2, : 128 - (tokens - lane)])
        lines.append(jnp.concatenate(pieces, axis=1))
    logp = jnp.concatenate(lines, axis=0)
    logp_ref[...] = logp
    kl_ref[...] = 0.5 * (policy_ref[...] - logp) * (policy_ref[...] - logp)


def neighbours(stats, axis):
    return [stats] + [shift(stats, axis, k) for k in range(1, lax.axis_size(axis))]


def ring(block, axis):
    half = block.shape[0] // 2
    behind, ahead = shift(block, axis, 1), shift(block, axis, -1)
    return behind, shift(behind[:half], axis, 1), shift(ahead[half:], axis, -1), ahead


def like(*shape, dtype=BF):
    return jax.ShapeDtypeStruct(shape, dtype)


def vmem(mib):
    return pltpu.CompilerParams(vmem_limit_bytes=mib * 1024 * 1024)


def over_nodes(rows):
    nodes = lax.axis_size("x") * lax.axis_size("z")
    cut = rows.reshape(nodes, rows.shape[0] // nodes, rows.shape[1])
    return lax.all_to_all(cut, ("x", "z"), split_axis=0, concat_axis=0, tiled=True).reshape(rows.shape)


def shards(hidden, routes, route_weights, w_gate, w_up, w_down, gain, head, targets, policy_logp):
    tokens, width = hidden.shape
    second = width - FIRST
    y = lax.axis_index("y")
    core = lax.axis_index("core")
    n_node = lax.axis_size("x") * lax.axis_size("z")
    slots = n_node * SLOTS
    half = slots // 2
    model = 8 * width
    hid = w_gate.shape[2]
    hbm = pl.BlockSpec(memory_space=pl.ANY)
    in_vmem = pl.BlockSpec(memory_space=pltpu.VMEM)

    near_own = pl.pallas_call(
        near_kernel, out_shape=like(tokens + 16, second), compiler_params=vmem(VMEM), name="near"
    )(hidden, gain.reshape(1, width))
    near = [near_own]
    near = near + [shift(near[0], "y", k) for k in (1, 2, 3)]
    pick, mix_hi, mix_lo, send_a = pl.pallas_call(
        route_kernel,
        out_shape=(like(slots, tokens),) * 3 + (like(slots, FIRST),),
        compiler_params=vmem(VMEM),
        name="route",
    )(routes.T, route_weights.T, hidden)
    a0 = over_nodes(send_a)
    send_b, inverse = pl.pallas_call(
        spread_kernel,
        out_shape=(like(slots, 4 * second), like(4, width, dtype=F32)),
        compiler_params=vmem(VMEM),
        name="spread",
    )(pick, *near)
    gate_mat, up_mat, down_mat = w_gate[0], w_up[0], w_down[0]
    gate_other, up_other, down_other = (shift(w, "core", 1) for w in (gate_mat, up_mat, down_mat))
    a0, send_b = lax.optimization_barrier((a0, send_b))
    a1, a3 = shift(a0, "y", 1), shift(a0, "y", -1)
    b = over_nodes(send_b)
    a2_top, a2_low = shift(a1[:half], "y", 1), shift(a3[half:], "y", -1)

    head_other = shift(head, "core", 1)
    place = jnp.stack([y, core]).astype(jnp.int32)

    def rows_of(columns):
        return pl.BlockSpec((half, columns), lambda i, place: (i, 0))

    def whole(columns):
        return pl.BlockSpec((half, columns), lambda i, place: (0, 0))

    partial = pl.pallas_call(
        up_first_kernel,
        grid_spec=pltpu.PrefetchScalarGridSpec(
            num_scalar_prefetch=1,
            grid=(2,),
            in_specs=[rows_of(FIRST)] * 3 + [hbm] * 4,
            out_specs=rows_of(4 * hid),
            scratch_shapes=[pltpu.VMEM((3 * FIRST, 4 * hid), BF), pltpu.SemaphoreType.DMA((4, 3))],
        ),
        out_shape=like(slots, 4 * hid, dtype=F32),
        compiler_params=vmem(VMEM),
        cost_estimate=pl.CostEstimate(
            flops=24 * slots * FIRST * hid, bytes_accessed=24 * FIRST * hid, transcendentals=0
        ),
        name="up_first",
    )(place, a0, a1, a3, gate_mat, up_mat, gate_other, up_other)
    partial, partial_out = pl.pallas_call(
        up_second_kernel,
        grid_spec=pltpu.PrefetchScalarGridSpec(
            num_scalar_prefetch=1,
            grid=(2,),
            in_specs=[rows_of(4 * hid), rows_of(4 * second), whole(FIRST), whole(FIRST)] + [hbm] * 4,
            out_specs=[rows_of(4 * hid)] * 2,
            scratch_shapes=[
                pltpu.VMEM((FIRST + 4 * second, 4 * hid), BF),
                pltpu.SemaphoreType.DMA((2, 4, 4)),
            ],
        ),
        out_shape=(like(slots, 4 * hid, dtype=F32), like(slots, 4 * hid)),
        compiler_params=vmem(VMEM),
        name="up_second",
    )(place, partial, b, a2_top, a2_low, gate_mat, up_mat, gate_other, up_other)
    partial_got = shift(partial_out, "core", 1)

    a0, a1_top, a1_low, a2_top, a2_low, a3_top, a3_low, b = pl.pallas_call(
        down_kernel,
        grid_spec=pltpu.PrefetchScalarGridSpec(
            num_scalar_prefetch=1,
            grid=(2,),
            in_specs=[rows_of(4 * hid), rows_of(4 * hid), hbm, hbm],
            out_specs=[rows_of(FIRST)] + [whole(FIRST)] * 6 + [rows_of(4 * second)],
            scratch_shapes=[
                pltpu.VMEM((2 * hid, 4 * width), BF),
                pltpu.VMEM((half, 2 * hid), BF),
                pltpu.SemaphoreType.DMA((2, 8)),
            ],
        ),
        out_shape=(like(slots, FIRST),) + (like(half, FIRST),) * 6 + (like(slots, 4 * second),),
        compiler_params=vmem(58),
        name="down",
    )(place, partial, partial_got, down_mat, down_other)

    got1, got3 = shift(a2_top, "y", -1), shift(a2_low, "y", 1)
    left_low, right_top = shift(a1_low, "y", -1), shift(a3_top, "y", 1)
    back_b = over_nodes(b)
    a1_top, a3_low = pl.pallas_call(
        add_kernel, out_shape=(like(half, FIRST),) * 2, compiler_params=vmem(VMEM), name="add"
    )(a1_top, got1, a3_low, got3)
    left_top, right_low = shift(a1_top, "y", -1), shift(a3_low, "y", 1)
    summed = pl.pallas_call(
        ysum_kernel, out_shape=like(slots, FIRST), compiler_params=vmem(VMEM), name="ysum"
    )(a0, left_top, left_low, right_top, right_low)
    back_a = over_nodes(summed)
    own, *others = pl.pallas_call(
        mix_kernel,
        out_shape=(like(tokens, second, dtype=F32),) + (like(tokens, second),) * 3,
        compiler_params=vmem(VMEM),
        name="mix",
    )(mix_hi, mix_lo, back_b)
    arrived = [shift(part, "y", -k) for k, part in zip((1, 2, 3), others)]
    layer_out, scaled = pl.pallas_call(
        layer_kernel,
        out_shape=(like(tokens, width), like(tokens, width)),
        compiler_params=vmem(VMEM),
        name="layer",
    )(hidden, mix_hi, mix_lo, back_a, own, *arrived, gain.reshape(1, width))

    part = tokens // 2
    by_y = [scaled] + [shift(scaled, "y", k) for k in (1, 2, 3)]
    part_a = jnp.stack([rows[:part] for rows in by_y])
    part_b = jnp.stack([rows[part:] for rows in by_y])
    behind_a, far_a1, far_a2, ahead_a = ring(part_a, "x")
    behind_b, far_b1, far_b2, ahead_b = ring(part_b, "z")
    line_a = jnp.stack([part_a, behind_a, jnp.concatenate([far_a1, far_a2]), ahead_a])
    line_b = jnp.stack([part_b, behind_b, jnp.concatenate([far_b1, far_b2]), ahead_b])
    vocab_rows = head.shape[0]
    first_id = (lax.axis_index(AXES) * vocab_rows).reshape(1).astype(jnp.int32)
    x, z = lax.axis_index("x"), lax.axis_index("z")
    wanted = targets.reshape(n_node, 2, part, 1)

    def node_at(back_x, back_z):
        return ((x - back_x) % 4) * 4 + (z - back_z) % 4

    def scored(pieces):
        rows = sum(piece.shape[0] for piece in pieces) * part
        own, other = pl.pallas_call(
            head_kernel,
            grid_spec=pltpu.PrefetchScalarGridSpec(
                num_scalar_prefetch=1,
                grid=(),
                in_specs=[in_vmem] + [hbm] * (2 + len(pieces)),
                out_specs=[in_vmem] * 2,
                scratch_shapes=[
                    pltpu.VMEM((2 * vocab_rows, 4 * width), BF),
                    pltpu.VMEM((rows // part, part, 4 * width), BF),
                    pltpu.SemaphoreType.DMA((2, 4)),
                    pltpu.SemaphoreType.DMA((len(pieces), 4)),
                ],
            ),
            out_shape=(like(rows, vocab_rows + 128, dtype=F32),) * 2,
            compiler_params=vmem(VMEM),
            cost_estimate=pl.CostEstimate(
                flops=16 * rows * width * vocab_rows,
                bytes_accessed=16 * width * vocab_rows,
                transcendentals=0,
            ),
            name="head",
        )(place, inverse, head, head_other, *pieces)
        return own, other

    def counted(own, got, order, stats):
        return pl.pallas_call(
            functools.partial(stats_kernel, model),
            grid_spec=pltpu.PrefetchScalarGridSpec(
                num_scalar_prefetch=2, grid=(), in_specs=[in_vmem] * 4, out_specs=in_vmem
            ),
            out_shape=like(3 * n_node, 128, dtype=F32),
            compiler_params=vmem(VMEM),
            cost_estimate=pl.CostEstimate(flops=1000, bytes_accessed=1000, transcendentals=0),
            name="stats",
        )(first_id, jnp.stack(order).astype(jnp.int32), own, got, wanted, stats)

    behind_a, ahead_a = shift(line_a, "z", 1), shift(line_a, "z", -1)
    behind_b, ahead_b = shift(line_b, "x", 1), shift(line_b, "x", -1)
    scores = scored((line_a, line_b))
    nearby = (behind_a, ahead_a, behind_b, ahead_b)
    nearby, (own, other) = lax.optimization_barrier((nearby, scores))
    behind_a, ahead_a, behind_b, ahead_b = nearby
    far_a1, far_a2 = shift(behind_a[:2], "z", 1), shift(ahead_a[2:], "z", -1)
    far_b1, far_b2 = shift(behind_b[:2], "x", 1), shift(ahead_b[2:], "x", -1)
    order = [node_at(i, 0) for i in range(4)] + [node_at(0, i) for i in range(4)]
    stats = jnp.zeros((3 * n_node, 128), F32)
    stats = counted(own, shift(other, "core", 1), order, stats)
    scores = scored((behind_a, ahead_a, behind_b, ahead_b))
    far = (far_a1, far_a2, far_b1, far_b2)
    far, (own, other), stats = lax.optimization_barrier((far, scores, stats))
    order = [node_at(i, k) for k in (1, 3) for i in range(4)]
    order = order + [node_at(k, i) for k in (1, 3) for i in range(4)]
    stats = counted(own, shift(other, "core", 1), order, stats)
    own, other = scored(far)
    order = [node_at(i, 2) for i in range(4)] + [node_at(2, i) for i in range(4)]
    stats = counted(own, shift(other, "core", 1), order, stats)
    for axis in ("core", "y", "z"):
        stats = pl.pallas_call(
            merge_kernel, out_shape=like(3 * n_node, 128, dtype=F32), name="merge"
        )(*neighbours(stats, axis))
    ref_logp, kl = pl.pallas_call(
        final_kernel, out_shape=(like(n_node * tokens // 128, 128, dtype=F32),) * 2, name="final"
    )(*neighbours(stats, "x"), policy_logp.reshape(-1, 128))
    return layer_out, ref_logp.reshape(-1), kl.reshape(-1)


def solution(mesh):
    split = Mesh(mesh.devices.reshape(4, 4, 4, 2), AXES)
    node, local = ("x", "z"), ("y", "core")
    placed = (
        P(node, local),
        P(node, None),
        P(node, None),
        P(node, None, local),
        P(node, None, local),
        P(node, local, None),
        P(local),
        P(AXES, None),
        P(),
        P(),
    )
    return jax.shard_map(
        shards,
        mesh=split,
        in_specs=placed,
        out_specs=(P(node, local), P(), P()),
        check_vma=False,
    )
```

```python
import functools
import jax
import jax.numpy as jnp
from jax import lax
from jax.experimental import pallas as pl
from jax.experimental.pallas import tpu as pltpu
from jax.sharding import Mesh, PartitionSpec as P

BF = jnp.bfloat16
F32 = jnp.float32
AXES = ("x", "z", "y", "core")
SLOTS = 40
FIRST = 512
VMEM = 48


def shift(value, axis, step):
    size = lax.axis_size(axis)
    return lax.ppermute(value, axis, [(i, (i + step) % size) for i in range(size)])


def dot(a, b):
    return jnp.dot(a, b, preferred_element_type=F32)


def near_kernel(hidden_ref, gain_ref, near_ref):
    tokens, width = hidden_ref.shape
    second = near_ref.shape[1]
    near_ref[:tokens] = hidden_ref[:, FIRST:]
    gain = gain_ref[...]
    hi = gain.astype(BF).astype(F32)
    rows = jnp.zeros((near_ref.shape[0] - tokens, second), F32)
    row = lax.broadcasted_iota(jnp.int32, rows.shape, 0)
    for i, part in enumerate((hi, gain - hi)):
        for j, start in enumerate(range(0, width, second)):
            piece = part[:, start : start + second]
            piece = jnp.pad(piece, ((0, 0), (0, second - piece.shape[1])))
            rows = jnp.where(row == 4 * i + j, piece, rows)
    near_ref[tokens:] = rows.astype(BF)


def route_kernel(routes_ref, weights_ref, hidden_ref, pick_ref, hi_ref, lo_ref, send_ref):
    top, tokens = routes_ref.shape
    slots = pick_ref.shape[0]
    experts = slots // SLOTS
    ids = lax.broadcasted_iota(jnp.int32, (experts, tokens), 0)
    named = jnp.zeros((experts, tokens), F32)
    gates = jnp.zeros((experts, tokens), F32)
    for k in range(top):
        hit = routes_ref[k : k + 1, :] == ids
        named = named + jnp.where(hit, 1.0, 0.0)
        gates = gates + jnp.where(hit, weights_ref[k : k + 1, :], 0.0)
    row = lax.broadcasted_iota(jnp.int32, (tokens, tokens), 0)
    col = lax.broadcasted_iota(jnp.int32, (tokens, tokens), 1)
    count = dot(named.astype(BF), jnp.where(row < col, 1.0, 0.0).astype(BF))
    slot = lax.broadcasted_iota(jnp.int32, (slots, experts), 0)
    expert = lax.broadcasted_iota(jnp.int32, (slots, experts), 1)
    inside = (slot >= expert * SLOTS) & (slot < expert * SLOTS + SLOTS)
    spread = jnp.where(inside, 1.0, 0.0).astype(BF)
    at = jnp.sum(jnp.where(inside, slot - expert * SLOTS, 0).astype(F32), axis=1, keepdims=True)
    gates_hi = gates.astype(BF)
    gates_lo = (gates - gates_hi.astype(F32)).astype(BF)
    placed = (dot(spread, named.astype(BF)) > 0.5) & (dot(spread, count.astype(BF)) == at)
    hi_ref[...] = jnp.where(placed, dot(spread, gates_hi), 0.0).astype(BF)
    lo_ref[...] = jnp.where(placed, dot(spread, gates_lo), 0.0).astype(BF)
    pick = jnp.where(placed, 1.0, 0.0).astype(BF)
    pick_ref[...] = pick
    send_ref[...] = dot(pick, hidden_ref[:, :FIRST]).astype(BF)


def spread_kernel(pick_ref, h0, h1, h2, h3, send_ref, inverse_ref):
    tokens = pick_ref.shape[1]
    second = h0.shape[1]
    width = inverse_ref.shape[1]
    for k, ref in enumerate((h0, h1, h2, h3)):
        send_ref[:, k * second : (k + 1) * second] = dot(pick_ref[...], ref[:tokens]).astype(BF)
        rows = ref[tokens:].astype(F32)
        for j, start in enumerate(range(0, width, second)):
            size = min(second, width - start)
            gain = rows[j : j + 1, :size] + rows[4 + j : 5 + j, :size]
            inverse_ref[k : k + 1, start : start + size] = 1.0 / (gain * gain)


def mixed(hi_ref, lo_ref, rows):
    across = (((0,), (0,)), ((), ()))
    hi = lax.dot_general(hi_ref[...], rows, across, preferred_element_type=F32)
    return hi + lax.dot_general(lo_ref[...], rows, across, preferred_element_type=F32)


def block_of(place_ref, k):
    return 2 * lax.rem(place_ref[0] + 4 - k, 4) + place_ref[1]


def up_copies(place_ref, sources, w_ref, sems, places, offset, size, base):
    hidden = sources[0].shape[1]
    width = sources[0].shape[0] // 8
    made = []
    for j, w in enumerate(sources):
        for i, k in enumerate(places):
            start = pl.multiple_of(block_of(place_ref, k) * width + offset, 128)
            made.append(
                pltpu.make_async_copy(
                    w.at[pl.ds(start, size), :],
                    w_ref.at[pl.ds(base + i * size, size), pl.ds(j * hidden, hidden)],
                    sems.at[j, i],
                )
            )
    return made


def up_first_kernel(place_ref, a0, a1, a3, w0, w1, w2, w3, sum_ref, w_ref, sems):
    hidden = w0.shape[1]

    @pl.when(pl.program_id(0) == 0)
    def _():
        copies = up_copies(place_ref, (w0, w1, w2, w3), w_ref, sems, (0, 1, 3), 0, FIRST, 0)
        for copy in copies:
            copy.start()
        for copy in copies:
            copy.wait()

    @pl.loop(0, 4)
    def _(j):
        cols = pl.ds(pl.multiple_of(j * hidden, hidden), hidden)
        part = dot(a0[...], w_ref[:FIRST, cols])
        for k, ref in ((1, a1), (2, a3)):
            part = part + dot(ref[...], w_ref[k * FIRST : (k + 1) * FIRST, cols])
        sum_ref[:, cols] = part


def up_second_kernel(
    place_ref, before_ref, b_ref, a2_top, a2_low, w0, w1, w2, w3, sum_ref, out_ref, w_ref, a2_ref, sems
):
    step = pl.program_id(0)
    hidden = w0.shape[1]
    second = w0.shape[0] // 8 - FIRST

    @pl.when(step == 0)
    def _():
        sources = (w0, w1, w2, w3)
        copies = up_copies(place_ref, sources, w_ref, sems.at[0], (2,), 0, FIRST, 0)
        copies = copies + up_copies(
            place_ref, sources, w_ref, sems.at[1], (0, 1, 2, 3), FIRST, second, FIRST
        )
        for copy in copies:
            copy.start()
        for copy in copies:
            copy.wait()

    @pl.when(step == 0)
    def _():
        a2_ref[...] = a2_top[...]

    @pl.when(step == 1)
    def _():
        a2_ref[...] = a2_low[...]

    @pl.loop(0, 4)
    def _(j):
        cols = pl.ds(pl.multiple_of(j * hidden, hidden), hidden)
        part = dot(b_ref[...], w_ref[FIRST:, cols]) + dot(a2_ref[...], w_ref[:FIRST, cols])
        part = part + before_ref[:, cols]
        sum_ref[:, cols] = part
        out_ref[:, cols] = part.astype(BF)


def down_kernel(
    place_ref, sum_ref, got_ref, w0, w1, a0, a1_top, a1_low, a2_top, a2_low, a3_top, a3_low, b_ref,
    w_ref, act_ref, done_ref, sems
):
    step = pl.program_id(0)
    hidden = w0.shape[0]
    width = w0.shape[1] // 8
    second = width - FIRST

    def copies():
        made = []
        for j, w in enumerate((w0, w1)):
            rows = pl.ds(j * hidden, hidden)
            for k in range(4):
                start = pl.multiple_of(block_of(place_ref, k) * width, 128)
                made.append(
                    pltpu.make_async_copy(
                        w.at[:, pl.ds(start, FIRST)],
                        w_ref.at[rows, pl.ds(k * FIRST, FIRST)],
                        sems.at[j, 2 * k],
                    )
                )
                made.append(
                    pltpu.make_async_copy(
                        w.at[:, pl.ds(start + FIRST, second)],
                        w_ref.at[rows, pl.ds(4 * FIRST + k * second, second)],
                        sems.at[j, 2 * k + 1],
                    )
                )
        return made

    @pl.when(step == 0)
    def _():
        for copy in copies()[0::2] + copies()[1::2]:
            copy.start()

    for j in range(2):
        own, got = 2 * j * hidden, 2 * (1 - j) * hidden
        gate = sum_ref[:, own : own + hidden] + got_ref[:, got : got + hidden].astype(F32)
        up = sum_ref[:, own + hidden : own + 2 * hidden] + got_ref[
            :, got + hidden : got + 2 * hidden
        ].astype(F32)
        act_ref[:, j * hidden : (j + 1) * hidden] = (gate / (1.0 + jnp.exp(-gate)) * up).astype(BF)

    @pl.when(step == 0)
    def _():
        for copy in copies()[0::2]:
            copy.wait()

    @pl.loop(0, 4)
    def _(k):
        cols = pl.ds(pl.multiple_of(k * FIRST, FIRST), FIRST)
        done_ref[k] = dot(act_ref[...], w_ref[:, cols]).astype(BF)

    @pl.when(step == 0)
    def _():
        for copy in copies()[1::2]:
            copy.wait()

    b_ref[...] = dot(act_ref[...], w_ref[:, 4 * FIRST :]).astype(BF)

    a0[...] = done_ref[0]

    @pl.when(step == 0)
    def _():
        for k, ref in ((1, a1_top), (2, a2_top), (3, a3_top)):
            ref[...] = done_ref[k]

    @pl.when(step == 1)
    def _():
        for k, ref in ((1, a1_low), (2, a2_low), (3, a3_low)):
            ref[...] = done_ref[k]


def add_kernel(a1, got1, a3, got3, out1, out3):
    out1[...] = (a1[...].astype(F32) + got1[...].astype(F32)).astype(BF)
    out3[...] = (a3[...].astype(F32) + got3[...].astype(F32)).astype(BF)


def ysum_kernel(a0, left_top, left_low, right_top, right_low, out_ref):
    half = left_top.shape[0]
    top = a0[:half].astype(F32) + left_top[...].astype(F32) + right_top[...].astype(F32)
    low = a0[half:].astype(F32) + left_low[...].astype(F32) + right_low[...].astype(F32)
    out_ref[:half] = top.astype(BF)
    out_ref[half:] = low.astype(BF)


def mix_kernel(hi_ref, lo_ref, back_ref, own_ref, p1, p2, p3):
    width = own_ref.shape[1]
    for k, ref in enumerate((own_ref, p1, p2, p3)):
        ref[...] = mixed(hi_ref, lo_ref, back_ref[:, k * width : (k + 1) * width]).astype(ref.dtype)


def layer_kernel(hidden_ref, hi_ref, lo_ref, back_ref, own_ref, p1, p2, p3, gain_ref, out_ref, scaled_ref):
    first = mixed(hi_ref, lo_ref, back_ref[...])
    second = own_ref[...] + p1[...].astype(F32) + p2[...].astype(F32) + p3[...].astype(F32)
    for mix, cols in ((first, slice(0, FIRST)), (second, slice(FIRST, hidden_ref.shape[1]))):
        total = hidden_ref[:, cols].astype(F32) + mix
        out_ref[:, cols] = total.astype(BF)
        scaled_ref[:, cols] = (total * gain_ref[:, cols]).astype(BF)


def squares_of(rows, inverse):
    total = jnp.zeros((rows.shape[0], 128), F32)
    for c in range(0, rows.shape[1], 128):
        value = rows[:, c : c + 128].astype(F32)
        total = total + value * value * inverse[:, c : c + 128]
    return total


def head_kernel(place_ref, inverse_ref, w0, w1, *refs):
    *pieces, own_ref, other_ref, w_ref, rows_ref, sems, row_sems = refs
    vocab = w0.shape[0]
    tokens, width = pieces[0].shape[2:]
    blocks = rows_ref.shape[0]

    copies = []
    for j, w in enumerate((w0, w1)):
        for k in range(4):
            start = pl.multiple_of(block_of(place_ref, k) * width, 128)
            copies.append(
                pltpu.make_async_copy(
                    w.at[:, pl.ds(start, width)],
                    w_ref.at[pl.ds(j * vocab, vocab), pl.ds(k * width, width)],
                    sems.at[j, k],
                )
            )
    moves = []
    base = 0
    for i, piece in enumerate(pieces):
        count = piece.shape[0]
        for k in range(4):
            moves.append(
                pltpu.make_async_copy(
                    piece.at[:, k],
                    rows_ref.at[pl.ds(base, count), :, pl.ds(k * width, width)],
                    row_sems.at[i, k],
                )
            )
        base += count
    for copy in moves + copies[4:] + copies[:4]:
        copy.start()
    for move in moves:
        move.wait()

    @pl.loop(0, blocks)
    def _(i):
        at = pl.ds(pl.multiple_of(i * tokens, tokens), tokens)
        squares = jnp.zeros((tokens, 128), F32)
        for k in range(4):
            rows = rows_ref[i, :, k * width : (k + 1) * width]
            squares = squares + squares_of(rows, inverse_ref[k : k + 1])
        own_ref[at, vocab:] = squares
        other_ref[at, vocab:] = squares

    for j, ref in ((1, other_ref), (0, own_ref)):
        for copy in copies[4 * j : 4 * j + 4]:
            copy.wait()

        @pl.loop(0, blocks // 8 * (vocab // 256))
        def _(i, j=j, ref=ref):
            group, part = i // (vocab // 256), i % (vocab // 256)
            at = pl.ds(pl.multiple_of(group * 8 * tokens, 8 * tokens), 8 * tokens)
            rows = rows_ref[pl.ds(group * 8, 8)].reshape(8 * tokens, 4 * width)
            cols = pl.ds(pl.multiple_of(part * 256, 256), 256)
            ref[at, cols] = lax.dot_general(
                rows,
                w_ref[pl.ds(pl.multiple_of(j * vocab + part * 256, 256), 256), :],
                (((1,), (1,)), ((), ())),
                preferred_element_type=F32,
            )


def columns_of(full, ids, wanted):
    peak = jnp.max(full, axis=1, keepdims=True)
    total = jnp.sum(jnp.exp(full - peak), axis=1, keepdims=True)
    target = jnp.sum(jnp.where(ids == wanted, full, 0.0), axis=1, keepdims=True)
    lane = lax.broadcasted_iota(jnp.int32, (full.shape[0], 128), 1)
    return jnp.where(lane == 0, peak, jnp.where(lane == 1, total, target)).T


def stats_kernel(model, first_ref, order_ref, own_ref, got_ref, wanted_ref, before_ref, stats_ref):
    vocab = own_ref.shape[1] - 128
    nodes, _, tokens, _ = wanted_ref.shape
    blocks = own_ref.shape[0] // tokens
    halves = [i // (blocks // 2) for i in range(blocks)]
    wanted = jnp.concatenate([wanted_ref[order_ref[i], halves[i]] for i in range(blocks)], axis=0)
    squares = jnp.sum(own_ref[:, vocab:] + got_ref[:, vocab:], axis=1, keepdims=True)
    scale = lax.rsqrt(squares / model + 1e-06)
    full = (own_ref[:, :vocab] + got_ref[:, :vocab]) * scale
    ids = first_ref[0] + lax.broadcasted_iota(jnp.int32, full.shape, 1)
    columns = columns_of(full, ids, wanted)
    stats_ref[...] = before_ref[...]
    for i in range(blocks):
        for j in range(3):
            row = columns[j : j + 1, i * tokens : (i + 1) * tokens]
            lane = 64 * halves[i]
            stats_ref[pl.ds(j * nodes + order_ref[i], 1), lane : lane + tokens] = row


def paired(terms):
    if len(terms) == 2:
        return terms[0] + terms[1]
    return (terms[0] + terms[2]) + (terms[1] + terms[3])


def combined(refs):
    third = refs[0].shape[0] // 3
    peaks = [ref[:third] for ref in refs]
    peak = functools.reduce(jnp.maximum, peaks)
    total = paired([ref[third : 2 * third] * jnp.exp(own - peak) for ref, own in zip(refs, peaks)])
    return peak, total, paired([ref[2 * third :] for ref in refs])


def merge_kernel(*refs):
    *ins, out_ref = refs
    third = out_ref.shape[0] // 3
    for j, value in enumerate(combined(ins)):
        out_ref[j * third : (j + 1) * third] = value


def final_kernel(*refs):
    *ins, policy_ref, logp_ref, kl_ref = refs
    peak, total, target = combined(ins)
    spaced = target - peak - jnp.log(total)
    half = policy_ref.shape[0] * 128 // (2 * spaced.shape[0])
    tokens = 2 * half
    packed = jnp.concatenate([spaced[:, :half], spaced[:, 64 : 64 + half]], axis=1)
    lines = []
    for at in range(0, spaced.shape[0] * tokens, 128):
        node, lane = at // tokens, at % tokens
        pieces = [packed[node : node + 1, lane:]]
        pieces.append(packed[node + 1 : node + 2, : 128 - (tokens - lane)])
        lines.append(jnp.concatenate(pieces, axis=1))
    logp = jnp.concatenate(lines, axis=0)
    logp_ref[...] = logp
    kl_ref[...] = 0.5 * (policy_ref[...] - logp) * (policy_ref[...] - logp)


def neighbours(stats, axis):
    return [stats] + [shift(stats, axis, k) for k in range(1, lax.axis_size(axis))]


def ring(block, axis):
    half = block.shape[0] // 2
    behind, ahead = shift(block, axis, 1), shift(block, axis, -1)
    return behind, shift(behind[:half], axis, 1), shift(ahead[half:], axis, -1), ahead


def like(*shape, dtype=BF):
    return jax.ShapeDtypeStruct(shape, dtype)


def vmem(mib):
    return pltpu.CompilerParams(vmem_limit_bytes=mib * 1024 * 1024)


def over_nodes(rows):
    nodes = lax.axis_size("x") * lax.axis_size("z")
    cut = rows.reshape(nodes, rows.shape[0] // nodes, rows.shape[1])
    return lax.all_to_all(cut, ("x", "z"), split_axis=0, concat_axis=0, tiled=True).reshape(rows.shape)


def shards(hidden, routes, route_weights, w_gate, w_up, w_down, gain, head, targets, policy_logp):
    tokens, width = hidden.shape
    second = width - FIRST
    y = lax.axis_index("y")
    core = lax.axis_index("core")
    n_node = lax.axis_size("x") * lax.axis_size("z")
    slots = n_node * SLOTS
    half = slots // 2
    model = 8 * width
    hid = w_gate.shape[2]
    hbm = pl.BlockSpec(memory_space=pl.ANY)
    in_vmem = pl.BlockSpec(memory_space=pltpu.VMEM)

    near_own = pl.pallas_call(
        near_kernel, out_shape=like(tokens + 16, second), compiler_params=vmem(VMEM), name="near"
    )(hidden, gain.reshape(1, width))
    near = [near_own]
    near = near + [shift(near[0], "y", k) for k in (1, 2, 3)]
    pick, mix_hi, mix_lo, send_a = pl.pallas_call(
        route_kernel,
        out_shape=(like(slots, tokens),) * 3 + (like(slots, FIRST),),
        compiler_params=vmem(VMEM),
        name="route",
    )(routes.T, route_weights.T, hidden)
    a0 = over_nodes(send_a)
    send_b, inverse = pl.pallas_call(
        spread_kernel,
        out_shape=(like(slots, 4 * second), like(4, width, dtype=F32)),
        compiler_params=vmem(VMEM),
        name="spread",
    )(pick, *near)
    gate_mat, up_mat, down_mat = w_gate[0], w_up[0], w_down[0]
    gate_other, up_other, down_other = (shift(w, "core", 1) for w in (gate_mat, up_mat, down_mat))
    a0, send_b = lax.optimization_barrier((a0, send_b))
    a1, a3 = shift(a0, "y", 1), shift(a0, "y", -1)
    b = over_nodes(send_b)
    a2_top, a2_low = shift(a1[:half], "y", 1), shift(a3[half:], "y", -1)

    head_other = shift(head, "core", 1)
    place = jnp.stack([y, core]).astype(jnp.int32)

    def rows_of(columns):
        return pl.BlockSpec((half, columns), lambda i, place: (i, 0))

    def whole(columns):
        return pl.BlockSpec((half, columns), lambda i, place: (0, 0))

    partial = pl.pallas_call(
        up_first_kernel,
        grid_spec=pltpu.PrefetchScalarGridSpec(
            num_scalar_prefetch=1,
            grid=(2,),
            in_specs=[rows_of(FIRST)] * 3 + [hbm] * 4,
            out_specs=rows_of(4 * hid),
            scratch_shapes=[pltpu.VMEM((3 * FIRST, 4 * hid), BF), pltpu.SemaphoreType.DMA((4, 3))],
        ),
        out_shape=like(slots, 4 * hid, dtype=F32),
        compiler_params=vmem(VMEM),
        cost_estimate=pl.CostEstimate(
            flops=24 * slots * FIRST * hid, bytes_accessed=24 * FIRST * hid, transcendentals=0
        ),
        name="up_first",
    )(place, a0, a1, a3, gate_mat, up_mat, gate_other, up_other)
    partial, partial_out = pl.pallas_call(
        up_second_kernel,
        grid_spec=pltpu.PrefetchScalarGridSpec(
            num_scalar_prefetch=1,
            grid=(2,),
            in_specs=[rows_of(4 * hid), rows_of(4 * second), whole(FIRST), whole(FIRST)] + [hbm] * 4,
            out_specs=[rows_of(4 * hid)] * 2,
            scratch_shapes=[
                pltpu.VMEM((FIRST + 4 * second, 4 * hid), BF),
                pltpu.VMEM((half, FIRST), BF),
                pltpu.SemaphoreType.DMA((2, 4, 4)),
            ],
        ),
        out_shape=(like(slots, 4 * hid, dtype=F32), like(slots, 4 * hid)),
        compiler_params=vmem(VMEM),
        name="up_second",
    )(place, partial, b, a2_top, a2_low, gate_mat, up_mat, gate_other, up_other)
    partial_got = shift(partial_out, "core", 1)

    a0, a1_top, a1_low, a2_top, a2_low, a3_top, a3_low, b = pl.pallas_call(
        down_kernel,
        grid_spec=pltpu.PrefetchScalarGridSpec(
            num_scalar_prefetch=1,
            grid=(2,),
            in_specs=[rows_of(4 * hid), rows_of(4 * hid), hbm, hbm],
            out_specs=[rows_of(FIRST)] + [whole(FIRST)] * 6 + [rows_of(4 * second)],
            scratch_shapes=[
                pltpu.VMEM((2 * hid, 4 * width), BF),
                pltpu.VMEM((half, 2 * hid), BF),
                pltpu.VMEM((4, half, FIRST), BF),
                pltpu.SemaphoreType.DMA((2, 8)),
            ],
        ),
        out_shape=(like(slots, FIRST),) + (like(half, FIRST),) * 6 + (like(slots, 4 * second),),
        compiler_params=vmem(58),
        name="down",
    )(place, partial, partial_got, down_mat, down_other)

    got1, got3 = shift(a2_top, "y", -1), shift(a2_low, "y", 1)
    left_low, right_top = shift(a1_low, "y", -1), shift(a3_top, "y", 1)
    back_b = over_nodes(b)
    a1_top, a3_low = pl.pallas_call(
        add_kernel, out_shape=(like(half, FIRST),) * 2, compiler_params=vmem(VMEM), name="add"
    )(a1_top, got1, a3_low, got3)
    left_top, right_low = shift(a1_top, "y", -1), shift(a3_low, "y", 1)
    summed = pl.pallas_call(
        ysum_kernel, out_shape=like(slots, FIRST), compiler_params=vmem(VMEM), name="ysum"
    )(a0, left_top, left_low, right_top, right_low)
    back_a = over_nodes(summed)
    own, *others = pl.pallas_call(
        mix_kernel,
        out_shape=(like(tokens, second, dtype=F32),) + (like(tokens, second),) * 3,
        compiler_params=vmem(VMEM),
        name="mix",
    )(mix_hi, mix_lo, back_b)
    arrived = [shift(part, "y", -k) for k, part in zip((1, 2, 3), others)]
    layer_out, scaled = pl.pallas_call(
        layer_kernel,
        out_shape=(like(tokens, width), like(tokens, width)),
        compiler_params=vmem(VMEM),
        name="layer",
    )(hidden, mix_hi, mix_lo, back_a, own, *arrived, gain.reshape(1, width))

    part = tokens // 2
    by_y = [scaled] + [shift(scaled, "y", k) for k in (1, 2, 3)]
    part_a = jnp.stack([rows[:part] for rows in by_y])
    part_b = jnp.stack([rows[part:] for rows in by_y])
    behind_a, far_a1, far_a2, ahead_a = ring(part_a, "x")
    behind_b, far_b1, far_b2, ahead_b = ring(part_b, "z")
    line_a = jnp.stack([part_a, behind_a, jnp.concatenate([far_a1, far_a2]), ahead_a])
    line_b = jnp.stack([part_b, behind_b, jnp.concatenate([far_b1, far_b2]), ahead_b])
    vocab_rows = head.shape[0]
    first_id = (lax.axis_index(AXES) * vocab_rows).reshape(1).astype(jnp.int32)
    x, z = lax.axis_index("x"), lax.axis_index("z")
    wanted = targets.reshape(n_node, 2, part, 1)

    def node_at(back_x, back_z):
        return ((x - back_x) % 4) * 4 + (z - back_z) % 4

    def scored(pieces, mib):
        rows = sum(piece.shape[0] for piece in pieces) * part
        own, other = pl.pallas_call(
            head_kernel,
            grid_spec=pltpu.PrefetchScalarGridSpec(
                num_scalar_prefetch=1,
                grid=(),
                in_specs=[in_vmem] + [hbm] * (2 + len(pieces)),
                out_specs=[in_vmem] * 2,
                scratch_shapes=[
                    pltpu.VMEM((2 * vocab_rows, 4 * width), BF),
                    pltpu.VMEM((rows // part, part, 4 * width), BF),
                    pltpu.SemaphoreType.DMA((2, 4)),
                    pltpu.SemaphoreType.DMA((len(pieces), 4)),
                ],
            ),
            out_shape=(like(rows, vocab_rows + 128, dtype=F32),) * 2,
            compiler_params=vmem(mib),
            cost_estimate=pl.CostEstimate(
                flops=16 * rows * width * vocab_rows,
                bytes_accessed=16 * width * vocab_rows,
                transcendentals=0,
            ),
            name="head",
        )(place, inverse, head, head_other, *pieces)
        return own, other

    def counted(own, got, order, stats):
        return pl.pallas_call(
            functools.partial(stats_kernel, model),
            grid_spec=pltpu.PrefetchScalarGridSpec(
                num_scalar_prefetch=2, grid=(), in_specs=[in_vmem] * 4, out_specs=in_vmem
            ),
            out_shape=like(3 * n_node, 128, dtype=F32),
            compiler_params=vmem(VMEM),
            cost_estimate=pl.CostEstimate(flops=1000, bytes_accessed=1000, transcendentals=0),
            name="stats",
        )(first_id, jnp.stack(order).astype(jnp.int32), own, got, wanted, stats)

    behind_a, ahead_a = shift(line_a, "z", 1), shift(line_a, "z", -1)
    behind_b, ahead_b = shift(line_b, "x", 1), shift(line_b, "x", -1)
    scores = scored((line_a, line_b), 60)
    nearby = (behind_a, ahead_a, behind_b, ahead_b)
    nearby, (own, other) = lax.optimization_barrier((nearby, scores))
    behind_a, ahead_a, behind_b, ahead_b = nearby
    far_a1, far_a2 = shift(behind_a[:2], "z", 1), shift(ahead_a[2:], "z", -1)
    far_b1, far_b2 = shift(behind_b[:2], "x", 1), shift(ahead_b[2:], "x", -1)
    order = [node_at(i, 0) for i in range(4)] + [node_at(0, i) for i in range(4)]
    stats = jnp.zeros((3 * n_node, 128), F32)
    stats = counted(own, shift(other, "core", 1), order, stats)
    scores = scored((behind_a, ahead_a, behind_b, ahead_b), 60)
    far = (far_a1, far_a2, far_b1, far_b2)
    far, (own, other), stats = lax.optimization_barrier((far, scores, stats))
    order = [node_at(i, k) for k in (1, 3) for i in range(4)]
    order = order + [node_at(k, i) for k in (1, 3) for i in range(4)]
    stats = counted(own, shift(other, "core", 1), order, stats)
    own, other = scored(far, VMEM)
    order = [node_at(i, 2) for i in range(4)] + [node_at(2, i) for i in range(4)]
    stats = counted(own, shift(other, "core", 1), order, stats)
    for axis in ("core", "y", "z"):
        stats = pl.pallas_call(
            merge_kernel, out_shape=like(3 * n_node, 128, dtype=F32), name="merge"
        )(*neighbours(stats, axis))
    ref_logp, kl = pl.pallas_call(
        final_kernel, out_shape=(like(n_node * tokens // 128, 128, dtype=F32),) * 2, name="final"
    )(*neighbours(stats, "x"), policy_logp.reshape(-1, 128))
    return layer_out, ref_logp.reshape(-1), kl.reshape(-1)


def solution(mesh):
    split = Mesh(mesh.devices.reshape(4, 4, 4, 2), AXES)
    node, local = ("x", "z"), ("y", "core")
    placed = (
        P(node, local),
        P(node, None),
        P(node, None),
        P(node, None, local),
        P(node, None, local),
        P(node, local, None),
        P(local),
        P(AXES, None),
        P(),
        P(),
    )
    return jax.shard_map(
        shards,
        mesh=split,
        in_specs=placed,
        out_specs=(P(node, local), P(), P()),
        check_vma=False,
    )
```

```python
import functools
import jax
import jax.numpy as jnp
from jax import lax
from jax.experimental import pallas as pl
from jax.experimental.pallas import tpu as pltpu
from jax.sharding import Mesh, PartitionSpec as P

BF = jnp.bfloat16
F32 = jnp.float32
AXES = ("x", "z", "y", "core")
SLOTS = 40
FIRST = 512
VMEM = 48


def shift(value, axis, step):
    size = lax.axis_size(axis)
    return lax.ppermute(value, axis, [(i, (i + step) % size) for i in range(size)])


def dot(a, b):
    return jnp.dot(a, b, preferred_element_type=F32)


def near_kernel(hidden_ref, gain_ref, near_ref):
    tokens, width = hidden_ref.shape
    second = near_ref.shape[1]
    near_ref[:tokens] = hidden_ref[:, FIRST:]
    gain = gain_ref[...]
    hi = gain.astype(BF).astype(F32)
    rows = jnp.zeros((near_ref.shape[0] - tokens, second), F32)
    row = lax.broadcasted_iota(jnp.int32, rows.shape, 0)
    for i, part in enumerate((hi, gain - hi)):
        for j, start in enumerate(range(0, width, second)):
            piece = part[:, start : start + second]
            piece = jnp.pad(piece, ((0, 0), (0, second - piece.shape[1])))
            rows = jnp.where(row == 4 * i + j, piece, rows)
    near_ref[tokens:] = rows.astype(BF)


def route_kernel(routes_ref, weights_ref, hidden_ref, pick_ref, hi_ref, lo_ref, send_ref):
    top, tokens = routes_ref.shape
    slots = pick_ref.shape[0]
    experts = slots // SLOTS
    ids = lax.broadcasted_iota(jnp.int32, (experts, tokens), 0)
    named = jnp.zeros((experts, tokens), F32)
    gates = jnp.zeros((experts, tokens), F32)
    for k in range(top):
        hit = routes_ref[k : k + 1, :] == ids
        named = named + jnp.where(hit, 1.0, 0.0)
        gates = gates + jnp.where(hit, weights_ref[k : k + 1, :], 0.0)
    row = lax.broadcasted_iota(jnp.int32, (tokens, tokens), 0)
    col = lax.broadcasted_iota(jnp.int32, (tokens, tokens), 1)
    count = dot(named.astype(BF), jnp.where(row < col, 1.0, 0.0).astype(BF))
    slot = lax.broadcasted_iota(jnp.int32, (slots, experts), 0)
    expert = lax.broadcasted_iota(jnp.int32, (slots, experts), 1)
    inside = (slot >= expert * SLOTS) & (slot < expert * SLOTS + SLOTS)
    spread = jnp.where(inside, 1.0, 0.0).astype(BF)
    at = jnp.sum(jnp.where(inside, slot - expert * SLOTS, 0).astype(F32), axis=1, keepdims=True)
    gates_hi = gates.astype(BF)
    gates_lo = (gates - gates_hi.astype(F32)).astype(BF)
    placed = (dot(spread, named.astype(BF)) > 0.5) & (dot(spread, count.astype(BF)) == at)
    hi_ref[...] = jnp.where(placed, dot(spread, gates_hi), 0.0).astype(BF)
    lo_ref[...] = jnp.where(placed, dot(spread, gates_lo), 0.0).astype(BF)
    pick = jnp.where(placed, 1.0, 0.0).astype(BF)
    pick_ref[...] = pick
    send_ref[...] = dot(pick, hidden_ref[:, :FIRST]).astype(BF)


def spread_kernel(pick_ref, h0, h1, h2, h3, send_ref, inverse_ref):
    tokens = pick_ref.shape[1]
    second = h0.shape[1]
    width = inverse_ref.shape[1]
    for k, ref in enumerate((h0, h1, h2, h3)):
        send_ref[:, k * second : (k + 1) * second] = dot(pick_ref[...], ref[:tokens]).astype(BF)
        rows = ref[tokens:].astype(F32)
        for j, start in enumerate(range(0, width, second)):
            size = min(second, width - start)
            gain = rows[j : j + 1, :size] + rows[4 + j : 5 + j, :size]
            inverse_ref[k : k + 1, start : start + size] = 1.0 / (gain * gain)


def mixed(hi_ref, lo_ref, rows):
    across = (((0,), (0,)), ((), ()))
    hi = lax.dot_general(hi_ref[...], rows, across, preferred_element_type=F32)
    return hi + lax.dot_general(lo_ref[...], rows, across, preferred_element_type=F32)


def block_of(place_ref, k):
    return 2 * lax.rem(place_ref[0] + 4 - k, 4) + place_ref[1]


def up_copies(place_ref, sources, w_ref, sems, places, offset, size, base):
    hidden = sources[0].shape[1]
    width = sources[0].shape[0] // 8
    made = []
    for j, w in enumerate(sources):
        for i, k in enumerate(places):
            start = pl.multiple_of(block_of(place_ref, k) * width + offset, 128)
            made.append(
                pltpu.make_async_copy(
                    w.at[pl.ds(start, size), :],
                    w_ref.at[pl.ds(base + i * size, size), pl.ds(j * hidden, hidden)],
                    sems.at[j, i],
                )
            )
    return made


def up_first_kernel(place_ref, a0, a1, a3, w0, w1, w2, w3, sum_ref, w_ref, sems):
    hidden = w0.shape[1]

    @pl.when(pl.program_id(0) == 0)
    def _():
        copies = up_copies(place_ref, (w0, w1, w2, w3), w_ref, sems, (0, 1, 3), 0, FIRST, 0)
        for copy in copies:
            copy.start()
        for copy in copies:
            copy.wait()

    @pl.loop(0, 4)
    def _(j):
        cols = pl.ds(pl.multiple_of(j * hidden, hidden), hidden)
        part = dot(a0[...], w_ref[:FIRST, cols])
        for k, ref in ((1, a1), (2, a3)):
            part = part + dot(ref[...], w_ref[k * FIRST : (k + 1) * FIRST, cols])
        sum_ref[:, cols] = part


def up_second_kernel(
    place_ref, before_ref, b_ref, a2_top, a2_low, w0, w1, w2, w3, sum_ref, out_ref, w_ref, a2_ref, sems
):
    step = pl.program_id(0)
    hidden = w0.shape[1]
    second = w0.shape[0] // 8 - FIRST

    @pl.when(step == 0)
    def _():
        sources = (w0, w1, w2, w3)
        copies = up_copies(place_ref, sources, w_ref, sems.at[0], (2,), 0, FIRST, 0)
        copies = copies + up_copies(
            place_ref, sources, w_ref, sems.at[1], (0, 1, 2, 3), FIRST, second, FIRST
        )
        for copy in copies:
            copy.start()
        for copy in copies:
            copy.wait()

    @pl.when(step == 0)
    def _():
        a2_ref[...] = a2_top[...]

    @pl.when(step == 1)
    def _():
        a2_ref[...] = a2_low[...]

    @pl.loop(0, 4)
    def _(j):
        cols = pl.ds(pl.multiple_of(j * hidden, hidden), hidden)
        part = dot(b_ref[...], w_ref[FIRST:, cols]) + dot(a2_ref[...], w_ref[:FIRST, cols])
        part = part + before_ref[:, cols]
        sum_ref[:, cols] = part
        out_ref[:, cols] = part.astype(BF)


def down_kernel(
    place_ref, sum_ref, got_ref, w0, w1, a0, a1_top, a1_low, a2_top, a2_low, a3_top, a3_low, b_ref,
    w_ref, act_ref, done_ref, sems
):
    step = pl.program_id(0)
    hidden = w0.shape[0]
    width = w0.shape[1] // 8
    second = width - FIRST

    def copies():
        made = []
        for j, w in enumerate((w0, w1)):
            rows = pl.ds(j * hidden, hidden)
            for k in range(4):
                start = pl.multiple_of(block_of(place_ref, k) * width, 128)
                made.append(
                    pltpu.make_async_copy(
                        w.at[:, pl.ds(start, FIRST)],
                        w_ref.at[rows, pl.ds(k * FIRST, FIRST)],
                        sems.at[j, 2 * k],
                    )
                )
                made.append(
                    pltpu.make_async_copy(
                        w.at[:, pl.ds(start + FIRST, second)],
                        w_ref.at[rows, pl.ds(4 * FIRST + k * second, second)],
                        sems.at[j, 2 * k + 1],
                    )
                )
        return made

    @pl.when(step == 0)
    def _():
        for copy in copies()[0::2] + copies()[1::2]:
            copy.start()

    for j in range(2):
        own, got = 2 * j * hidden, 2 * (1 - j) * hidden
        gate = sum_ref[:, own : own + hidden] + got_ref[:, got : got + hidden].astype(F32)
        up = sum_ref[:, own + hidden : own + 2 * hidden] + got_ref[
            :, got + hidden : got + 2 * hidden
        ].astype(F32)
        act_ref[:, j * hidden : (j + 1) * hidden] = (gate / (1.0 + jnp.exp(-gate)) * up).astype(BF)

    @pl.when(step == 0)
    def _():
        for copy in copies()[0::2]:
            copy.wait()

    @pl.loop(0, 4)
    def _(k):
        cols = pl.ds(pl.multiple_of(k * FIRST, FIRST), FIRST)
        done_ref[k] = dot(act_ref[...], w_ref[:, cols]).astype(BF)

    @pl.when(step == 0)
    def _():
        for copy in copies()[1::2]:
            copy.wait()

    b_ref[...] = dot(act_ref[...], w_ref[:, 4 * FIRST :]).astype(BF)

    a0[...] = done_ref[0]

    @pl.when(step == 0)
    def _():
        for k, ref in ((1, a1_top), (2, a2_top), (3, a3_top)):
            ref[...] = done_ref[k]

    @pl.when(step == 1)
    def _():
        for k, ref in ((1, a1_low), (2, a2_low), (3, a3_low)):
            ref[...] = done_ref[k]


def add_kernel(a1, got1, a3, got3, out1, out3):
    out1[...] = (a1[...].astype(F32) + got1[...].astype(F32)).astype(BF)
    out3[...] = (a3[...].astype(F32) + got3[...].astype(F32)).astype(BF)


def ysum_kernel(a0, left_top, left_low, right_top, right_low, out_ref):
    half = left_top.shape[0]
    top = a0[:half].astype(F32) + left_top[...].astype(F32) + right_top[...].astype(F32)
    low = a0[half:].astype(F32) + left_low[...].astype(F32) + right_low[...].astype(F32)
    out_ref[:half] = top.astype(BF)
    out_ref[half:] = low.astype(BF)


def mix_kernel(hi_ref, lo_ref, back_ref, own_ref, p1, p2, p3):
    width = own_ref.shape[1]
    for k, ref in enumerate((own_ref, p1, p2, p3)):
        ref[...] = mixed(hi_ref, lo_ref, back_ref[:, k * width : (k + 1) * width]).astype(ref.dtype)


def layer_kernel(hidden_ref, hi_ref, lo_ref, back_ref, own_ref, p1, p2, p3, gain_ref, out_ref, scaled_ref):
    first = mixed(hi_ref, lo_ref, back_ref[...])
    second = own_ref[...] + p1[...].astype(F32) + p2[...].astype(F32) + p3[...].astype(F32)
    for mix, cols in ((first, slice(0, FIRST)), (second, slice(FIRST, hidden_ref.shape[1]))):
        total = hidden_ref[:, cols].astype(F32) + mix
        out_ref[:, cols] = total.astype(BF)
        scaled_ref[:, cols] = (total * gain_ref[:, cols]).astype(BF)


def squares_of(rows, inverse):
    total = jnp.zeros((rows.shape[0], 128), F32)
    for c in range(0, rows.shape[1], 128):
        value = rows[:, c : c + 128].astype(F32)
        total = total + value * value * inverse[:, c : c + 128]
    return total


def head_kernel(place_ref, inverse_ref, w0, w1, *refs):
    *pieces, own_ref, other_ref, w_ref, rows_ref, sems, row_sems = refs
    vocab = w0.shape[0]
    tokens, width = pieces[0].shape[2:]
    blocks = rows_ref.shape[0]

    copies = []
    for j, w in enumerate((w0, w1)):
        for k in range(4):
            start = pl.multiple_of(block_of(place_ref, k) * width, 128)
            copies.append(
                pltpu.make_async_copy(
                    w.at[:, pl.ds(start, width)],
                    w_ref.at[pl.ds(j * vocab, vocab), pl.ds(k * width, width)],
                    sems.at[j, k],
                )
            )
    moves = []
    base = 0
    for i, piece in enumerate(pieces):
        count = piece.shape[0]
        for k in range(4):
            moves.append(
                pltpu.make_async_copy(
                    piece.at[:, k],
                    rows_ref.at[pl.ds(base, count), :, pl.ds(k * width, width)],
                    row_sems.at[i, k],
                )
            )
        base += count
    for copy in moves + copies[4:] + copies[:4]:
        copy.start()
    for move in moves:
        move.wait()

    @pl.loop(0, blocks)
    def _(i):
        at = pl.ds(pl.multiple_of(i * tokens, tokens), tokens)
        squares = jnp.zeros((tokens, 128), F32)
        for k in range(4):
            rows = rows_ref[i, :, k * width : (k + 1) * width]
            squares = squares + squares_of(rows, inverse_ref[k : k + 1])
        own_ref[at, vocab:] = squares
        other_ref[at, vocab:] = squares

    for j, ref in ((1, other_ref), (0, own_ref)):
        for copy in copies[4 * j : 4 * j + 4]:
            copy.wait()

        @pl.loop(0, blocks // 8 * (vocab // 256))
        def _(i, j=j, ref=ref):
            group, part = i // (vocab // 256), i % (vocab // 256)
            at = pl.ds(pl.multiple_of(group * 8 * tokens, 8 * tokens), 8 * tokens)
            rows = rows_ref[pl.ds(group * 8, 8)].reshape(8 * tokens, 4 * width)
            cols = pl.ds(pl.multiple_of(part * 256, 256), 256)
            ref[at, cols] = lax.dot_general(
                rows,
                w_ref[pl.ds(pl.multiple_of(j * vocab + part * 256, 256), 256), :],
                (((1,), (1,)), ((), ())),
                preferred_element_type=F32,
            )


def columns_of(full, ids, wanted):
    peak = jnp.max(full, axis=1, keepdims=True)
    total = jnp.sum(jnp.exp(full - peak), axis=1, keepdims=True)
    target = jnp.sum(jnp.where(ids == wanted, full, 0.0), axis=1, keepdims=True)
    lane = lax.broadcasted_iota(jnp.int32, (full.shape[0], 128), 1)
    return jnp.where(lane == 0, peak, jnp.where(lane == 1, total, target)).T


def stats_kernel(model, first_ref, order_ref, own_ref, got_ref, wanted_ref, before_ref, stats_ref):
    vocab = own_ref.shape[1] - 128
    nodes, _, tokens, _ = wanted_ref.shape
    blocks = own_ref.shape[0] // tokens
    halves = [i // (blocks // 2) for i in range(blocks)]
    wanted = jnp.concatenate([wanted_ref[order_ref[i], halves[i]] for i in range(blocks)], axis=0)
    squares = jnp.sum(own_ref[:, vocab:] + got_ref[:, vocab:], axis=1, keepdims=True)
    scale = lax.rsqrt(squares / model + 1e-06)
    full = (own_ref[:, :vocab] + got_ref[:, :vocab]) * scale
    ids = first_ref[0] + lax.broadcasted_iota(jnp.int32, full.shape, 1)
    columns = columns_of(full, ids, wanted)
    stats_ref[...] = before_ref[...]
    for i in range(blocks):
        for j in range(3):
            row = columns[j : j + 1, i * tokens : (i + 1) * tokens]
            lane = 64 * halves[i]
            stats_ref[pl.ds(j * nodes + order_ref[i], 1), lane : lane + tokens] = row


def paired(terms):
    if len(terms) == 2:
        return terms[0] + terms[1]
    return (terms[0] + terms[2]) + (terms[1] + terms[3])


def combined(refs):
    third = refs[0].shape[0] // 3
    peaks = [ref[:third] for ref in refs]
    peak = functools.reduce(jnp.maximum, peaks)
    total = paired([ref[third : 2 * third] * jnp.exp(own - peak) for ref, own in zip(refs, peaks)])
    return peak, total, paired([ref[2 * third :] for ref in refs])


def merge_kernel(*refs):
    *ins, out_ref = refs
    third = out_ref.shape[0] // 3
    for j, value in enumerate(combined(ins)):
        out_ref[j * third : (j + 1) * third] = value


def final_kernel(*refs):
    *ins, policy_ref, logp_ref, kl_ref = refs
    peak, total, target = combined(ins)
    spaced = target - peak - jnp.log(total)
    half = policy_ref.shape[0] * 128 // (2 * spaced.shape[0])
    tokens = 2 * half
    packed = jnp.concatenate([spaced[:, :half], spaced[:, 64 : 64 + half]], axis=1)
    lines = []
    for at in range(0, spaced.shape[0] * tokens, 128):
        node, lane = at // tokens, at % tokens
        pieces = [packed[node : node + 1, lane:]]
        pieces.append(packed[node + 1 : node + 2, : 128 - (tokens - lane)])
        lines.append(jnp.concatenate(pieces, axis=1))
    logp = jnp.concatenate(lines, axis=0)
    logp_ref[...] = logp
    kl_ref[...] = 0.5 * (policy_ref[...] - logp) * (policy_ref[...] - logp)


def neighbours(stats, axis):
    return [stats] + [shift(stats, axis, k) for k in range(1, lax.axis_size(axis))]


def ring(block, axis):
    half = block.shape[0] // 2
    behind, ahead = shift(block, axis, 1), shift(block, axis, -1)
    return behind, shift(behind[:half], axis, 1), shift(ahead[half:], axis, -1), ahead


def like(*shape, dtype=BF):
    return jax.ShapeDtypeStruct(shape, dtype)


def vmem(mib):
    return pltpu.CompilerParams(vmem_limit_bytes=mib * 1024 * 1024)


def over_nodes(rows):
    nodes = lax.axis_size("x") * lax.axis_size("z")
    cut = rows.reshape(nodes, rows.shape[0] // nodes, rows.shape[1])
    return lax.all_to_all(cut, ("x", "z"), split_axis=0, concat_axis=0, tiled=True).reshape(rows.shape)


def shards(hidden, routes, route_weights, w_gate, w_up, w_down, gain, head, targets, policy_logp):
    tokens, width = hidden.shape
    second = width - FIRST
    y = lax.axis_index("y")
    core = lax.axis_index("core")
    n_node = lax.axis_size("x") * lax.axis_size("z")
    slots = n_node * SLOTS
    half = slots // 2
    model = 8 * width
    hid = w_gate.shape[2]
    hbm = pl.BlockSpec(memory_space=pl.ANY)
    in_vmem = pl.BlockSpec(memory_space=pltpu.VMEM)

    near_own = pl.pallas_call(
        near_kernel, out_shape=like(tokens + 16, second), compiler_params=vmem(VMEM), name="near"
    )(hidden, gain.reshape(1, width))
    near = [near_own]
    near = near + [shift(near[0], "y", k) for k in (1, 2, 3)]
    pick, mix_hi, mix_lo, send_a = pl.pallas_call(
        route_kernel,
        out_shape=(like(slots, tokens),) * 3 + (like(slots, FIRST),),
        compiler_params=vmem(VMEM),
        name="route",
    )(routes.T, route_weights.T, hidden)
    a0 = over_nodes(send_a)
    send_b, inverse = pl.pallas_call(
        spread_kernel,
        out_shape=(like(slots, 4 * second), like(4, width, dtype=F32)),
        compiler_params=vmem(VMEM),
        name="spread",
    )(pick, *near)
    gate_mat, up_mat, down_mat = w_gate[0], w_up[0], w_down[0]
    gate_other, up_other, down_other = (shift(w, "core", 1) for w in (gate_mat, up_mat, down_mat))
    a0, send_b = lax.optimization_barrier((a0, send_b))
    a1, a3 = shift(a0, "y", 1), shift(a0, "y", -1)
    b = over_nodes(send_b)
    a2_top, a2_low = shift(a1[:half], "y", 1), shift(a3[half:], "y", -1)

    head_other = shift(head, "core", 1)
    place = jnp.stack([y, core]).astype(jnp.int32)

    def rows_of(columns):
        return pl.BlockSpec((half, columns), lambda i, place: (i, 0))

    def whole(columns):
        return pl.BlockSpec((half, columns), lambda i, place: (0, 0))

    partial = pl.pallas_call(
        up_first_kernel,
        grid_spec=pltpu.PrefetchScalarGridSpec(
            num_scalar_prefetch=1,
            grid=(2,),
            in_specs=[rows_of(FIRST)] * 3 + [hbm] * 4,
            out_specs=rows_of(4 * hid),
            scratch_shapes=[pltpu.VMEM((3 * FIRST, 4 * hid), BF), pltpu.SemaphoreType.DMA((4, 3))],
        ),
        out_shape=like(slots, 4 * hid, dtype=F32),
        compiler_params=vmem(VMEM),
        cost_estimate=pl.CostEstimate(
            flops=24 * slots * FIRST * hid, bytes_accessed=24 * FIRST * hid, transcendentals=0
        ),
        name="up_first",
    )(place, a0, a1, a3, gate_mat, up_mat, gate_other, up_other)
    partial, partial_out = pl.pallas_call(
        up_second_kernel,
        grid_spec=pltpu.PrefetchScalarGridSpec(
            num_scalar_prefetch=1,
            grid=(2,),
            in_specs=[rows_of(4 * hid), rows_of(4 * second), whole(FIRST), whole(FIRST)] + [hbm] * 4,
            out_specs=[rows_of(4 * hid)] * 2,
            scratch_shapes=[
                pltpu.VMEM((FIRST + 4 * second, 4 * hid), BF),
                pltpu.VMEM((half, FIRST), BF),
                pltpu.SemaphoreType.DMA((2, 4, 4)),
            ],
        ),
        out_shape=(like(slots, 4 * hid, dtype=F32), like(slots, 4 * hid)),
        compiler_params=vmem(VMEM),
        name="up_second",
    )(place, partial, b, a2_top, a2_low, gate_mat, up_mat, gate_other, up_other)
    partial_got = shift(partial_out, "core", 1)

    a0, a1_top, a1_low, a2_top, a2_low, a3_top, a3_low, b = pl.pallas_call(
        down_kernel,
        grid_spec=pltpu.PrefetchScalarGridSpec(
            num_scalar_prefetch=1,
            grid=(2,),
            in_specs=[rows_of(4 * hid), rows_of(4 * hid), hbm, hbm],
            out_specs=[rows_of(FIRST)] + [whole(FIRST)] * 6 + [rows_of(4 * second)],
            scratch_shapes=[
                pltpu.VMEM((2 * hid, 4 * width), BF),
                pltpu.VMEM((half, 2 * hid), BF),
                pltpu.VMEM((4, half, FIRST), BF),
                pltpu.SemaphoreType.DMA((2, 8)),
            ],
        ),
        out_shape=(like(slots, FIRST),) + (like(half, FIRST),) * 6 + (like(slots, 4 * second),),
        compiler_params=vmem(58),
        name="down",
    )(place, partial, partial_got, down_mat, down_other)

    got1, got3 = shift(a2_top, "y", -1), shift(a2_low, "y", 1)
    left_low, right_top = shift(a1_low, "y", -1), shift(a3_top, "y", 1)
    back_b = over_nodes(b)
    a1_top, a3_low = pl.pallas_call(
        add_kernel, out_shape=(like(half, FIRST),) * 2, compiler_params=vmem(VMEM), name="add"
    )(a1_top, got1, a3_low, got3)
    left_top, right_low = shift(a1_top, "y", -1), shift(a3_low, "y", 1)
    summed = pl.pallas_call(
        ysum_kernel, out_shape=like(slots, FIRST), compiler_params=vmem(VMEM), name="ysum"
    )(a0, left_top, left_low, right_top, right_low)
    back_a = over_nodes(summed)
    own, *others = pl.pallas_call(
        mix_kernel,
        out_shape=(like(tokens, second, dtype=F32),) + (like(tokens, second),) * 3,
        compiler_params=vmem(VMEM),
        name="mix",
    )(mix_hi, mix_lo, back_b)
    arrived = [shift(part, "y", -k) for k, part in zip((1, 2, 3), others)]
    layer_out, scaled = pl.pallas_call(
        layer_kernel,
        out_shape=(like(tokens, width), like(tokens, width)),
        compiler_params=vmem(VMEM),
        name="layer",
    )(hidden, mix_hi, mix_lo, back_a, own, *arrived, gain.reshape(1, width))

    part = tokens // 2
    by_y = [scaled] + [shift(scaled, "y", k) for k in (1, 2, 3)]
    part_a = jnp.stack([rows[:part] for rows in by_y])
    part_b = jnp.stack([rows[part:] for rows in by_y])
    behind_a, far_a1, far_a2, ahead_a = ring(part_a, "x")
    behind_b, far_b1, far_b2, ahead_b = ring(part_b, "z")
    lines_a = (jnp.stack([part_a, behind_a]), jnp.stack([jnp.concatenate([far_a1, far_a2]), ahead_a]))
    lines_b = (jnp.stack([part_b, behind_b]), jnp.stack([jnp.concatenate([far_b1, far_b2]), ahead_b]))

    vocab_rows = head.shape[0]
    first_id = (lax.axis_index(AXES) * vocab_rows).reshape(1).astype(jnp.int32)
    x, z = lax.axis_index("x"), lax.axis_index("z")
    wanted = targets.reshape(n_node, 2, part, 1)

    def node_at(back_x, back_z):
        return ((x - back_x) % 4) * 4 + (z - back_z) % 4

    def scored(pieces, mib):
        rows = sum(piece.shape[0] for piece in pieces) * part
        own, other = pl.pallas_call(
            head_kernel,
            grid_spec=pltpu.PrefetchScalarGridSpec(
                num_scalar_prefetch=1,
                grid=(),
                in_specs=[in_vmem] + [hbm] * (2 + len(pieces)),
                out_specs=[in_vmem] * 2,
                scratch_shapes=[
                    pltpu.VMEM((2 * vocab_rows, 4 * width), BF),
                    pltpu.VMEM((rows // part, part, 4 * width), BF),
                    pltpu.SemaphoreType.DMA((2, 4)),
                    pltpu.SemaphoreType.DMA((len(pieces), 4)),
                ],
            ),
            out_shape=(like(rows, vocab_rows + 128, dtype=F32),) * 2,
            compiler_params=vmem(mib),
            cost_estimate=pl.CostEstimate(
                flops=16 * rows * width * vocab_rows,
                bytes_accessed=16 * width * vocab_rows,
                transcendentals=0,
            ),
            name="head",
        )(place, inverse, head, head_other, *pieces)
        return own, other

    def counted(own, got, order, stats):
        return pl.pallas_call(
            functools.partial(stats_kernel, model),
            grid_spec=pltpu.PrefetchScalarGridSpec(
                num_scalar_prefetch=2, grid=(), in_specs=[in_vmem] * 4, out_specs=in_vmem
            ),
            out_shape=like(3 * n_node, 128, dtype=F32),
            compiler_params=vmem(VMEM),
            cost_estimate=pl.CostEstimate(flops=1000, bytes_accessed=1000, transcendentals=0),
            name="stats",
        )(first_id, jnp.stack(order).astype(jnp.int32), own, got, wanted, stats)

    onward_a = (shift(lines_a[0], "z", 1), shift(lines_a[1], "z", -1))
    onward_b = (shift(lines_b[0], "x", 1), shift(lines_b[1], "x", -1))
    rest_a = (shift(lines_a[1], "z", 1), shift(lines_a[0], "z", -1))
    rest_b = (shift(lines_b[1], "x", 1), shift(lines_b[0], "x", -1))
    scores = scored(lines_a + lines_b, 60)
    (onward_a, onward_b), (own, other) = lax.optimization_barrier(((onward_a, onward_b), scores))
    far_a1, far_a2 = shift(onward_a[0], "z", 1), shift(onward_a[1], "z", -1)
    far_b1, far_b2 = shift(onward_b[0], "x", 1), shift(onward_b[1], "x", -1)
    order = [node_at(i, 0) for i in range(4)] + [node_at(0, i) for i in range(4)]
    stats = jnp.zeros((3 * n_node, 128), F32)
    stats = counted(own, shift(other, "core", 1), order, stats)
    scores = scored(
        (onward_a[0], rest_a[0], rest_a[1], onward_a[1], onward_b[0], rest_b[0], rest_b[1], onward_b[1]), 60
    )
    far = (far_a1, far_a2, far_b1, far_b2)
    far, (own, other), stats = lax.optimization_barrier((far, scores, stats))
    order = [node_at(i, k) for k in (1, 3) for i in range(4)]
    order = order + [node_at(k, i) for k in (1, 3) for i in range(4)]
    stats = counted(own, shift(other, "core", 1), order, stats)
    own, other = scored(far, VMEM)
    order = [node_at(i, 2) for i in range(4)] + [node_at(2, i) for i in range(4)]
    stats = counted(own, shift(other, "core", 1), order, stats)
    for axis in ("core", "y", "z"):
        stats = pl.pallas_call(
            merge_kernel, out_shape=like(3 * n_node, 128, dtype=F32), name="merge"
        )(*neighbours(stats, axis))
    ref_logp, kl = pl.pallas_call(
        final_kernel, out_shape=(like(n_node * tokens // 128, 128, dtype=F32),) * 2, name="final"
    )(*neighbours(stats, "x"), policy_logp.reshape(-1, 128))
    return layer_out, ref_logp.reshape(-1), kl.reshape(-1)


def solution(mesh):
    split = Mesh(mesh.devices.reshape(4, 4, 4, 2), AXES)
    node, local = ("x", "z"), ("y", "core")
    placed = (
        P(node, local),
        P(node, None),
        P(node, None),
        P(node, None, local),
        P(node, None, local),
        P(node, local, None),
        P(local),
        P(AXES, None),
        P(),
        P(),
    )
    return jax.shard_map(
        shards,
        mesh=split,
        in_specs=placed,
        out_specs=(P(node, local), P(), P()),
        check_vma=False,
    )
```

```python
import functools
import jax
import jax.numpy as jnp
from jax import lax
from jax.experimental import pallas as pl
from jax.experimental.pallas import tpu as pltpu
from jax.sharding import Mesh, PartitionSpec as P

BF = jnp.bfloat16
F32 = jnp.float32
AXES = ("x", "z", "y", "core")
SLOTS = 40
FIRST = 512
VMEM = 48


def shift(value, axis, step):
    size = lax.axis_size(axis)
    return lax.ppermute(value, axis, [(i, (i + step) % size) for i in range(size)])


def dot(a, b):
    return jnp.dot(a, b, preferred_element_type=F32)


def near_kernel(hidden_ref, gain_ref, near_ref):
    tokens, width = hidden_ref.shape
    second = near_ref.shape[1]
    near_ref[:tokens] = hidden_ref[:, FIRST:]
    gain = gain_ref[...]
    hi = gain.astype(BF).astype(F32)
    rows = jnp.zeros((near_ref.shape[0] - tokens, second), F32)
    row = lax.broadcasted_iota(jnp.int32, rows.shape, 0)
    for i, part in enumerate((hi, gain - hi)):
        for j, start in enumerate(range(0, width, second)):
            piece = part[:, start : start + second]
            piece = jnp.pad(piece, ((0, 0), (0, second - piece.shape[1])))
            rows = jnp.where(row == 4 * i + j, piece, rows)
    near_ref[tokens:] = rows.astype(BF)


def route_kernel(routes_ref, weights_ref, hidden_ref, pick_ref, hi_ref, lo_ref, send_ref):
    top, tokens = routes_ref.shape
    slots = pick_ref.shape[0]
    experts = slots // SLOTS
    ids = lax.broadcasted_iota(jnp.int32, (experts, tokens), 0)
    named = jnp.zeros((experts, tokens), F32)
    gates = jnp.zeros((experts, tokens), F32)
    for k in range(top):
        hit = routes_ref[k : k + 1, :] == ids
        named = named + jnp.where(hit, 1.0, 0.0)
        gates = gates + jnp.where(hit, weights_ref[k : k + 1, :], 0.0)
    row = lax.broadcasted_iota(jnp.int32, (tokens, tokens), 0)
    col = lax.broadcasted_iota(jnp.int32, (tokens, tokens), 1)
    count = dot(named.astype(BF), jnp.where(row < col, 1.0, 0.0).astype(BF))
    slot = lax.broadcasted_iota(jnp.int32, (slots, experts), 0)
    expert = lax.broadcasted_iota(jnp.int32, (slots, experts), 1)
    inside = (slot >= expert * SLOTS) & (slot < expert * SLOTS + SLOTS)
    spread = jnp.where(inside, 1.0, 0.0).astype(BF)
    at = jnp.sum(jnp.where(inside, slot - expert * SLOTS, 0).astype(F32), axis=1, keepdims=True)
    gates_hi = gates.astype(BF)
    gates_lo = (gates - gates_hi.astype(F32)).astype(BF)
    placed = (dot(spread, named.astype(BF)) > 0.5) & (dot(spread, count.astype(BF)) == at)
    hi_ref[...] = jnp.where(placed, dot(spread, gates_hi), 0.0).astype(BF)
    lo_ref[...] = jnp.where(placed, dot(spread, gates_lo), 0.0).astype(BF)
    pick = jnp.where(placed, 1.0, 0.0).astype(BF)
    pick_ref[...] = pick
    send_ref[...] = dot(pick, hidden_ref[:, :FIRST]).astype(BF)


def spread_kernel(pick_ref, h0, h1, h2, h3, send_ref, inverse_ref):
    tokens = pick_ref.shape[1]
    second = h0.shape[1]
    width = inverse_ref.shape[1]
    for k, ref in enumerate((h0, h1, h2, h3)):
        send_ref[:, k * second : (k + 1) * second] = dot(pick_ref[...], ref[:tokens]).astype(BF)
        rows = ref[tokens:].astype(F32)
        for j, start in enumerate(range(0, width, second)):
            size = min(second, width - start)
            gain = rows[j : j + 1, :size] + rows[4 + j : 5 + j, :size]
            inverse_ref[k : k + 1, start : start + size] = 1.0 / (gain * gain)


def mixed(hi_ref, lo_ref, rows):
    across = (((0,), (0,)), ((), ()))
    hi = lax.dot_general(hi_ref[...], rows, across, preferred_element_type=F32)
    return hi + lax.dot_general(lo_ref[...], rows, across, preferred_element_type=F32)


def block_of(place_ref, k):
    return 2 * lax.rem(place_ref[0] + 4 - k, 4) + place_ref[1]


def up_copies(place_ref, sources, w_ref, sems, places, offset, size, base):
    hidden = sources[0].shape[1]
    width = sources[0].shape[0] // 8
    made = []
    for j, w in enumerate(sources):
        for i, k in enumerate(places):
            start = pl.multiple_of(block_of(place_ref, k) * width + offset, 128)
            made.append(
                pltpu.make_async_copy(
                    w.at[pl.ds(start, size), :],
                    w_ref.at[pl.ds(base + i * size, size), pl.ds(j * hidden, hidden)],
                    sems.at[j, i],
                )
            )
    return made


def up_first_kernel(place_ref, a0, a1, a3, w0, w1, w2, w3, sum_ref, w_ref, sems):
    hidden = w0.shape[1]

    @pl.when(pl.program_id(0) == 0)
    def _():
        copies = up_copies(place_ref, (w0, w1, w2, w3), w_ref, sems, (0, 1, 3), 0, FIRST, 0)
        for copy in copies:
            copy.start()
        for copy in copies:
            copy.wait()

    @pl.loop(0, 4)
    def _(j):
        cols = pl.ds(pl.multiple_of(j * hidden, hidden), hidden)
        part = dot(a0[...], w_ref[:FIRST, cols])
        for k, ref in ((1, a1), (2, a3)):
            part = part + dot(ref[...], w_ref[k * FIRST : (k + 1) * FIRST, cols])
        sum_ref[:, cols] = part


def up_second_kernel(
    place_ref, before_ref, b_ref, a2_top, a2_low, w0, w1, w2, w3, sum_ref, out_ref, w_ref, a2_ref, sems
):
    step = pl.program_id(0)
    hidden = w0.shape[1]
    second = w0.shape[0] // 8 - FIRST

    @pl.when(step == 0)
    def _():
        sources = (w0, w1, w2, w3)
        copies = up_copies(place_ref, sources, w_ref, sems.at[0], (2,), 0, FIRST, 0)
        copies = copies + up_copies(
            place_ref, sources, w_ref, sems.at[1], (0, 1, 2, 3), FIRST, second, FIRST
        )
        for copy in copies:
            copy.start()
        for copy in copies:
            copy.wait()

    @pl.when(step == 0)
    def _():
        a2_ref[...] = a2_top[...]

    @pl.when(step == 1)
    def _():
        a2_ref[...] = a2_low[...]

    @pl.loop(0, 4)
    def _(j):
        cols = pl.ds(pl.multiple_of(j * hidden, hidden), hidden)
        part = dot(b_ref[...], w_ref[FIRST:, cols]) + dot(a2_ref[...], w_ref[:FIRST, cols])
        part = part + before_ref[:, cols]
        sum_ref[:, cols] = part
        out_ref[:, cols] = part.astype(BF)


def down_kernel(
    place_ref, sum_ref, got_ref, w0, w1, a0, a1_top, a1_low, a2_top, a2_low, a3_top, a3_low, b_ref,
    w_ref, act_ref, done_ref, sems
):
    step = pl.program_id(0)
    hidden = w0.shape[0]
    width = w0.shape[1] // 8
    second = width - FIRST

    def copies():
        made = []
        for j, w in enumerate((w0, w1)):
            rows = pl.ds(j * hidden, hidden)
            for k in range(4):
                start = pl.multiple_of(block_of(place_ref, k) * width, 128)
                made.append(
                    pltpu.make_async_copy(
                        w.at[:, pl.ds(start, FIRST)],
                        w_ref.at[rows, pl.ds(k * FIRST, FIRST)],
                        sems.at[j, 2 * k],
                    )
                )
                made.append(
                    pltpu.make_async_copy(
                        w.at[:, pl.ds(start + FIRST, second)],
                        w_ref.at[rows, pl.ds(4 * FIRST + k * second, second)],
                        sems.at[j, 2 * k + 1],
                    )
                )
        return made

    @pl.when(step == 0)
    def _():
        for copy in copies()[0::2] + copies()[1::2]:
            copy.start()

    for j in range(2):
        own, got = 2 * j * hidden, 2 * (1 - j) * hidden
        gate = sum_ref[:, own : own + hidden] + got_ref[:, got : got + hidden].astype(F32)
        up = sum_ref[:, own + hidden : own + 2 * hidden] + got_ref[
            :, got + hidden : got + 2 * hidden
        ].astype(F32)
        act_ref[:, j * hidden : (j + 1) * hidden] = (gate / (1.0 + jnp.exp(-gate)) * up).astype(BF)

    @pl.when(step == 0)
    def _():
        for copy in copies()[0::2]:
            copy.wait()

    @pl.loop(0, 4)
    def _(k):
        cols = pl.ds(pl.multiple_of(k * FIRST, FIRST), FIRST)
        done_ref[k] = dot(act_ref[...], w_ref[:, cols]).astype(BF)

    @pl.when(step == 0)
    def _():
        for copy in copies()[1::2]:
            copy.wait()

    b_ref[...] = dot(act_ref[...], w_ref[:, 4 * FIRST :]).astype(BF)

    a0[...] = done_ref[0]

    @pl.when(step == 0)
    def _():
        for k, ref in ((1, a1_top), (2, a2_top), (3, a3_top)):
            ref[...] = done_ref[k]

    @pl.when(step == 1)
    def _():
        for k, ref in ((1, a1_low), (2, a2_low), (3, a3_low)):
            ref[...] = done_ref[k]


def add_kernel(a1, got1, a3, got3, out1, out3):
    out1[...] = (a1[...].astype(F32) + got1[...].astype(F32)).astype(BF)
    out3[...] = (a3[...].astype(F32) + got3[...].astype(F32)).astype(BF)


def ysum_kernel(a0, left_top, left_low, right_top, right_low, out_ref):
    half = left_top.shape[0]
    top = a0[:half].astype(F32) + left_top[...].astype(F32) + right_top[...].astype(F32)
    low = a0[half:].astype(F32) + left_low[...].astype(F32) + right_low[...].astype(F32)
    out_ref[:half] = top.astype(BF)
    out_ref[half:] = low.astype(BF)


def mix_kernel(hi_ref, lo_ref, back_ref, own_ref, p1, p2, p3):
    width = own_ref.shape[1]
    for k, ref in enumerate((own_ref, p1, p2, p3)):
        ref[...] = mixed(hi_ref, lo_ref, back_ref[:, k * width : (k + 1) * width]).astype(ref.dtype)


def layer_kernel(hidden_ref, hi_ref, lo_ref, back_ref, own_ref, p1, p2, p3, gain_ref, out_ref, scaled_ref):
    first = mixed(hi_ref, lo_ref, back_ref[...])
    second = own_ref[...] + p1[...].astype(F32) + p2[...].astype(F32) + p3[...].astype(F32)
    for mix, cols in ((first, slice(0, FIRST)), (second, slice(FIRST, hidden_ref.shape[1]))):
        total = hidden_ref[:, cols].astype(F32) + mix
        out_ref[:, cols] = total.astype(BF)
        scaled_ref[:, cols] = (total * gain_ref[:, cols]).astype(BF)


def squares_of(rows, inverse):
    total = jnp.zeros((rows.shape[0], 128), F32)
    for c in range(0, rows.shape[1], 128):
        value = rows[:, c : c + 128].astype(F32)
        total = total + value * value * inverse[:, c : c + 128]
    return total


def head_kernel(place_ref, inverse_ref, w0, w1, *refs):
    *pieces, own_ref, other_ref, w_ref, rows_ref, sems, row_sems = refs
    vocab = w0.shape[0]
    tokens, width = pieces[0].shape[2:]
    blocks = rows_ref.shape[0]

    copies = []
    for j, w in enumerate((w0, w1)):
        for k in range(4):
            start = pl.multiple_of(block_of(place_ref, k) * width, 128)
            copies.append(
                pltpu.make_async_copy(
                    w.at[:, pl.ds(start, width)],
                    w_ref.at[pl.ds(j * vocab, vocab), pl.ds(k * width, width)],
                    sems.at[j, k],
                )
            )
    moves = []
    base = 0
    for i, piece in enumerate(pieces):
        count = piece.shape[0]
        for k in range(4):
            moves.append(
                pltpu.make_async_copy(
                    piece.at[:, k],
                    rows_ref.at[pl.ds(base, count), :, pl.ds(k * width, width)],
                    row_sems.at[i, k],
                )
            )
        base += count
    for copy in moves + copies[4:] + copies[:4]:
        copy.start()
    for move in moves:
        move.wait()

    @pl.loop(0, blocks)
    def _(i):
        at = pl.ds(pl.multiple_of(i * tokens, tokens), tokens)
        squares = jnp.zeros((tokens, 128), F32)
        for k in range(4):
            rows = rows_ref[i, :, k * width : (k + 1) * width]
            squares = squares + squares_of(rows, inverse_ref[k : k + 1])
        own_ref[at, vocab:] = squares
        other_ref[at, vocab:] = squares

    for j, ref in ((1, other_ref), (0, own_ref)):
        for copy in copies[4 * j : 4 * j + 4]:
            copy.wait()

        @pl.loop(0, blocks // 8 * (vocab // 256))
        def _(i, j=j, ref=ref):
            group, part = i // (vocab // 256), i % (vocab // 256)
            at = pl.ds(pl.multiple_of(group * 8 * tokens, 8 * tokens), 8 * tokens)
            rows = rows_ref[pl.ds(group * 8, 8)].reshape(8 * tokens, 4 * width)
            cols = pl.ds(pl.multiple_of(part * 256, 256), 256)
            ref[at, cols] = lax.dot_general(
                rows,
                w_ref[pl.ds(pl.multiple_of(j * vocab + part * 256, 256), 256), :],
                (((1,), (1,)), ((), ())),
                preferred_element_type=F32,
            )


def columns_of(full, ids, wanted):
    peak = jnp.max(full, axis=1, keepdims=True)
    total = jnp.sum(jnp.exp(full - peak), axis=1, keepdims=True)
    target = jnp.sum(jnp.where(ids == wanted, full, 0.0), axis=1, keepdims=True)
    lane = lax.broadcasted_iota(jnp.int32, (full.shape[0], 128), 1)
    return jnp.where(lane == 0, peak, jnp.where(lane == 1, total, target)).T


def stats_kernel(model, first_ref, order_ref, own_ref, got_ref, wanted_ref, before_ref, stats_ref):
    vocab = own_ref.shape[1] - 128
    nodes, _, tokens, _ = wanted_ref.shape
    blocks = own_ref.shape[0] // tokens
    halves = [i // (blocks // 2) for i in range(blocks)]
    wanted = jnp.concatenate([wanted_ref[order_ref[i], halves[i]] for i in range(blocks)], axis=0)
    squares = jnp.sum(own_ref[:, vocab:] + got_ref[:, vocab:], axis=1, keepdims=True)
    scale = lax.rsqrt(squares / model + 1e-06)
    full = (own_ref[:, :vocab] + got_ref[:, :vocab]) * scale
    ids = first_ref[0] + lax.broadcasted_iota(jnp.int32, full.shape, 1)
    columns = columns_of(full, ids, wanted)
    stats_ref[...] = before_ref[...]
    for i in range(blocks):
        for j in range(3):
            row = columns[j : j + 1, i * tokens : (i + 1) * tokens]
            lane = 64 * halves[i]
            stats_ref[pl.ds(j * nodes + order_ref[i], 1), lane : lane + tokens] = row


def paired(terms):
    if len(terms) == 2:
        return terms[0] + terms[1]
    return (terms[0] + terms[2]) + (terms[1] + terms[3])


def combined(refs):
    third = refs[0].shape[0] // 3
    peaks = [ref[:third] for ref in refs]
    peak = functools.reduce(jnp.maximum, peaks)
    total = paired([ref[third : 2 * third] * jnp.exp(own - peak) for ref, own in zip(refs, peaks)])
    return peak, total, paired([ref[2 * third :] for ref in refs])


def merge_kernel(*refs):
    *ins, out_ref = refs
    third = out_ref.shape[0] // 3
    for j, value in enumerate(combined(ins)):
        out_ref[j * third : (j + 1) * third] = value


def final_kernel(*refs):
    *ins, policy_ref, logp_ref, kl_ref = refs
    peak, total, target = combined(ins)
    spaced = target - peak - jnp.log(total)
    half = policy_ref.shape[0] * 128 // (2 * spaced.shape[0])
    tokens = 2 * half
    packed = jnp.concatenate([spaced[:, :half], spaced[:, 64 : 64 + half]], axis=1)
    lines = []
    for at in range(0, spaced.shape[0] * tokens, 128):
        node, lane = at // tokens, at % tokens
        pieces = [packed[node : node + 1, lane:]]
        pieces.append(packed[node + 1 : node + 2, : 128 - (tokens - lane)])
        lines.append(jnp.concatenate(pieces, axis=1))
    logp = jnp.concatenate(lines, axis=0)
    logp_ref[...] = logp
    kl_ref[...] = 0.5 * (policy_ref[...] - logp) * (policy_ref[...] - logp)


def neighbours(stats, axis):
    return [stats] + [shift(stats, axis, k) for k in range(1, lax.axis_size(axis))]


def ring(block, axis):
    half = block.shape[0] // 2
    behind, ahead = shift(block, axis, 1), shift(block, axis, -1)
    return behind, shift(behind[:half], axis, 1), shift(ahead[half:], axis, -1), ahead


def like(*shape, dtype=BF):
    return jax.ShapeDtypeStruct(shape, dtype)


def vmem(mib):
    return pltpu.CompilerParams(vmem_limit_bytes=mib * 1024 * 1024)


def over_nodes(rows):
    nodes = lax.axis_size("x") * lax.axis_size("z")
    cut = rows.reshape(nodes, rows.shape[0] // nodes, rows.shape[1])
    return lax.all_to_all(cut, ("x", "z"), split_axis=0, concat_axis=0, tiled=True).reshape(rows.shape)


def shards(hidden, routes, route_weights, w_gate, w_up, w_down, gain, head, targets, policy_logp):
    tokens, width = hidden.shape
    second = width - FIRST
    y = lax.axis_index("y")
    core = lax.axis_index("core")
    n_node = lax.axis_size("x") * lax.axis_size("z")
    slots = n_node * SLOTS
    half = slots // 2
    model = 8 * width
    hid = w_gate.shape[2]
    hbm = pl.BlockSpec(memory_space=pl.ANY)
    in_vmem = pl.BlockSpec(memory_space=pltpu.VMEM)

    near_own = pl.pallas_call(
        near_kernel, out_shape=like(tokens + 16, second), compiler_params=vmem(VMEM), name="near"
    )(hidden, gain.reshape(1, width))
    near = [near_own]
    near = near + [shift(near[0], "y", k) for k in (1, 2, 3)]
    pick, mix_hi, mix_lo, send_a = pl.pallas_call(
        route_kernel,
        out_shape=(like(slots, tokens),) * 3 + (like(slots, FIRST),),
        compiler_params=vmem(VMEM),
        name="route",
    )(routes.T, route_weights.T, hidden)
    a0 = over_nodes(send_a)
    send_b, inverse = pl.pallas_call(
        spread_kernel,
        out_shape=(like(slots, 4 * second), like(4, width, dtype=F32)),
        compiler_params=vmem(VMEM),
        name="spread",
    )(pick, *near)
    gate_mat, up_mat, down_mat = w_gate[0], w_up[0], w_down[0]
    gate_other, up_other, down_other = (shift(w, "core", 1) for w in (gate_mat, up_mat, down_mat))
    a0, send_b = lax.optimization_barrier((a0, send_b))
    a1, a3 = shift(a0, "y", 1), shift(a0, "y", -1)
    b = over_nodes(send_b)
    a2_top, a2_low = shift(a1[:half], "y", 1), shift(a3[half:], "y", -1)

    head_other = shift(head, "core", 1)
    place = jnp.stack([y, core]).astype(jnp.int32)

    def rows_of(columns):
        return pl.BlockSpec((half, columns), lambda i, place: (i, 0))

    def whole(columns):
        return pl.BlockSpec((half, columns), lambda i, place: (0, 0))

    partial = pl.pallas_call(
        up_first_kernel,
        grid_spec=pltpu.PrefetchScalarGridSpec(
            num_scalar_prefetch=1,
            grid=(2,),
            in_specs=[rows_of(FIRST)] * 3 + [hbm] * 4,
            out_specs=rows_of(4 * hid),
            scratch_shapes=[pltpu.VMEM((3 * FIRST, 4 * hid), BF), pltpu.SemaphoreType.DMA((4, 3))],
        ),
        out_shape=like(slots, 4 * hid, dtype=F32),
        compiler_params=vmem(VMEM),
        cost_estimate=pl.CostEstimate(
            flops=24 * slots * FIRST * hid, bytes_accessed=24 * FIRST * hid, transcendentals=0
        ),
        name="up_first",
    )(place, a0, a1, a3, gate_mat, up_mat, gate_other, up_other)
    partial, partial_out = pl.pallas_call(
        up_second_kernel,
        grid_spec=pltpu.PrefetchScalarGridSpec(
            num_scalar_prefetch=1,
            grid=(2,),
            in_specs=[rows_of(4 * hid), rows_of(4 * second), whole(FIRST), whole(FIRST)] + [hbm] * 4,
            out_specs=[rows_of(4 * hid)] * 2,
            scratch_shapes=[
                pltpu.VMEM((FIRST + 4 * second, 4 * hid), BF),
                pltpu.VMEM((half, FIRST), BF),
                pltpu.SemaphoreType.DMA((2, 4, 4)),
            ],
        ),
        out_shape=(like(slots, 4 * hid, dtype=F32), like(slots, 4 * hid)),
        compiler_params=vmem(VMEM),
        name="up_second",
    )(place, partial, b, a2_top, a2_low, gate_mat, up_mat, gate_other, up_other)
    partial_got = shift(partial_out, "core", 1)

    a0, a1_top, a1_low, a2_top, a2_low, a3_top, a3_low, b = pl.pallas_call(
        down_kernel,
        grid_spec=pltpu.PrefetchScalarGridSpec(
            num_scalar_prefetch=1,
            grid=(2,),
            in_specs=[rows_of(4 * hid), rows_of(4 * hid), hbm, hbm],
            out_specs=[rows_of(FIRST)] + [whole(FIRST)] * 6 + [rows_of(4 * second)],
            scratch_shapes=[
                pltpu.VMEM((2 * hid, 4 * width), BF),
                pltpu.VMEM((half, 2 * hid), BF),
                pltpu.VMEM((4, half, FIRST), BF),
                pltpu.SemaphoreType.DMA((2, 8)),
            ],
        ),
        out_shape=(like(slots, FIRST),) + (like(half, FIRST),) * 6 + (like(slots, 4 * second),),
        compiler_params=vmem(58),
        name="down",
    )(place, partial, partial_got, down_mat, down_other)

    got1, got3 = shift(a2_top, "y", -1), shift(a2_low, "y", 1)
    left_low, right_top = shift(a1_low, "y", -1), shift(a3_top, "y", 1)
    back_b = over_nodes(b)
    a1_top, a3_low = pl.pallas_call(
        add_kernel, out_shape=(like(half, FIRST),) * 2, compiler_params=vmem(VMEM), name="add"
    )(a1_top, got1, a3_low, got3)
    left_top, right_low = shift(a1_top, "y", -1), shift(a3_low, "y", 1)
    summed = pl.pallas_call(
        ysum_kernel, out_shape=like(slots, FIRST), compiler_params=vmem(VMEM), name="ysum"
    )(a0, left_top, left_low, right_top, right_low)
    back_a = over_nodes(summed)
    own, *others = pl.pallas_call(
        mix_kernel,
        out_shape=(like(tokens, second, dtype=F32),) + (like(tokens, second),) * 3,
        compiler_params=vmem(VMEM),
        name="mix",
    )(mix_hi, mix_lo, back_b)
    arrived = [shift(part, "y", -k) for k, part in zip((1, 2, 3), others)]
    layer_out, scaled = pl.pallas_call(
        layer_kernel,
        out_shape=(like(tokens, width), like(tokens, width)),
        compiler_params=vmem(VMEM),
        name="layer",
    )(hidden, mix_hi, mix_lo, back_a, own, *arrived, gain.reshape(1, width))

    part = tokens // 2
    by_y = [scaled] + [shift(scaled, "y", k) for k in (1, 2, 3)]
    part_a = jnp.stack([rows[:part] for rows in by_y])
    part_b = jnp.stack([rows[part:] for rows in by_y])
    behind_a, far_a1, far_a2, ahead_a = ring(part_a, "x")
    behind_b, far_b1, far_b2, ahead_b = ring(part_b, "z")
    lines_a = (jnp.stack([part_a, behind_a]), jnp.stack([jnp.concatenate([far_a1, far_a2]), ahead_a]))
    lines_b = (jnp.stack([part_b, behind_b]), jnp.stack([jnp.concatenate([far_b1, far_b2]), ahead_b]))

    vocab_rows = head.shape[0]
    first_id = (lax.axis_index(AXES) * vocab_rows).reshape(1).astype(jnp.int32)
    x, z = lax.axis_index("x"), lax.axis_index("z")
    wanted = targets.reshape(n_node, 2, part, 1)

    def node_at(back_x, back_z):
        return ((x - back_x) % 4) * 4 + (z - back_z) % 4

    def scored(pieces, mib):
        rows = sum(piece.shape[0] for piece in pieces) * part
        own, other = pl.pallas_call(
            head_kernel,
            grid_spec=pltpu.PrefetchScalarGridSpec(
                num_scalar_prefetch=1,
                grid=(),
                in_specs=[in_vmem] + [hbm] * (2 + len(pieces)),
                out_specs=[in_vmem] * 2,
                scratch_shapes=[
                    pltpu.VMEM((2 * vocab_rows, 4 * width), BF),
                    pltpu.VMEM((rows // part, part, 4 * width), BF),
                    pltpu.SemaphoreType.DMA((2, 4)),
                    pltpu.SemaphoreType.DMA((len(pieces), 4)),
                ],
            ),
            out_shape=(like(rows, vocab_rows + 128, dtype=F32),) * 2,
            compiler_params=vmem(mib),
            cost_estimate=pl.CostEstimate(
                flops=16 * rows * width * vocab_rows,
                bytes_accessed=16 * width * vocab_rows,
                transcendentals=0,
            ),
            name="head",
        )(place, inverse, head, head_other, *pieces)
        return own, other

    def counted(own, got, order, stats):
        return pl.pallas_call(
            functools.partial(stats_kernel, model),
            grid_spec=pltpu.PrefetchScalarGridSpec(
                num_scalar_prefetch=2, grid=(), in_specs=[in_vmem] * 4, out_specs=in_vmem
            ),
            out_shape=like(3 * n_node, 128, dtype=F32),
            compiler_params=vmem(VMEM),
            cost_estimate=pl.CostEstimate(flops=1000, bytes_accessed=1000, transcendentals=0),
            name="stats",
        )(first_id, jnp.stack(order).astype(jnp.int32), own, got, wanted, stats)

    onward_a = (shift(lines_a[0], "z", 1), shift(lines_a[1], "z", -1))
    onward_b = (shift(lines_b[0], "x", 1), shift(lines_b[1], "x", -1))
    rest_a = (shift(lines_a[1], "z", 1), shift(lines_a[0], "z", -1))
    rest_b = (shift(lines_b[1], "x", 1), shift(lines_b[0], "x", -1))
    scores = scored(lines_a + lines_b, VMEM)
    (onward_a, onward_b), (own, other) = lax.optimization_barrier(((onward_a, onward_b), scores))
    far_a1, far_a2 = shift(onward_a[0], "z", 1), shift(onward_a[1], "z", -1)
    far_b1, far_b2 = shift(onward_b[0], "x", 1), shift(onward_b[1], "x", -1)
    order = [node_at(i, 0) for i in range(4)] + [node_at(0, i) for i in range(4)]
    stats = jnp.zeros((3 * n_node, 128), F32)
    stats = counted(own, shift(other, "core", 1), order, stats)
    scores = scored(
        (onward_a[0], rest_a[0], rest_a[1], onward_a[1], onward_b[0], rest_b[0], rest_b[1], onward_b[1]), 60
    )
    far = (far_a1, far_a2, far_b1, far_b2)
    far, (own, other), stats = lax.optimization_barrier((far, scores, stats))
    order = [node_at(i, k) for k in (1, 3) for i in range(4)]
    order = order + [node_at(k, i) for k in (1, 3) for i in range(4)]
    stats = counted(own, shift(other, "core", 1), order, stats)
    own, other = scored(far, VMEM)
    order = [node_at(i, 2) for i in range(4)] + [node_at(2, i) for i in range(4)]
    stats = counted(own, shift(other, "core", 1), order, stats)
    for axis in ("core", "y", "z"):
        stats = pl.pallas_call(
            merge_kernel, out_shape=like(3 * n_node, 128, dtype=F32), name="merge"
        )(*neighbours(stats, axis))
    ref_logp, kl = pl.pallas_call(
        final_kernel, out_shape=(like(n_node * tokens // 128, 128, dtype=F32),) * 2, name="final"
    )(*neighbours(stats, "x"), policy_logp.reshape(-1, 128))
    return layer_out, ref_logp.reshape(-1), kl.reshape(-1)


def solution(mesh):
    split = Mesh(mesh.devices.reshape(4, 4, 4, 2), AXES)
    node, local = ("x", "z"), ("y", "core")
    placed = (
        P(node, local),
        P(node, None),
        P(node, None),
        P(node, None, local),
        P(node, None, local),
        P(node, local, None),
        P(local),
        P(AXES, None),
        P(),
        P(),
    )
    return jax.shard_map(
        shards,
        mesh=split,
        in_specs=placed,
        out_specs=(P(node, local), P(), P()),
        check_vma=False,
    )
```
